32 devices in a mesh: images: 8 (over y, x, core), rows: 4 (over z).
Axes of the slice: x: 2, y: 2, z: 4, core: 2. Of those that a mesh axis runs over, the one named last changes fastest.
Arguments:
- tokens: bfloat16 [16, 16, 32, 1152], P('images', 'rows'), may hold values from -6 to 6
- cotangent: bfloat16 [16, 16, 32, 1152], P('images', 'rows'), may hold values from -6 to 6
- heights: int32 [16], P('images'), may hold values from 8 to 16, as said below
- widths: int32 [16], P('images'), may hold values from 12 to 32, as said below
- timesteps: int32 [16], P('images'), may hold values from 0 to 999
- rel_index: int32 [5, 63], replicated, may hold values from 0 to 255
- ln1_gain: bfloat16 [1152], replicated, may hold values from 0.5 to 1.5
- ln1_bias: bfloat16 [1152], replicated, may hold values from -4 to 4
- w_qkv: bfloat16 [1152, 3456], P('images', 'rows'), may hold values from -0.1875 to 0.1875
- w_time: bfloat16 [1152, 2304], P('images', 'rows'), may hold values from -0.1875 to 0.1875
- rel_table: bfloat16 [256, 16], replicated, may hold values from -6 to 6
- w_out: bfloat16 [1152, 1152], P('images', 'rows'), may hold values from -1.5 to 1.5
- out_bias: bfloat16 [1152], replicated, may hold values from -4 to 4
- ln2_gain: bfloat16 [1152], replicated, may hold values from 0.5 to 1.5
- ln2_bias: bfloat16 [1152], replicated, may hold values from -4 to 4
- w_fc1: bfloat16 [1152, 4608], P('images', 'rows'), may hold values from -0.1875 to 0.1875
- fc1_bias: bfloat16 [4608], replicated, may hold values from -4 to 4
- w_fc2: bfloat16 [4608, 1152], P('images', 'rows'), may hold values from -0.09375 to 0.09375
- fc2_bias: bfloat16 [1152], replicated, may hold values from -4 to 4
Outputs:
- mixed: bfloat16 [16, 16, 32, 1152], P('images', 'rows')
- grad_tokens: bfloat16 [16, 16, 32, 1152], P('images', 'rows')
- grad_ln1_gain: float32 [1152], replicated
- grad_ln1_bias: float32 [1152], replicated
- grad_w_qkv: float32 [1152, 3456], P('images', 'rows')
- grad_w_time: float32 [1152, 2304], P('images', 'rows')
- grad_rel_table: float32 [256, 16], replicated
- grad_w_out: float32 [1152, 1152], P('images', 'rows')
- grad_out_bias: float32 [1152], replicated
- grad_ln2_gain: float32 [1152], replicated
- grad_ln2_bias: float32 [1152], replicated
- grad_w_fc1: float32 [1152, 4608], P('images', 'rows')
- grad_fc1_bias: float32 [4608], replicated
- grad_w_fc2: float32 [4608, 1152], P('images', 'rows')
- grad_fc2_bias: float32 [1152], replicated
The draws below stay inside these ranges and needn't reach their ends.
Inputs may be any that keep to these rules, and one draw needn't show every extreme that they name: `heights`: in each block of 2 images of one images index, one image has the height 16 and another the height 16 / 2. `widths`: each image's height times width lies between 192 and 320; in each block of 2 images of one images index, an image of height 16 / 2 has the width 32.
All inputs are finite; a program needn't handle non-finite values.
Results may differ from the reference program's by a relative error of at most 0.014.
Values may be sent and summed in bfloat16 or wider, within the bound.
No kernel may reach another device: no remote copies, remote signals or barrier semaphores. Data moves between devices by JAX's collectives and lax.ppermute only.
A program may use at most 192 MiB of HBM per device.

```python
import math
import jax
import jax.numpy as jnp
from jax import lax

D = 1152
FF = 4608
HEADS = 16
HALO = 2
BUCKETS = 256
GRID_COLS = 32
IMG_DEV = 2
GRID_ROWS = 16
IMAGES = 16


def grid_shapes(key):
    block_count = IMAGES // IMG_DEV
    key_height, key_width, key_first, key_second = jax.random.split(key, 4)
    least_cells = 3 * GRID_ROWS * GRID_COLS // 8
    most_cells = 5 * GRID_ROWS * GRID_COLS // 8
    height_all = jax.random.randint(key_height, (block_count, IMG_DEV), GRID_ROWS // 2, GRID_ROWS + 1)
    width_draw = jax.random.randint(key_width, (block_count, IMG_DEV), 0, 1 << 20)
    first_slot = jax.random.randint(key_first, (block_count, 1), 0, IMG_DEV)
    step_slot = jax.random.randint(key_second, (block_count, 1), 1, IMG_DEV)
    second_slot = (first_slot + step_slot) % IMG_DEV
    slot_ids = jnp.arange(IMG_DEV, dtype=jnp.int32)[None, :]
    height_all = jnp.where(slot_ids == first_slot, GRID_ROWS, height_all)
    height_all = jnp.where(slot_ids == second_slot, GRID_ROWS // 2, height_all)
    lowest = (least_cells + height_all - 1) // height_all
    highest = jnp.minimum(GRID_COLS, most_cells // height_all)
    width_all = lowest + width_draw % (highest - lowest + 1)
    width_all = jnp.where(slot_ids == second_slot, GRID_COLS, width_all)
    return (height_all.reshape(-1).astype(jnp.int32), width_all.reshape(-1).astype(jnp.int32))


def draw_heights(key, part):
    shapes = grid_shapes(key)
    return shapes[0]


def draw_widths(key, part):
    shapes = grid_shapes(key)
    return shapes[1]


def place_ends(values, rng, least, high):
    longest = values.shape.index(max(values.shape))
    spots = []
    for shift in (0, 1):
        where = [jax.random.randint(jax.random.fold_in(rng, axis), (), 0, length) for axis, length in enumerate(values.shape)]
        where[longest] = (where[longest] + shift) % values.shape[longest]
        spots.append(tuple(where))
    return values.at[spots[0]].set(least).at[spots[1]].set(high)


def raised(drawn, stream_key, source, target, parts, factor):
    def block_of(axis_at):
        return (jnp.arange(drawn.shape[axis_at]) // (drawn.shape[axis_at] // parts)).reshape((-1,) + (1,) * (drawn.ndim - 1 - axis_at))

    one_side = jax.random.permutation(stream_key, parts)[block_of(target)]
    far = (block_of(target) + parts // 2) % parts
    return jnp.where((block_of(source) == one_side) | (block_of(source) == far), factor * drawn, drawn)


def block_scale(stream_key, dims, cuts, least, largest):
    def one(axis_at, shards_of):
        steps = jax.random.uniform(jax.random.fold_in(jax.random.fold_in(stream_key, 6), axis_at), (shards_of,), jnp.float32, least / len(cuts), largest / len(cuts))
        return jnp.repeat(jnp.exp(steps), dims[axis_at] // shards_of).reshape((-1,) + (1,) * (len(dims) - axis_at - 1))

    loudness = one(*cuts[0])
    for cut in cuts[1:]:
        loudness = loudness * one(*cut)
    return loudness


def noise(own_key, dims, scale, limit, pieces=(), held_as=jnp.bfloat16):
    gain = block_scale(own_key, dims, pieces, -0.22, 0.18) if pieces else 1.0
    values = jax.random.normal(own_key, dims, jnp.float32) * scale * gain
    return jnp.minimum(jnp.maximum(values, -limit), limit).astype(held_as)


def heavy_noise(rng, dims, width, limit, cuts, heavy, kind=jnp.bfloat16):
    entries = width * jax.random.normal(rng, dims, jnp.float32)
    if cuts:
        entries = entries * block_scale(rng, dims, cuts, -0.22, 0.18)
    return jnp.clip(raised(entries, jax.random.fold_in(rng, 3), *heavy), -limit, limit).astype(kind)


def setup_inputs(seed: int = 0) -> dict:
    keys = jax.random.split(jax.random.key(seed), 20)
    return {
        "tokens": noise(keys[0], (IMAGES, GRID_ROWS, GRID_COLS, D), 1.0, 6.0, ((0, 8), (1, 4))),
        "cotangent": heavy_noise(keys[1], (IMAGES, GRID_ROWS, GRID_COLS, D), 1.0, 6.0, ((0, 8), (1, 4)), (0, 3, 8, 2.0)),
        "heights": draw_heights(jax.random.fold_in(keys[19], 71), 0),
        "widths": draw_widths(jax.random.fold_in(keys[19], 71), 0),
        "timesteps": place_ends(jax.random.randint(keys[4], (IMAGES,), 0, 1000), jax.random.fold_in(keys[4], 1), 0, 999).astype(jnp.int32),
        "rel_index": place_ends(jax.random.randint(keys[5], (2 * HALO + 1, 2 * GRID_COLS - 1), 0, BUCKETS), jax.random.fold_in(keys[5], 1), 0, BUCKETS - 1).astype(jnp.int32),
        "ln1_gain": jnp.clip(1.0 + 0.1 * jax.random.normal(keys[6], (D,), jnp.float32), 0.5, 1.5).astype(jnp.bfloat16),
        "ln1_bias": noise(keys[7], (D,), 0.3, 4.0),
        "w_qkv": noise(keys[8], (D, 3 * D), D ** -0.5, 0.1875, ((0, 8), (1, 4))),
        "w_time": noise(keys[9], (D, 2 * D), D ** -0.5, 0.1875, ((0, 8), (1, 4))),
        "rel_table": noise(keys[10], (BUCKETS, HEADS), 0.5, 6.0),
        "w_out": noise(keys[11], (D, D), (D // 64) ** -0.5, 1.5, ((0, 8), (1, 4))),
        "out_bias": noise(keys[12], (D,), 0.3, 4.0),
        "ln2_gain": jnp.clip(1.0 + 0.1 * jax.random.normal(keys[13], (D,), jnp.float32), 0.5, 1.5).astype(jnp.bfloat16),
        "ln2_bias": noise(keys[14], (D,), 0.3, 4.0),
        "w_fc1": noise(keys[15], (D, FF), D ** -0.5, 0.1875, ((0, 8), (1, 4))),
        "fc1_bias": noise(keys[16], (FF,), 0.3, 4.0),
        "w_fc2": noise(keys[17], (FF, D), FF ** -0.5, 0.09375, ((0, 8), (1, 4))),
        "fc2_bias": noise(keys[18], (D,), 0.3, 4.0),
    }


@jax.custom_vjp
def low(v):
    return lax.optimization_barrier(v.astype(jnp.bfloat16)).astype(jnp.float32)

@jax.custom_vjp
def low_back(v):
    return v

def low_keep(v):
    return (low(v), None)

def low_pass(kept, grad):
    return (grad,)

def back_keep(v):
    return (v, None)

def back_low(kept, grad):
    return (low(grad),)
low.defvjp(low_keep, low_pass)
low_back.defvjp(back_keep, back_low)
norm_eps = 1e-06
masked_score = -1000000000.0

def product(left, right):
    return jnp.dot(left, right, precision=lax.Precision.HIGHEST)

def normalize(values):
    centre = values - lax.optimization_barrier(jnp.mean(values, -1, keepdims=True))
    spread = lax.optimization_barrier(jnp.mean(centre * centre, -1, keepdims=True))
    return centre * lax.rsqrt(spread + norm_eps)

def time_features(steps, model_width):
    half_width = model_width // 2
    frequency = jnp.exp(-math.log(10000.0) * jnp.arange(half_width, dtype=jnp.float32) / half_width)
    phases = steps.astype(jnp.float32)[:, None] * frequency[None, :]
    return jnp.concatenate([jnp.cos(phases), jnp.sin(phases)], -1)

def layer(params, image_block, heights_blk, widths_blk, steps_blk, rel_index):
    gain_one, shift_one, w_qkv, w_time, rel_table, w_out, out_bias, gain_two, shift_two, w_fc1, fc1_bias, w_fc2, fc2_bias = params
    image_count, grid_rows, grid_cols, model_width = image_block.shape
    cell_count = grid_rows * grid_cols
    head_count = rel_table.shape[1]
    head_dim = model_width // head_count
    score_scale = head_dim ** (-0.5)
    flat_tokens = image_block.reshape(image_count, cell_count, model_width)
    normed = low(normalize(flat_tokens) * gain_one + shift_one)
    timing = low(time_features(steps_blk, model_width))
    projected = product(normed, w_qkv)
    time_terms = product(timing, w_time)
    query_all = low_back(low(projected[..., :model_width] + time_terms[:, None, :model_width]))
    key_all = low_back(low(projected[..., model_width:2 * model_width]))
    value_all = low_back(low(projected[..., 2 * model_width:] + time_terms[:, None, model_width:]))
    cell_row = jnp.arange(cell_count) // grid_cols
    cell_col = jnp.arange(cell_count) % grid_cols
    row_gap = cell_row[None, :] - cell_row[:, None]
    col_gap = cell_col[None, :] - cell_col[:, None]
    offsets = (jnp.clip(row_gap, -HALO, HALO) + HALO) * (2 * grid_cols - 1) + col_gap + grid_cols - 1
    bucket_hits = (rel_index.reshape(-1)[:, None] == jnp.arange(rel_table.shape[0])[None, :]).astype(jnp.float32)
    rel_bias = product(bucket_hits, rel_table).T[:, offsets]
    window = jnp.abs(row_gap) <= HALO
    itself = jnp.eye(cell_count, dtype=bool)

    def attend(image_item):
        query_one, key_one, value_one, img_height, img_width = image_item
        key_ok = (cell_row < img_height) & (cell_col < img_width)
        allowed = window & key_ok[None, :] | itself
        scores = jnp.einsum('qhd,khd->hqk', query_one.reshape(cell_count, head_count, head_dim), key_one.reshape(cell_count, head_count, head_dim), precision=lax.Precision.HIGHEST) * score_scale + rel_bias
        scores = jnp.where(allowed[None], low_back(scores), masked_score)
        weights = low(jax.nn.softmax(scores, axis=-1))
        mixed_heads = jnp.einsum('hqk,khd->qhd', weights, value_one.reshape(cell_count, head_count, head_dim), precision=lax.Precision.HIGHEST)
        return mixed_heads.reshape(cell_count, model_width)
    attended = lax.map(jax.checkpoint(attend), (query_all, key_all, value_all, heights_blk, widths_blk))
    attended = low_back(low(attended))
    branch_out = low_back(product(attended, w_out) + out_bias)
    middle = flat_tokens + branch_out
    second = low(normalize(middle) * gain_two + shift_two)
    hidden_pre = low_back(product(second, w_fc1) + fc1_bias)
    hidden_act = low(jax.nn.gelu(hidden_pre, approximate=True))
    mlp_out = low_back(product(hidden_act, w_fc2) + fc2_bias)
    valid = (cell_row[None, :] < heights_blk[:, None]) & (cell_col[None, :] < widths_blk[:, None])
    valid_mask = valid.astype(jnp.float32)[..., None]
    return (valid_mask * (middle + mlp_out)).reshape(image_block.shape)

def reference(tokens, cotangent, heights, widths, timesteps, rel_index, ln1_gain, ln1_bias, w_qkv, w_time, rel_table, w_out, out_bias, ln2_gain, ln2_bias, w_fc1, fc1_bias, w_fc2, fc2_bias):
    params = tuple((weight_item.astype(jnp.float32) for weight_item in (ln1_gain, ln1_bias, w_qkv, w_time, rel_table, w_out, out_bias, ln2_gain, ln2_bias, w_fc1, fc1_bias, w_fc2, fc2_bias)))
    group_count = IMAGES // 8
    token_groups = tokens.astype(jnp.float32).reshape(group_count, 8, GRID_ROWS, GRID_COLS, D)
    cot_groups = cotangent.astype(jnp.float32).reshape(group_count, 8, GRID_ROWS, GRID_COLS, D)
    height_groups = heights.reshape(group_count, 8)
    width_groups = widths.reshape(group_count, 8)
    step_groups = timesteps.reshape(group_count, 8)
    zeros_start = jax.tree.map(jnp.zeros_like, params)

    def accumulate(running, group_item):
        token_blk, cot_blk, height_blk, width_blk, step_blk = group_item

        def forward(param_set, token_set):
            return layer(param_set, token_set, height_blk, width_blk, step_blk, rel_index)
        result_rows, pullback = jax.vjp(forward, params, token_blk)
        grad_params, grad_input = pullback(cot_blk)
        return (jax.tree.map(jnp.add, running, grad_params), (result_rows, grad_input))
    totals, (outputs, input_grads) = lax.scan(accumulate, zeros_start, (token_groups, cot_groups, height_groups, width_groups, step_groups))
    shape_full = (IMAGES, GRID_ROWS, GRID_COLS, D)
    return (outputs.reshape(shape_full).astype(jnp.bfloat16), input_grads.reshape(shape_full).astype(jnp.bfloat16), totals[0], totals[1], totals[2], totals[3], totals[4], totals[5], totals[6], totals[7], totals[8], totals[9], totals[10], totals[11], totals[12])
```

```python
import functools
import math

import jax
import jax.numpy as jnp
from jax import lax
from jax.experimental import pallas as pl
from jax.experimental.pallas import tpu as pltpu
from jax.sharding import PartitionSpec as P

HALO = 2
LANES = 128

norm_eps = 1e-06
masked_score = -1000000000.0

f32 = jnp.float32
bf16 = jnp.bfloat16

NN = (((1,), (0,)), ((), ()))
NT = (((1,), (1,)), ((), ()))
TN = (((0,), (0,)), ((), ()))


def dot(left, right, dims=NN):
    return lax.dot_general(left, right, dims, preferred_element_type=f32)


def normalize(values):
    centre = values - jnp.mean(values, -1, keepdims=True)
    spread = jnp.mean(centre * centre, -1, keepdims=True)
    inverse = lax.rsqrt(spread + norm_eps)
    return (centre * inverse, inverse)


def norm_back(grad_hat, normal_part, inverse):
    first_mean = jnp.mean(grad_hat, -1, keepdims=True)
    second_mean = jnp.mean(grad_hat * normal_part, -1, keepdims=True)
    return inverse * (grad_hat - first_mean - normal_part * second_mean)


def gelu_tanh(values):
    return jax.nn.gelu(values, approximate=True)


def window(head, head_dim, width):
    first, last = head * head_dim, (head + 1) * head_dim
    start = first // LANES * LANES
    stop = min(-(-last // LANES) * LANES, width)
    return first, last, start, stop


def lane_mask(first, last, start, stop, kind):
    lane = lax.broadcasted_iota(jnp.int32, (1, stop - start), 1) + start
    return jnp.where((lane >= first) & (lane < last), 1.0, 0.0).astype(kind)


def add_tiles(tiles, values, start, stop):
    for at in range(start, stop, LANES):
        part = values[:, at - start : min(at + LANES, stop) - start]
        tiles[at] = part if at not in tiles else tiles[at] + part


def store_tiles(ref, tiles, scale=None):
    for at, part in tiles.items():
        if scale is not None:
            part = part * scale
        ref[0, :, at : at + part.shape[1]] = part.astype(ref.dtype)


def attend_kernel(heads, scale, q_ref, k_ref, v_ref, bias_ref, allow_ref, o_ref, p_ref):
    width = q_ref.shape[-1]
    allowed = allow_ref[0] > 0.5
    tiles = {}
    for head in range(heads):
        span = window(head, width // heads, width)
        start, stop = span[2:]
        query = q_ref[0, :, start:stop] * lane_mask(*span, bf16)
        scores = dot(query, k_ref[0, :, start:stop], NT) * scale + bias_ref[head].astype(f32)
        scores = jnp.where(allowed, scores, masked_score)
        expo = jnp.exp(scores - jnp.max(scores, -1, keepdims=True))
        prob = (expo / jnp.sum(expo, -1, keepdims=True)).astype(bf16)
        p_ref[0, head] = prob
        out = dot(prob, v_ref[0, :, start:stop]) * lane_mask(*span, f32)
        add_tiles(tiles, out, start, stop)
    store_tiles(o_ref, tiles)


def attend_back_kernel(
    heads, scale, cols, q_ref, k_ref, v_ref, p_ref, do_ref, dq_ref, dk_ref, dv_ref, g_ref, sum_ref
):
    width = q_ref.shape[-1]
    rows = q_ref.shape[1] // cols
    step = pl.program_id(0)

    @pl.when(step == 0)
    def _():
        sum_ref[...] = jnp.zeros_like(sum_ref)

    dq_tiles, dk_tiles, dv_tiles = {}, {}, {}
    for head in range(heads):
        span = window(head, width // heads, width)
        start, stop = span[2:]
        mask = lane_mask(*span, bf16)
        query = q_ref[0, :, start:stop] * mask
        grad_out = do_ref[0, :, start:stop] * mask
        prob = p_ref[0, head]
        full = prob.astype(f32)
        grad_prob = dot(grad_out, v_ref[0, :, start:stop], NT)
        weighted = full * grad_prob
        grad_score = (weighted - full * jnp.sum(weighted, -1, keepdims=True)).astype(bf16)
        sum_ref[head] += grad_score.astype(f32)
        dq = dot(grad_score, k_ref[0, :, start:stop]) * lane_mask(*span, f32)
        add_tiles(dq_tiles, dq, start, stop)
        add_tiles(dk_tiles, dot(grad_score, query, TN), start, stop)
        add_tiles(dv_tiles, dot(prob, grad_out, TN), start, stop)
    store_tiles(dq_ref, dq_tiles, scale)
    store_tiles(dk_ref, dk_tiles, scale)
    store_tiles(dv_ref, dv_tiles)

    @pl.when(step == pl.num_programs(0) - 1)
    def _():
        for head in range(heads):
            total = sum_ref[head, :cols]
            for row in range(1, rows):
                part = sum_ref[head, row * cols : (row + 1) * cols]
                total += pltpu.roll(part, part.shape[1] - row * cols, 1)
            g_ref[head] = total


def per_image(*dims):
    return pl.BlockSpec((1,) + dims, lambda i: (i,) + (0,) * len(dims))


def whole(*dims):
    return pl.BlockSpec(dims, lambda i: (0,) * len(dims))


def attend(query, key, value, bias, allowed, scale):
    images, cells, width = query.shape
    heads, _, keys = bias.shape
    return pl.pallas_call(
        functools.partial(attend_kernel, heads, scale),
        grid=(images,),
        in_specs=[
            per_image(cells, width),
            per_image(keys, width),
            per_image(keys, width),
            whole(heads, cells, keys),
            per_image(cells, keys),
        ],
        out_specs=[per_image(cells, width), per_image(heads, cells, keys)],
        out_shape=[
            jax.ShapeDtypeStruct((images, cells, width), bf16),
            jax.ShapeDtypeStruct((images, heads, cells, keys), bf16),
        ],
        compiler_params=pltpu.CompilerParams(vmem_limit_bytes=32 << 20),
        cost_estimate=pl.CostEstimate(
            flops=4 * images * heads * cells * keys * 256,
            bytes_accessed=4 * images * heads * cells * keys,
            transcendentals=images * heads * cells * keys,
        ),
        name="attend",
    )(query, key, value, bias, allowed)


def attend_back(query, key, value, prob, grad_out, scale, cols):
    images, cells, width = query.shape
    _, heads, _, keys = prob.shape
    return pl.pallas_call(
        functools.partial(attend_back_kernel, heads, scale, cols),
        grid=(images,),
        in_specs=[
            per_image(cells, width),
            per_image(keys, width),
            per_image(keys, width),
            per_image(heads, cells, keys),
            per_image(cells, width),
        ],
        out_specs=[
            per_image(cells, width),
            per_image(keys, width),
            per_image(keys, width),
            whole(heads, cols, keys),
        ],
        out_shape=[
            jax.ShapeDtypeStruct((images, cells, width), bf16),
            jax.ShapeDtypeStruct((images, keys, width), bf16),
            jax.ShapeDtypeStruct((images, keys, width), bf16),
            jax.ShapeDtypeStruct((heads, cols, keys), f32),
        ],
        scratch_shapes=[pltpu.VMEM((heads, cells, keys), f32)],
        compiler_params=pltpu.CompilerParams(vmem_limit_bytes=32 << 20),
        cost_estimate=pl.CostEstimate(
            flops=8 * images * heads * cells * keys * 256,
            bytes_accessed=4 * images * heads * cells * keys,
            transcendentals=0,
        ),
        name="attend_back",
    )(query, key, value, prob, grad_out)


def shards(
    tokens,
    cotangent,
    heights,
    widths,
    timesteps,
    rel_index,
    ln1_gain,
    ln1_bias,
    w_qkv,
    w_time,
    rel_table,
    w_out,
    out_bias,
    ln2_gain,
    ln2_bias,
    w_fc1,
    fc1_bias,
    w_fc2,
    fc2_bias,
):
    here, rows_here, cols, width = tokens.shape
    cells = rows_here * cols
    slots = here * cells
    key_rows = rows_here + 2 * HALO
    keys = key_rows * cols
    head_count = rel_table.shape[1]
    head_dim = width // head_count
    scale = head_dim ** (-0.5)
    image_devices = lax.axis_size("images")
    tiles = lax.axis_size("rows")
    low = image_devices // 8
    chunk = width // 8
    quarter = width // 4
    ff_part = fc1_bias.shape[0] // 16
    place = lax.axis_index("images")
    tile = lax.axis_index("rows")
    bits = {"c": low, "x": 2 * low, "y": 4 * low}
    at_c, at_x, at_y = (place // bits[name] % 2 for name in "cxy")


    def partner(value, bit):
        route = [(d, d ^ bit) for d in range(image_devices)]
        return lax.ppermute(value, "images", route)

    def swap(value, name):
        return partner(value, bits[name])

    def pick(at, pair):
        return jnp.where(at == 0, pair[0], pair[1]), jnp.where(at == 0, pair[1], pair[0])

    def in_order(at, own, other):
        return jnp.concatenate(pick(at, (own, other)), 0)

    def with_partner(value, name):
        return jnp.concatenate([value, swap(value, name)], 0)

    def shift(value, step):
        return lax.ppermute(value, "rows", [(d, (d + step) % tiles) for d in range(tiles)])

    def tile_gather(value):
        parts = [value] + [shift(value, step) for step in range(1, tiles)]
        blocks = [lax.select_n((tile - at) % tiles, *parts) for at in range(tiles)]
        return jnp.concatenate(blocks, 1)

    def tile_scatter(value):
        size = value.shape[1] // tiles
        blocks = [value[:, at * size : (at + 1) * size] for at in range(tiles)]
        total = lax.select_n(tile, *blocks).astype(f32)
        for step in range(1, tiles):
            sent = lax.select_n((tile + step) % tiles, *blocks)
            total = total + shift(sent, step).astype(f32)
        return total

    low_groups = [[g * low + d for d in range(low)] for g in range(8)]
    plane_groups = [
        [(j * 2 + c) * low + d for j in range(4)] for c in range(2) for d in range(low)
    ]

    def low_gather(value):
        if low == 1:
            return value
        return lax.all_gather(value, "images", axis=0, tiled=True, axis_index_groups=low_groups)

    def low_scatter(value):
        if low == 1:
            return value
        return lax.psum_scatter(
            value, "images", scatter_dimension=0, tiled=True, axis_index_groups=low_groups
        )

    def plane_gather(value):
        return lax.all_gather(value, "images", axis=0, tiled=True, axis_index_groups=plane_groups)

    def plane_scatter(value):
        return lax.psum_scatter(
            value, "images", scatter_dimension=0, tiled=True, axis_index_groups=plane_groups
        )

    def halves(value, at):
        half = value.shape[0] // 2
        return pick(at, (value[:half], value[half:]))


    qkv_low = low_gather(w_qkv)
    qkv_pairs = qkv_low.reshape(chunk, -1, 2, chunk)
    mine, other = pick(at_c, (qkv_pairs[:, :, 0], qkv_pairs[:, :, 1]))
    qkv_block = in_order(at_c, mine.reshape(chunk, -1), swap(other.reshape(chunk, -1), "c"))
    qkv_rows = tile_gather(qkv_block)
    qkv_full = plane_gather(qkv_rows)

    fc1_low = low_gather(w_fc1).reshape(chunk, 2, 2 * ff_part)
    mine, other = pick(at_c, (fc1_low[:, 0], fc1_low[:, 1]))
    fc1_core = in_order(at_c, mine, swap(other, "c"))
    fc1_mine, fc1_other = pick(at_x, (fc1_core[:, :ff_part], fc1_core[:, ff_part:]))
    fc2_low = low_gather(w_fc2)
    fc2_mine, fc2_other = halves(fc2_low, at_x)
    fc1_swapped = swap(fc1_other, "x")
    fc2_swapped = swap(fc2_other, "x")
    fc1_block = in_order(at_x, fc1_mine, fc1_swapped)
    fc2_block = in_order(at_x, fc2_mine, fc2_swapped)
    out_block = low_gather(w_out)
    rest_rows = tile_gather(jnp.concatenate([out_block, fc1_block, fc2_block], 0))
    out_rows = rest_rows[:chunk]
    fc1_rows = rest_rows[chunk : chunk + 4 * chunk]
    fc2_rows = rest_rows[5 * chunk :]
    out_full = plane_gather(out_rows)
    fc1_full = in_order(at_y, fc1_rows, swap(fc1_rows, "y"))
    fc2_full = in_order(at_y, fc2_rows, swap(fc2_rows, "y"))


    gain_one, shift_one = ln1_gain.astype(f32), ln1_bias.astype(f32)
    gain_two, shift_two = ln2_gain.astype(f32), ln2_bias.astype(f32)
    flat_tokens = tokens.astype(f32).reshape(slots, width)
    normal_one, inverse_one = normalize(flat_tokens)
    normed = (normal_one * gain_one + shift_one).astype(bf16).reshape(tokens.shape)

    down = [(d, d + 1) for d in range(tiles - 1)]
    up = [(d + 1, d) for d in range(tiles - 1)]
    above = lax.ppermute(normed[:, rows_here - HALO :], "rows", down)
    below = lax.ppermute(normed[:, :HALO], "rows", up)
    normed_ext = jnp.concatenate([above, normed, below], 1)
    normed_all = with_partner(normed_ext, "c")
    images = 2 * here
    normed_mid = normed_all[:, HALO : HALO + rows_here].reshape(images * cells, width)
    normed_all = normed_all.reshape(images * keys, width)


    orders = [bits["c"], bits["x"], bits["y"]]
    orders += [1 << b for b in range(low.bit_length() - 1)]
    steps_all = timesteps
    for bit in orders:
        steps_all = jnp.concatenate([steps_all, partner(steps_all, bit)], 0)
    time_rows = w_time.shape[0]
    half_width = width // 2
    feature = place * time_rows + jnp.arange(time_rows)
    exponent = (feature % half_width).astype(f32)
    frequency = jnp.exp(-math.log(10000.0) * exponent / half_width)
    phases = steps_all.astype(f32)[:, None] * frequency[None, :]
    timing = jnp.where(feature[None, :] < half_width, jnp.cos(phases), jnp.sin(phases)).astype(bf16)
    time_part = dot(timing, w_time)
    for bit in orders[:0:-1]:
        half = time_part.shape[0] // 2
        time_part = time_part[:half] + partner(time_part[half:], bit)
    turned = jnp.concatenate([time_part[here:], time_part[:here]], 0)
    time_part = time_part + swap(turned, "c")
    time_pairs = tile_gather(time_part).reshape(images, -1, 2, chunk)
    time_mine = pick(at_c, (time_pairs[:, :, 0], time_pairs[:, :, 1]))[0].reshape(images, width)
    half = width // 2
    time_query, time_value = time_mine[:, :half], time_mine[:, half:]


    heights_all = with_partner(heights, "c")
    widths_all = with_partner(widths, "c")
    query_row = jnp.arange(cells) // cols
    query_col = jnp.arange(cells) % cols
    key_row = jnp.arange(keys) // cols - HALO
    key_col = jnp.arange(keys) % cols
    near = jnp.abs(key_row[None, :] - query_row[:, None]) <= HALO
    itself = jnp.arange(keys)[None, :] == jnp.arange(cells)[:, None] + HALO * cols
    global_key = tile * rows_here + key_row
    key_ok = (
        (global_key[None, :] >= 0)
        & (global_key[None, :] < heights_all[:, None])
        & (key_col[None, :] < widths_all[:, None])
    )
    allowed = (key_ok[:, None, :] & near[None] | itself[None]).astype(f32)
    global_query = tile * rows_here + query_row
    valid = (global_query[None, :] < heights[:, None]) & (query_col[None, :] < widths[:, None])
    valid_mask = valid.reshape(slots, 1).astype(f32)

    heads = head_count // 2
    gaps = 2 * HALO + 1
    spans = 2 * cols - 1
    exact = lax.Precision.HIGHEST
    bucket_hits = (
        rel_index.reshape(-1)[:, None] == jnp.arange(rel_table.shape[0])[None, :]
    ).astype(f32)
    table_pairs = rel_table.astype(f32).reshape(rel_table.shape[0], -1, 2, 2)
    table_mine = pick(at_c, (table_pairs[:, :, 0], table_pairs[:, :, 1]))[0].reshape(-1, heads)
    offset_values = jnp.dot(bucket_hits, table_mine, precision=exact).T
    col_step = jnp.arange(cols)[None, :] - jnp.arange(cols)[:, None] + cols - 1
    step_hits = (jnp.arange(spans)[:, None] == col_step.reshape(1, -1)).astype(f32)
    spread = jnp.dot(offset_values.reshape(heads * gaps, spans), step_hits, precision=exact)
    strip = spread.reshape(heads, gaps, cols, cols).transpose(0, 2, 1, 3)
    strip = strip.reshape(heads, cols, gaps * cols).astype(bf16)
    bias = jnp.concatenate(
        [
            jnp.pad(strip, ((0, 0), (0, 0), (r * cols, keys - (r + gaps) * cols)))
            for r in range(rows_here)
        ],
        1,
    )


    query = (
        dot(normed_mid, qkv_full[:, :half]).reshape(images, cells, half) + time_query[:, None]
    ).astype(bf16)
    key = dot(normed_all, qkv_full[:, half : 2 * half]).astype(bf16).reshape(images, keys, half)
    value = (
        dot(normed_all, qkv_full[:, 2 * half :]).reshape(images, keys, half) + time_value[:, None]
    ).astype(bf16)
    attended, prob = attend(query, key, value, bias, allowed, scale)
    attended = attended.reshape(images * cells, half)

    def core_sum(part):
        size = part.shape[0] // 2
        return part[:size] + swap(part[size:].astype(bf16), "c").astype(f32)

    def quad_sum(part):
        size = part.shape[0] // 2
        part = part[:size] + swap(part[size:].astype(bf16), "c").astype(f32)
        size = size // 2
        return part[:size] + swap(part[size:].astype(bf16), "x").astype(f32)

    def quad_all(value):
        return with_partner(with_partner(value, "x"), "c")

    middle = flat_tokens + core_sum(dot(attended, out_full)) + out_bias.astype(f32)
    normal_two, inverse_two = normalize(middle)
    second = quad_all((normal_two * gain_two + shift_two).astype(bf16))


    grad_out = cotangent.astype(f32).reshape(slots, width) * valid_mask
    grad_mlp_own = grad_out.astype(bf16)
    grad_mlp = quad_all(grad_mlp_own)
    member = at_c * 2 + at_x
    bias_parts = fc1_bias.astype(f32).reshape(tiles, 4, ff_part)
    bias_mine = lax.dynamic_index_in_dim(bias_parts, member, 1, keepdims=False).reshape(-1)
    hidden_pre = dot(second, fc1_full) + bias_mine
    hidden_act, gelu_pull = jax.vjp(gelu_tanh, hidden_pre)
    hidden = hidden_act.astype(bf16)
    grad_fc2 = dot(hidden, grad_mlp, TN).astype(bf16)
    grad_pre = gelu_pull(dot(grad_mlp, fc2_full, NT))[0].astype(bf16)
    grad_second = quad_sum(dot(grad_pre, fc1_full, NT))
    grad_fc1 = dot(second, grad_pre, TN).astype(bf16)
    mlp_out = quad_sum(dot(hidden, fc2_full)) + fc2_bias.astype(f32)
    mixed = (valid_mask * (middle + mlp_out)).reshape(tokens.shape).astype(bf16)
    grad_fc2_bias = jnp.sum(grad_mlp_own, 0, dtype=f32)
    grad_fc1_bias = jnp.sum(grad_pre, 0, dtype=f32)

    grad_gain_two = jnp.sum(grad_second * normal_two, 0)
    grad_shift_two = jnp.sum(grad_second, 0)
    grad_middle = grad_out + norm_back(grad_second * gain_two, normal_two, inverse_two)
    grad_branch_own = grad_middle.astype(bf16)
    grad_out_bias = jnp.sum(grad_branch_own, 0, dtype=f32)
    grad_branch = with_partner(grad_branch_own, "c")


    grad_out_weight = dot(attended, grad_branch, TN).astype(bf16)
    grad_att = dot(grad_branch, out_full, NT).astype(bf16).reshape(images, cells, half)
    grad_query, grad_key, grad_value, grad_strip = attend_back(
        query, key, value, prob, grad_att, scale, cols
    )
    flat_query = grad_query.reshape(images * cells, half)
    flat_key = grad_key.reshape(images * keys, half)
    flat_value = grad_value.reshape(images * keys, half)
    grad_qkv = jnp.concatenate(
        [
            dot(normed_mid, flat_query, TN).astype(bf16),
            dot(normed_all, flat_key, TN).astype(bf16),
            dot(normed_all, flat_value, TN).astype(bf16),
        ],
        1,
    )
    grad_mid = dot(flat_query, qkv_full[:, :half], NT).reshape(images, rows_here, cols, width)
    grad_ext = dot(flat_key, qkv_full[:, half : 2 * half], NT) + dot(
        flat_value, qkv_full[:, 2 * half :], NT
    )
    grad_ext = grad_ext.reshape(images, key_rows, cols, width) + jnp.pad(
        grad_mid, ((0, 0), (HALO, HALO), (0, 0), (0, 0))
    )
    grad_ext = core_sum(grad_ext)
    from_below = lax.ppermute(grad_ext[:, :HALO].astype(bf16), "rows", up).astype(f32)
    from_above = lax.ppermute(grad_ext[:, HALO + rows_here :].astype(bf16), "rows", down)
    from_above = from_above.astype(f32)
    rest = ((0, 0), (rows_here - HALO, 0), (0, 0), (0, 0))
    grad_normed = (
        grad_ext[:, HALO : HALO + rows_here]
        + jnp.pad(from_below, rest)
        + jnp.pad(from_above, (rest[0], rest[1][::-1], rest[2], rest[3]))
    ).reshape(slots, width)
    grad_gain_one = jnp.sum(grad_normed * normal_one, 0)
    grad_shift_one = jnp.sum(grad_normed, 0)
    grad_input = grad_middle + norm_back(grad_normed * gain_one, normal_one, inverse_one)
    grad_tokens = grad_input.reshape(tokens.shape).astype(bf16)


    grad_strip = grad_strip[:, :, : gaps * cols].reshape(heads, cols, gaps, cols)
    grad_strip = grad_strip.transpose(0, 2, 1, 3).reshape(heads * gaps, cols * cols)
    grad_offsets = lax.dot_general(grad_strip, step_hits, NT, precision=exact)
    grad_table = lax.dot_general(
        bucket_hits, grad_offsets.reshape(heads, gaps * spans), (((0,), (1,)), ((), ())),
        precision=exact,
    )


    sums = jnp.concatenate(
        [
            jnp.sum(grad_query, 1, dtype=f32),
            jnp.sum(grad_value, 1, dtype=f32),
        ],
        -1,
    )
    sums = tile_scatter(sums).reshape(images, -1, 1, chunk)
    sums_other = swap(jnp.concatenate([sums[here:], sums[:here]], 0), "c")
    sums = jnp.concatenate(pick(at_c, (sums, sums_other)), 2).reshape(images, -1)
    for bit in orders[1:]:
        sums = jnp.concatenate([sums, partner(sums, bit)], 0)
    grad_time = lax.dot_general(timing.astype(f32), sums, TN, precision=exact)


    def over_y(grad):
        kept, sent = halves(grad, at_y)
        return (kept.astype(f32) + swap(sent, "y").astype(f32)).astype(bf16)

    fc2_sum = tile_scatter(over_y(grad_fc2))
    fc1_sum = tile_scatter(over_y(grad_fc1))
    out_sum = tile_scatter(plane_scatter(grad_out_weight))
    qkv_sum = tile_scatter(plane_scatter(grad_qkv))

    kept, sent = halves(fc2_sum, at_x)
    fc2_own = in_order(at_x, kept, swap(sent.astype(bf16), "x").astype(f32))
    kept, sent = halves(fc1_sum, at_x)
    fc1_pair = jnp.concatenate(pick(at_x, (kept, swap(sent.astype(bf16), "x").astype(f32))), 1)
    kept, sent = halves(fc1_pair, at_c)
    fc1_own = jnp.concatenate(pick(at_c, (kept, swap(sent.astype(bf16), "c").astype(f32))), 1)
    kept, sent = halves(qkv_sum, at_c)
    other = swap(sent.astype(bf16), "c").astype(f32)
    pair = pick(at_c, (kept.reshape(chunk, -1, 1, chunk), other.reshape(chunk, -1, 1, chunk)))
    qkv_own = jnp.concatenate(pair, 2).reshape(chunk, -1)


    mine = (jnp.arange(4) == member).astype(f32)
    fc1_bias_all = grad_fc1_bias.reshape(tiles, 1, ff_part) * mine[None, :, None]
    core = (jnp.arange(2) == at_c).astype(f32)
    table_all = grad_table.reshape(-1, heads // 2, 1, 2) * core[None, None, :, None]
    small = [
        grad_gain_one,
        grad_shift_one,
        table_all.reshape(-1),
        grad_out_bias,
        grad_gain_two,
        grad_shift_two,
        fc1_bias_all.reshape(-1),
        grad_fc2_bias,
    ]
    total = jnp.concatenate(small)
    for bit in orders:
        total = total + partner(total, bit)
    for step in range(tiles.bit_length() - 1):
        route = [(d, d ^ (1 << step)) for d in range(tiles)]
        total = total + lax.ppermute(total, "rows", route)
    pieces = []
    for part in small:
        pieces.append(total[: part.shape[0]])
        total = total[part.shape[0] :]
    return (
        mixed,
        grad_tokens,
        pieces[0],
        pieces[1],
        low_scatter(qkv_own),
        grad_time,
        pieces[2].reshape(rel_table.shape),
        low_scatter(out_sum),
        pieces[3],
        pieces[4],
        pieces[5],
        low_scatter(fc1_own),
        pieces[6],
        low_scatter(fc2_own),
        pieces[7],
    )


def solution(mesh):
    tokens, image, weight = P("images", "rows", None, None), P("images"), P("images", "rows")
    return jax.shard_map(
        shards,
        mesh=mesh,
        in_specs=(
            tokens, tokens, image, image, image, P(), P(), P(), weight, weight,
            P(), weight, P(), P(), P(), weight, P(), weight, P(),
        ),
        out_specs=(
            tokens, tokens, P(), P(), weight, weight, P(), weight, P(), P(),
            P(), weight, P(), weight, P(),
        ),
        check_vma=False,
    )
```

```python
import functools
import math

import jax
import jax.numpy as jnp
from jax import lax
from jax.experimental import pallas as pl
from jax.experimental.layout import Layout, with_layout_constraint
from jax.experimental.pallas import tpu as pltpu
from jax.sharding import PartitionSpec as P

HALO = 2
LANES = 128

norm_eps = 1e-06
masked_score = -1000000000.0

f32 = jnp.float32
bf16 = jnp.bfloat16

NN = (((1,), (0,)), ((), ()))
NT = (((1,), (1,)), ((), ()))
TN = (((0,), (0,)), ((), ()))


def dot(left, right, dims=NN):
    return lax.dot_general(left, right, dims, preferred_element_type=f32)


def row_major(value):
    return with_layout_constraint(value, Layout(major_to_minor=tuple(range(value.ndim))))


def normalize(values):
    centre = values - jnp.mean(values, -1, keepdims=True)
    spread = jnp.mean(centre * centre, -1, keepdims=True)
    inverse = lax.rsqrt(spread + norm_eps)
    return (centre * inverse, inverse)


def norm_back(grad_hat, normal_part, inverse):
    first_mean = jnp.mean(grad_hat, -1, keepdims=True)
    second_mean = jnp.mean(grad_hat * normal_part, -1, keepdims=True)
    return inverse * (grad_hat - first_mean - normal_part * second_mean)


def gelu_tanh(values):
    return jax.nn.gelu(values, approximate=True)


def window(head, head_dim, width):
    first, last = head * head_dim, (head + 1) * head_dim
    start = first // LANES * LANES
    stop = min(-(-last // LANES) * LANES, width)
    return first, last, start, stop


def lane_mask(first, last, start, stop, kind):
    lane = lax.broadcasted_iota(jnp.int32, (1, stop - start), 1) + start
    return jnp.where((lane >= first) & (lane < last), 1.0, 0.0).astype(kind)


def add_tiles(tiles, values, start, stop):
    for at in range(start, stop, LANES):
        part = values[:, at - start : min(at + LANES, stop) - start]
        tiles[at] = part if at not in tiles else tiles[at] + part


def store_tiles(ref, tiles, scale=None, rows=slice(None), base=0):
    for at, part in tiles.items():
        if scale is not None:
            part = part * scale
        ref[0, rows, base + at : base + at + part.shape[1]] = part.astype(ref.dtype)


def attend_kernel(heads, scale, edge, qkv_ref, bias_ref, allow_ref, o_ref, p_ref):
    half = o_ref.shape[-1]
    cells = o_ref.shape[1]
    allowed = allow_ref[0] > 0.5
    queries = qkv_ref[0, edge : edge + cells, :half]
    key = qkv_ref[0, :, half : 2 * half]
    value = qkv_ref[0, :, 2 * half :]
    tiles = {}
    for head in range(heads):
        span = window(head, half // heads, half)
        start, stop = span[2:]
        query = queries[:, start:stop] * lane_mask(*span, bf16)
        scores = dot(query, key[:, start:stop], NT) * scale + bias_ref[head].astype(f32)
        scores = jnp.where(allowed, scores, masked_score)
        expo = jnp.exp(scores - jnp.max(scores, -1, keepdims=True))
        prob = (expo / jnp.sum(expo, -1, keepdims=True)).astype(bf16)
        p_ref[0, head] = prob
        out = dot(prob, value[:, start:stop]) * lane_mask(*span, f32)
        add_tiles(tiles, out, start, stop)
    store_tiles(o_ref, tiles)


def attend_back_kernel(heads, scale, edge, cols, qkv_ref, p_ref, do_ref, d_ref, g_ref, sum_ref):
    cells, half = do_ref.shape[1:]
    rows = cells // cols
    middle = slice(edge, edge + cells)
    step = pl.program_id(0)

    @pl.when(step == 0)
    def _():
        sum_ref[...] = jnp.zeros_like(sum_ref)

    queries = qkv_ref[0, middle, :half]
    key = qkv_ref[0, :, half : 2 * half]
    value = qkv_ref[0, :, 2 * half :]
    dq_tiles, dk_tiles, dv_tiles = {}, {}, {}
    for head in range(heads):
        span = window(head, half // heads, half)
        start, stop = span[2:]
        mask = lane_mask(*span, bf16)
        query = queries[:, start:stop] * mask
        grad_out = do_ref[0, :, start:stop] * mask
        prob = p_ref[0, head]
        full = prob.astype(f32)
        weighted = full * dot(grad_out, value[:, start:stop], NT)
        grad_score = (weighted - full * jnp.sum(weighted, -1, keepdims=True)).astype(bf16)
        sum_ref[head] += grad_score.astype(f32)
        dq = dot(grad_score, key[:, start:stop]) * lane_mask(*span, f32)
        add_tiles(dq_tiles, dq, start, stop)
        add_tiles(dk_tiles, dot(grad_score, query, TN), start, stop)
        add_tiles(dv_tiles, dot(prob, grad_out, TN), start, stop)
    d_ref[0, :edge, :half] = jnp.zeros((edge, half), bf16)
    d_ref[0, edge + cells :, :half] = jnp.zeros((edge, half), bf16)
    store_tiles(d_ref, dq_tiles, scale, middle)
    store_tiles(d_ref, dk_tiles, scale, base=half)
    store_tiles(d_ref, dv_tiles, base=2 * half)

    @pl.when(step == pl.num_programs(0) - 1)
    def _():
        for head in range(heads):
            total = sum_ref[head, :cols]
            for row in range(1, rows):
                part = sum_ref[head, row * cols : (row + 1) * cols]
                total += pltpu.roll(part, part.shape[1] - row * cols, 1)
            g_ref[head] = total


def per_image(*dims):
    return pl.BlockSpec((1,) + dims, lambda i: (i,) + (0,) * len(dims))


def whole(*dims):
    return pl.BlockSpec(dims, lambda i: (0,) * len(dims))


def attend(qkv, bias, allowed, scale):
    images, keys, width = qkv.shape
    heads, cells, _ = bias.shape
    half = width // 3
    return pl.pallas_call(
        functools.partial(attend_kernel, heads, scale, (keys - cells) // 2),
        grid=(images,),
        in_specs=[per_image(keys, width), whole(heads, cells, keys), per_image(cells, keys)],
        out_specs=[per_image(cells, half), per_image(heads, cells, keys)],
        out_shape=[
            jax.ShapeDtypeStruct((images, cells, half), bf16),
            jax.ShapeDtypeStruct((images, heads, cells, keys), bf16),
        ],
        compiler_params=pltpu.CompilerParams(vmem_limit_bytes=32 << 20),
        cost_estimate=pl.CostEstimate(
            flops=4 * images * heads * cells * keys * 256,
            bytes_accessed=4 * images * heads * cells * keys,
            transcendentals=images * heads * cells * keys,
        ),
        name="attend",
    )(qkv, bias, allowed)


def attend_back(qkv, prob, grad_out, scale, cols):
    images, keys, width = qkv.shape
    heads = prob.shape[1]
    cells, half = grad_out.shape[1:]
    return pl.pallas_call(
        functools.partial(attend_back_kernel, heads, scale, (keys - cells) // 2, cols),
        grid=(images,),
        in_specs=[per_image(keys, width), per_image(heads, cells, keys), per_image(cells, half)],
        out_specs=[per_image(keys, width), whole(heads, cols, keys)],
        out_shape=[
            jax.ShapeDtypeStruct((images, keys, width), bf16),
            jax.ShapeDtypeStruct((heads, cols, keys), f32),
        ],
        scratch_shapes=[pltpu.VMEM((heads, cells, keys), f32)],
        compiler_params=pltpu.CompilerParams(vmem_limit_bytes=32 << 20),
        cost_estimate=pl.CostEstimate(
            flops=8 * images * heads * cells * keys * 256,
            bytes_accessed=4 * images * heads * cells * keys,
            transcendentals=0,
        ),
        name="attend_back",
    )(qkv, prob, grad_out)


def on_blocks(kernel, spot, values, shapes, name):
    block = pl.BlockSpec(memory_space=pltpu.VMEM)
    return pl.pallas_call(
        kernel,
        in_specs=[pl.BlockSpec(memory_space=pltpu.SMEM)] + [block] * len(values),
        out_specs=[block] * len(shapes),
        out_shape=[jax.ShapeDtypeStruct(shape, kind) for shape, kind in shapes],
        compiler_params=pltpu.CompilerParams(vmem_limit_bytes=32 << 20),
        name=name,
    )(spot, *values)


def for_each(value, count, body):
    for at in range(count):
        pl.when(value == at)(functools.partial(body, at))


def source_row(spot, group, size, by_core):
    side = jnp.bitwise_xor(spot[1], group >> 1)
    core = jnp.bitwise_xor(spot[2], group & 1) if by_core else group & 1
    return pl.multiple_of((side * 2 + core) * size, 16)


def split_core_kernel(spot, w_ref, keep_ref, send_ref):
    half = keep_ref.shape[1]

    def body(core):
        keep_ref[...] = w_ref[:, core * half : (core + 1) * half]
        send_ref[...] = w_ref[:, (1 - core) * half : (2 - core) * half]

    for_each(spot[2], 2, body)


def split_side_kernel(spot, own_ref, got_ref, fc2_ref, keep1_ref, keep2_ref, send_ref):
    rows, wide = own_ref.shape
    part = wide // 2

    def body(side):
        for at, ref in enumerate((own_ref, got_ref)):
            lanes = slice(at * part, (at + 1) * part)
            keep1_ref[:, lanes] = ref[:, side * part : (side + 1) * part]
            send_ref[:, lanes] = ref[:, (1 - side) * part : (2 - side) * part]
        for at in range(2):
            first = (side * 2 + at) * rows
            other = ((1 - side) * 2 + at) * rows
            keep2_ref[:, at * part : (at + 1) * part] = fc2_ref[first : first + rows]
            send_ref[:, wide + at * part : wide + (at + 1) * part] = fc2_ref[other : other + rows]

    for_each(spot[1], 2, body)


def fill_lanes(ref, first):
    if first < ref.shape[-1]:
        ref[:, first:] = jnp.zeros((ref.shape[0], ref.shape[-1] - first), ref.dtype)


def join_side_kernel(spot, out_ref, keep1_ref, keep2_ref, got_ref, one_ref, two_ref):
    part = out_ref.shape[1]
    wide = keep1_ref.shape[1]
    one_ref[:, :part] = out_ref[...]
    one_ref[:, part : part + wide] = keep1_ref[...]
    one_ref[:, part + wide : part + 2 * wide] = got_ref[:, :wide]
    fill_lanes(one_ref, part + 2 * wide)
    two_ref[:, :wide] = keep2_ref[...]
    two_ref[:, wide:] = got_ref[:, wide:]


def unpack_kernel(by_core, lead, sides, spot, pieces, *outs):
    rows = pieces.shape[1] // sides
    part = outs[-1].shape[1] // 4
    for block in range(4):
        lanes = slice(block * part, (block + 1) * part)
        if lead:
            outs[0][:, lanes] = pieces[block, :, :part]
        for side in range(sides):
            base = jnp.bitwise_xor(spot[3], side) * 4 * rows if sides > 1 else 0
            for group in range(4):
                first = (group + lead) * part
                row = base + source_row(spot, group, rows, by_core)
                outs[-1][pl.ds(pl.multiple_of(row, 16), rows), lanes] = pieces[
                    block, side * rows : (side + 1) * rows, first : first + part
                ]


def pack_kernel(by_core, spot, grad_ref, got_ref, out):
    rows = out.shape[1]
    part = grad_ref.shape[1] // 4
    base = spot[3] * got_ref.shape[0]
    for block in range(4):
        lanes = slice(block * part, (block + 1) * part)
        for group in range(4):
            row = source_row(spot, group, rows, by_core)
            own = grad_ref[pl.ds(pl.multiple_of(base + row, 16), rows), lanes]
            total = own.astype(f32) + got_ref[pl.ds(row, rows), lanes].astype(f32)
            out[block, :, group * part : (group + 1) * part] = total.astype(out.dtype)


def split_sums_kernel(spot, one, two, keep1_ref, keep2_ref, send_ref):
    wide = keep1_ref.shape[1]
    keep1_ref[...] = one[:, :wide]
    keep2_ref[...] = two[:, :wide]
    send_ref[:, :wide] = one[:, wide:]
    send_ref[:, wide:] = two[:, wide:]


def turn_core_kernel(spot, keep1_ref, got_ref, send_ref):
    part = send_ref.shape[1] // 2
    send_ref[:, :part] = keep1_ref[:, part:]
    send_ref[:, part:] = got_ref[:, part : 2 * part]


def finish_kernel(spot, keep1_ref, keep2_ref, side_ref, core_ref, fc1_ref, fc2_ref):
    rows, part = fc1_ref.shape[0], fc2_ref.shape[1]

    def body(place):
        core, side = place // 2, place % 2
        parts = {
            (core, side): keep1_ref[:, :part],
            (core, 1 - side): side_ref[:, :part],
            (1 - core, side): core_ref[:, :part],
            (1 - core, 1 - side): core_ref[:, part:],
        }
        for (c, x), value in parts.items():
            fc1_ref[:, (2 * c + x) * part : (2 * c + x + 1) * part] = value.astype(f32)
        for at in range(2):
            lanes = slice(at * part, (at + 1) * part)
            first, other = (side * 2 + at) * rows, ((1 - side) * 2 + at) * rows
            fc2_ref[first : first + rows] = keep2_ref[:, lanes].astype(f32)
            fc2_ref[other : other + rows] = side_ref[:, (2 + at) * part : (3 + at) * part].astype(f32)

    for_each(spot[2] * 2 + spot[1], 4, body)


def qkv_blocks(tile, rows, count):
    for block in range(4):
        for at in range(count):
            for core in range(2):
                yield (
                    block,
                    core,
                    slice((2 * at + core) * rows, (2 * at + core + 1) * rows),
                    slice((block * count + at) * rows, (block * count + at + 1) * rows),
                )


def unpack_qkv_kernel(spot, *refs):
    pieces, kept = refs[:4], refs[4:]
    rows, wide = pieces[0].shape

    def body(place):
        tile, mine = place // 2, place % 2
        for block, core, there, here in qkv_blocks(tile, rows, wide // (2 * rows)):
            kept[core != mine][:, here] = pieces[(tile - block) % 4][:, there]

    for_each(spot[0] * 2 + spot[2], 8, body)


def pack_qkv_kernel(spot, own_ref, got_ref, last_ref, *outs):
    rows, wide = outs[0].shape
    part = last_ref.shape[1] // 4
    wide = wide - part

    def body(place):
        tile, mine = place // 2, place % 2
        for block, core, there, here in qkv_blocks(tile, rows, wide // (2 * rows)):
            source = own_ref if core == mine else got_ref
            outs[(block - tile) % 4][:, there] = source[:, here]
        for block in range(4):
            lanes = slice(block * part, (block + 1) * part)
            outs[(block - tile) % 4][:, wide:] = last_ref[:, lanes]

    for_each(spot[0] * 2 + spot[2], 8, body)


def place_kernel(count, rows_ref, *refs):
    ins, out = refs[:count], refs[count]
    for at, ref in enumerate(ins):
        out[pl.ds(pl.multiple_of(rows_ref[at], 16), ref.shape[0])] = ref[...]


def place_rows(pieces, rows, name):
    height = sum(piece.shape[0] for piece in pieces)
    shape = (height, pieces[0].shape[1]), pieces[0].dtype
    kernel = functools.partial(place_kernel, len(pieces))
    return on_blocks(kernel, jnp.stack(rows).astype(jnp.int32), pieces, [shape], name)[0]


def shards(
    tokens,
    cotangent,
    heights,
    widths,
    timesteps,
    rel_index,
    ln1_gain,
    ln1_bias,
    w_qkv,
    w_time,
    rel_table,
    w_out,
    out_bias,
    ln2_gain,
    ln2_bias,
    w_fc1,
    fc1_bias,
    w_fc2,
    fc2_bias,
):
    here, rows_here, cols, width = tokens.shape
    cells = rows_here * cols
    slots = here * cells
    key_rows = rows_here + 2 * HALO
    keys = key_rows * cols
    head_count = rel_table.shape[1]
    head_dim = width // head_count
    scale = head_dim ** (-0.5)
    image_devices = lax.axis_size("images")
    tiles = lax.axis_size("rows")
    low = image_devices // 8
    chunk = width // 8
    quarter = width // 4
    ff_part = fc1_bias.shape[0] // 16
    place = lax.axis_index("images")
    tile = lax.axis_index("rows")
    bits = {"c": low, "x": 2 * low, "y": 4 * low}
    at_c, at_x, at_y = (place // bits[name] % 2 for name in "cxy")


    def partner(value, bit):
        route = [(d, d ^ bit) for d in range(image_devices)]
        return lax.ppermute(value, "images", route)

    def swap(value, name):
        return partner(value, bits[name])

    def pick(at, pair):
        return jnp.where(at == 0, pair[0], pair[1]), jnp.where(at == 0, pair[1], pair[0])

    def after(value, *others):
        return lax.optimization_barrier((value,) + others)[0]

    def all_after(values, *others):
        return list(lax.optimization_barrier(tuple(values) + others))[: len(values)]

    def with_partner(value, name):
        return jnp.concatenate([value, swap(value, name)], 0)

    def shift(value, step):
        return lax.ppermute(value, "rows", [(d, (d + step) % tiles) for d in range(tiles)])

    def tiles_all(value):
        return lax.all_gather(value, "rows", axis=0)

    def tiles_sum(value):
        return lax.psum_scatter(value, "rows", scatter_dimension=0)

    def shifts(value):
        return [shift(value, step) for step in range(1, tiles)]

    def tile_gather(value):
        for bit in (1, 2):
            other = lax.ppermute(value, "rows", [(d, d ^ bit) for d in range(tiles)])
            value = jnp.concatenate(pick(tile // bit % 2, (value, other)), 1)
        return value

    def tile_scatter(value):
        size = value.shape[1] // tiles
        blocks = [value[:, at * size : (at + 1) * size] for at in range(tiles)]
        total = lax.select_n(tile, *blocks).astype(f32)
        for step in range(1, tiles):
            sent = lax.select_n((tile + step) % tiles, *blocks)
            total = total + shift(sent, step).astype(f32)
        return total

    low_groups = [[g * low + d for d in range(low)] for g in range(8)]
    def low_gather(value):
        if low == 1:
            return value
        return lax.all_gather(value, "images", axis=0, tiled=True, axis_index_groups=low_groups)

    def low_scatter(value):
        if low == 1:
            return value
        return lax.psum_scatter(
            value, "images", scatter_dimension=0, tiled=True, axis_index_groups=low_groups
        )

    def part_of(value, at):
        return lax.dynamic_index_in_dim(value, at, 0, keepdims=False)


    slot_row = tile * rows_here + jnp.arange(cells) // cols
    slot_col = jnp.arange(cells) % cols
    valid = (slot_row[None, :] < heights[:, None]) & (slot_col[None, :] < widths[:, None])
    valid_mask = valid.reshape(slots, 1).astype(f32)
    grad_out = cotangent.astype(f32).reshape(slots, width) * valid_mask
    grad_mlp_own = grad_out.astype(bf16)


    gain_one, shift_one = ln1_gain.astype(f32), ln1_bias.astype(f32)
    gain_two, shift_two = ln2_gain.astype(f32), ln2_bias.astype(f32)
    flat_tokens = tokens.astype(f32).reshape(slots, width)
    normal_one, inverse_one = normalize(flat_tokens)
    normed = (normal_one * gain_one + shift_one).astype(bf16).reshape(tokens.shape)

    down = [(d, d + 1) for d in range(tiles - 1)]
    up = [(d + 1, d) for d in range(tiles - 1)]
    images = 2 * here


    spot = jnp.stack([tile, at_x, at_c, at_y]).astype(jnp.int32)
    w_qkv, w_out, w_fc1, w_fc2 = (low_gather(w) for w in (w_qkv, w_out, w_fc1, w_fc2))
    wide = 2 * ff_part
    padded = -(-(ff_part + 2 * wide) // LANES) * LANES

    def matrices(*dims):
        return [(dim, bf16) for dim in dims]

    qkv_parts = [w_qkv] + shifts(w_qkv)

    fc1_keep, fc1_send = on_blocks(
        split_core_kernel, spot, [w_fc1], matrices((chunk, wide), (chunk, wide)), "split_core"
    )
    fc1_got = swap(fc1_send, "c")
    keep1, keep2, send = on_blocks(
        split_side_kernel,
        spot,
        [fc1_keep, fc1_got, w_fc2],
        matrices((chunk, wide), (chunk, wide), (chunk, 2 * wide)),
        "split_side",
    )
    got = swap(send, "x")
    one, two = on_blocks(
        join_side_kernel,
        spot,
        [w_out, keep1, keep2, got],
        matrices((chunk, padded), (chunk, 2 * wide)),
        "join_side",
    )
    two = with_partner(two, "y")
    one_parts = tiles_all(one)
    two_parts = tiles_all(two)


    orders = [bits["c"], bits["x"], bits["y"]]
    orders += [1 << b for b in range(low.bit_length() - 1)]
    facts = with_partner(jnp.stack([timesteps, heights, widths], 1), "c")
    heights_all, widths_all = facts[:, 1], facts[:, 2]
    steps_all = facts[:, 0]
    for bit in orders[1:]:
        steps_all = jnp.concatenate([steps_all, partner(steps_all, bit)], 0)
    time_rows = w_time.shape[0]
    half_width = width // 2
    feature = place * time_rows + jnp.arange(time_rows)
    exponent = (feature % half_width).astype(f32)
    frequency = jnp.exp(-math.log(10000.0) * exponent / half_width)
    phases = steps_all.astype(f32)[:, None] * frequency[None, :]
    timing = jnp.where(feature[None, :] < half_width, jnp.cos(phases), jnp.sin(phases)).astype(bf16)
    time_part = dot(timing, after(w_time, *qkv_parts[1:]))
    for bit in orders[:0:-1]:
        half = time_part.shape[0] // 2
        time_part = time_part[:half] + partner(time_part[half:], bit)
    turned = jnp.concatenate([time_part[here:], time_part[:here]], 0)
    time_part = time_part + swap(turned, "c")
    qkv_keep, qkv_send = on_blocks(
        unpack_qkv_kernel,
        spot,
        qkv_parts,
        matrices((chunk, 12 * chunk), (chunk, 12 * chunk)),
        "unpack_qkv",
    )
    edges = [normed[:, rows_here - HALO :], normed[:, :HALO]]
    edges = all_after(edges, qkv_keep)
    above = lax.ppermute(edges[0], "rows", down)
    below = lax.ppermute(edges[1], "rows", up)
    normed_ext = jnp.concatenate([above, normed, below], 1)
    normed_all = with_partner(normed_ext, "c").reshape(images * keys, width)

    qkv_pair = jnp.concatenate([qkv_keep, swap(qkv_send, "c")], 0)
    qkv_pair = after(qkv_pair, time_part, two)
    qkv_x, qkv_y = swap(qkv_pair, "x"), swap(qkv_pair, "y")
    qkv_x, qkv_y = all_after([qkv_x, qkv_y], normed_all)
    qkv_far = [swap(qkv_x[:chunk], "y"), swap(qkv_y[chunk:], "x")]
    qkv_far = all_after(qkv_far, one_parts)
    spots = at_y * 4 + at_x * 2 + at_c
    qkv_full = place_rows(
        [qkv_pair[:chunk], qkv_pair[chunk:], qkv_x[:chunk], qkv_x[chunk:]]
        + [qkv_y[:chunk], qkv_y[chunk:]]
        + qkv_far,
        [jnp.bitwise_xor(spots, step) * chunk for step in range(8)],
        "place_qkv",
    )

    out_rows, fc1_rows = on_blocks(
        functools.partial(unpack_kernel, True, 1, 1),
        spot,
        [after(one_parts, qkv_full)],
        matrices((chunk, width), (4 * chunk, 4 * ff_part)),
        "unpack_fc1",
    )
    out_x, out_y = swap(out_rows, "x"), swap(out_rows, "y")
    out_xy = swap(out_y, "x")
    places = at_y * 2 + at_x
    out_full = place_rows(
        [out_rows, out_x, out_y, out_xy],
        [jnp.bitwise_xor(places, step) * chunk for step in range(4)],
        "place_out",
    )

    fc1_rows = after(fc1_rows, out_y)
    fc1_got = swap(fc1_rows, "y")
    fc1_full = place_rows(
        [fc1_rows, fc1_got], [at_y * 4 * chunk, (1 - at_y) * 4 * chunk], "place_fc1"
    )
    grad_mlp_x = with_partner(after(grad_mlp_own, qkv_full), "x")
    grad_mlp = with_partner(grad_mlp_x, "c")

    time_pairs = tile_gather(time_part).reshape(images, -1, 2, chunk)
    time_mine = pick(at_c, (time_pairs[:, :, 0], time_pairs[:, :, 1]))[0].reshape(images, width)
    half = width // 2
    time_all = jnp.concatenate(
        [time_mine[:, :half], jnp.zeros((images, half), f32), time_mine[:, half:]], 1
    )


    query_row = jnp.arange(cells) // cols
    query_col = jnp.arange(cells) % cols
    key_row = jnp.arange(keys) // cols - HALO
    key_col = jnp.arange(keys) % cols
    near = jnp.abs(key_row[None, :] - query_row[:, None]) <= HALO
    itself = jnp.arange(keys)[None, :] == jnp.arange(cells)[:, None] + HALO * cols
    global_key = tile * rows_here + key_row
    key_ok = (
        (global_key[None, :] >= 0)
        & (global_key[None, :] < heights_all[:, None])
        & (key_col[None, :] < widths_all[:, None])
    )
    allowed = (key_ok[:, None, :] & near[None] | itself[None]).astype(f32)
    heads = head_count // 2
    gaps = 2 * HALO + 1
    spans = 2 * cols - 1
    exact = lax.Precision.HIGHEST
    bucket_hits = (
        rel_index.reshape(-1)[:, None] == jnp.arange(rel_table.shape[0])[None, :]
    ).astype(f32)
    table_pairs = rel_table.astype(f32).reshape(rel_table.shape[0], -1, 2, 2)
    table_mine = pick(at_c, (table_pairs[:, :, 0], table_pairs[:, :, 1]))[0].reshape(-1, heads)
    offset_values = jnp.dot(bucket_hits, table_mine, precision=exact).T
    col_step = jnp.arange(cols)[None, :] - jnp.arange(cols)[:, None] + cols - 1
    step_hits = (jnp.arange(spans)[:, None] == col_step.reshape(1, -1)).astype(f32)
    spread = jnp.dot(offset_values.reshape(heads * gaps, spans), step_hits, precision=exact)
    strip = spread.reshape(heads, gaps, cols, cols).transpose(0, 2, 1, 3)
    strip = strip.reshape(heads, cols, gaps * cols).astype(bf16)
    bias = jnp.concatenate(
        [
            jnp.pad(strip, ((0, 0), (0, 0), (r * cols, keys - (r + gaps) * cols)))
            for r in range(rows_here)
        ],
        1,
    )


    normed_here = after(normed_all, out_rows)
    qkv = (
        dot(normed_here, qkv_full).reshape(images, keys, 3 * half) + time_all[:, None]
    ).astype(bf16)
    attended, prob = attend(after(qkv, out_x, out_y), bias, allowed, scale)
    attended = after(attended.reshape(images * cells, half), grad_mlp_x)

    def core_sum(left, right, dims=NN):
        size = left.shape[0] // 2
        sent = swap(dot(left[size:], right, dims).astype(bf16), "c")
        return dot(left[:size], right, dims) + sent.astype(f32)

    def quad_sum(left, right, dims=NN):
        part = core_sum(left, right, dims)
        size = part.shape[0] // 2
        return part[:size] + swap(part[size:].astype(bf16), "x").astype(f32)

    middle = flat_tokens + core_sum(attended, out_full) + out_bias.astype(f32)
    normal_two, inverse_two = normalize(middle)
    second = with_partner((normal_two * gain_two + shift_two).astype(bf16), "x")
    second = with_partner(after(second, fc1_full), "c")


    member = at_c * 2 + at_x
    bias_parts = fc1_bias.astype(f32).reshape(tiles, 4, ff_part)
    bias_mine = lax.dynamic_index_in_dim(bias_parts, member, 1, keepdims=False).reshape(-1)
    hidden_pre = dot(second, fc1_full) + bias_mine
    hidden_act, gelu_pull = jax.vjp(gelu_tanh, hidden_pre)
    hidden = hidden_act.astype(bf16)
    (fc2_full,) = on_blocks(
        functools.partial(unpack_kernel, False, 0, 2),
        spot,
        [after(two_parts, hidden)],
        matrices((8 * chunk, width)),
        "unpack_fc2",
    )
    grad_fc2 = dot(hidden, grad_mlp, TN).astype(bf16)
    grad_pre = gelu_pull(dot(after(grad_mlp, grad_fc2), fc2_full, NT))[0].astype(bf16)
    grad_second = quad_sum(grad_pre, fc1_full, NT)
    grad_fc1 = dot(second, grad_pre, TN).astype(bf16)
    grad_fc2_bias = jnp.sum(grad_mlp_own, 0, dtype=f32)
    grad_fc1_bias = jnp.sum(grad_pre, 0, dtype=f32)

    grad_gain_two = jnp.sum(grad_second * normal_two, 0)
    grad_shift_two = jnp.sum(grad_second, 0)
    grad_middle = grad_out + norm_back(grad_second * gain_two, normal_two, inverse_two)
    grad_branch_own = grad_middle.astype(bf16)
    grad_out_bias = jnp.sum(grad_branch_own, 0, dtype=f32)
    grad_branch = with_partner(grad_branch_own, "c")


    def add_bf16(one, two):
        return (one.astype(f32) + two.astype(f32)).astype(bf16)

    def sides(grad):
        return grad.reshape((2, -1) + grad.shape[1:])

    fc2_got = swap(part_of(sides(grad_fc2), 1 - at_y), "y")
    fc1_got = swap(part_of(sides(grad_fc1), 1 - at_y), "y")
    grad_att = dot(grad_branch, out_full, NT).astype(bf16)
    grad_out_weight = dot(attended, grad_branch, TN).astype(bf16)
    out_sides = sides(grad_out_weight)
    out_sent = part_of(out_sides, 1 - at_y)
    (two_packed,) = on_blocks(
        functools.partial(pack_kernel, False),
        spot,
        [grad_fc2, after(fc2_got, grad_att)],
        matrices((tiles, chunk, 2 * wide)),
        "pack_fc2",
    )
    grad_att = after(grad_att, out_sent, two_packed).reshape(images, cells, half)
    two_sum = tiles_sum(two_packed)
    out_got = swap(out_sent, "y")

    grad_proj, grad_strip = attend_back(qkv, prob, grad_att, scale, cols)
    flat_proj = grad_proj.reshape(images * keys, 3 * half)
    grad_qkv = row_major(dot(normed_all, flat_proj, TN).astype(bf16))
    blocks = grad_qkv.reshape(2, 2, 2, chunk, 12 * chunk)

    def blocks_at(y, x, core):
        first = [0 if at is None else at for at in (y, x, core)] + [0, 0]
        size = [2 if at is None else 1 for at in (y, x, core)] + list(blocks.shape[3:])
        return lax.dynamic_slice(blocks, first, size).reshape(-1, chunk, 12 * chunk)

    own_sent = blocks_at(1 - at_y, None, at_c)
    other_sent = blocks_at(None, 1 - at_x, 1 - at_c)
    own_got, other_got = swap(own_sent, "y"), swap(other_sent, "x")
    out_mine = sides(add_bf16(part_of(out_sides, at_y), after(out_got, grad_qkv)))
    out_got = swap(part_of(out_mine, 1 - at_x), "x")
    out_mine = add_bf16(part_of(out_mine, at_x), out_got)

    (one_packed,) = on_blocks(
        functools.partial(pack_kernel, True),
        spot,
        [grad_fc1, after(fc1_got, grad_qkv)],
        matrices((tiles, chunk, 2 * wide)),
        "pack_fc1",
    )
    one_sum = tiles_sum(one_packed)
    flat_proj = after(flat_proj, own_sent, other_sent, two_sum, one_packed)
    grad_ext = core_sum(flat_proj, qkv_full, NT).reshape(here, key_rows, cols, width)
    mlp_out = quad_sum(after(hidden, own_sent, other_sent), fc2_full) + fc2_bias.astype(f32)
    mixed = (valid_mask * (middle + mlp_out)).reshape(tokens.shape).astype(bf16)

    from_below = lax.ppermute(grad_ext[:, :HALO].astype(bf16), "rows", up).astype(f32)
    from_above = lax.ppermute(grad_ext[:, HALO + rows_here :].astype(bf16), "rows", down)
    from_above = from_above.astype(f32)
    rest = ((0, 0), (rows_here - HALO, 0), (0, 0), (0, 0))
    grad_normed = (
        grad_ext[:, HALO : HALO + rows_here]
        + jnp.pad(from_below, rest)
        + jnp.pad(from_above, (rest[0], rest[1][::-1], rest[2], rest[3]))
    ).reshape(slots, width)
    grad_gain_one = jnp.sum(grad_normed * normal_one, 0)
    grad_shift_one = jnp.sum(grad_normed, 0)
    grad_input = grad_middle + norm_back(grad_normed * gain_one, normal_one, inverse_one)
    grad_tokens = grad_input.reshape(tokens.shape).astype(bf16)


    grad_strip = grad_strip[:, :, : gaps * cols].reshape(heads, cols, gaps, cols)
    grad_strip = grad_strip.transpose(0, 2, 1, 3).reshape(heads * gaps, cols * cols)
    grad_offsets = lax.dot_general(grad_strip, step_hits, NT, precision=exact)
    grad_table = lax.dot_general(
        bucket_hits, grad_offsets.reshape(heads, gaps * spans), (((0,), (1,)), ((), ())),
        precision=exact,
    )


    sums = jnp.sum(grad_proj, 1, dtype=f32)
    sums = jnp.concatenate([sums[:, :half], sums[:, 2 * half :]], 1)
    sums = tile_scatter(sums).reshape(images, -1, 1, chunk)
    sums_other = swap(jnp.concatenate([sums[here:], sums[:here]], 0), "c")
    sums = jnp.concatenate(pick(at_c, (sums, sums_other)), 2).reshape(images, -1)
    for bit in orders[1:]:
        sums = jnp.concatenate([sums, partner(sums, bit)], 0)
    grad_time = lax.dot_general(timing.astype(f32), sums, TN, precision=exact)


    keep1, keep2, send = on_blocks(
        split_sums_kernel,
        spot,
        [one_sum, two_sum],
        matrices((chunk, wide), (chunk, wide), (chunk, 2 * wide)),
        "split_sums",
    )
    side_got = swap(send, "x")
    (send,) = on_blocks(
        turn_core_kernel, spot, [keep1, side_got], matrices((chunk, wide)), "turn_core"
    )
    fc1_own, fc2_own = on_blocks(
        finish_kernel,
        spot,
        [keep1, keep2, side_got, swap(send, "c")],
        [((chunk, 2 * wide), f32), ((4 * chunk, ff_part), f32)],
        "finish",
    )

    own_two = add_bf16(blocks_at(at_y, None, at_c), own_got)
    other_two = add_bf16(blocks_at(None, at_x, 1 - at_c), other_got)
    own_got = swap(part_of(own_two, 1 - at_x), "x")
    other_got = swap(part_of(other_two, 1 - at_y), "y")
    own_rows = add_bf16(part_of(own_two, at_x), own_got)
    other_rows = add_bf16(part_of(other_two, at_y), other_got)
    other_rows = swap(other_rows, "c")
    last_parts = on_blocks(
        pack_qkv_kernel,
        spot,
        [own_rows, other_rows, out_mine],
        matrices(*[(chunk, 6 * chunk + quarter)] * 4),
        "pack_qkv",
    )
    last = last_parts[0].astype(f32)
    for step in range(1, tiles):
        last = last + shift(last_parts[step], step).astype(f32)
    qkv_own, out_own = last[:, : 6 * chunk], last[:, 6 * chunk :]


    mine = (jnp.arange(4) == member).astype(f32)
    fc1_bias_all = grad_fc1_bias.reshape(tiles, 1, ff_part) * mine[None, :, None]
    core = (jnp.arange(2) == at_c).astype(f32)
    table_all = grad_table.reshape(-1, heads // 2, 1, 2) * core[None, None, :, None]
    small = [
        grad_gain_one,
        grad_shift_one,
        table_all.reshape(-1),
        grad_out_bias,
        grad_gain_two,
        grad_shift_two,
        fc1_bias_all.reshape(-1),
        grad_fc2_bias,
    ]
    total = jnp.concatenate(small)
    for bit in orders:
        total = total + partner(total, bit)
    for step in range(tiles.bit_length() - 1):
        route = [(d, d ^ (1 << step)) for d in range(tiles)]
        total = total + lax.ppermute(total, "rows", route)
    pieces = []
    for part in small:
        pieces.append(total[: part.shape[0]])
        total = total[part.shape[0] :]
    return (
        mixed,
        grad_tokens,
        pieces[0],
        pieces[1],
        low_scatter(qkv_own),
        grad_time,
        pieces[2].reshape(rel_table.shape),
        low_scatter(out_own),
        pieces[3],
        pieces[4],
        pieces[5],
        low_scatter(fc1_own),
        pieces[6],
        low_scatter(fc2_own),
        pieces[7],
    )


def solution(mesh):
    tokens, image, weight = P("images", "rows", None, None), P("images"), P("images", "rows")
    return jax.shard_map(
        shards,
        mesh=mesh,
        in_specs=(
            tokens, tokens, image, image, image, P(), P(), P(), weight, weight,
            P(), weight, P(), P(), P(), weight, P(), weight, P(),
        ),
        out_specs=(
            tokens, tokens, P(), P(), weight, weight, P(), weight, P(), P(),
            P(), weight, P(), weight, P(),
        ),
        check_vma=False,
    )
```

```python
import functools
import math

import jax
import jax.numpy as jnp
from jax import lax
from jax.experimental import pallas as pl
from jax.experimental.layout import Layout, with_layout_constraint
from jax.experimental.pallas import tpu as pltpu
from jax.sharding import PartitionSpec as P

HALO = 2
LANES = 128

norm_eps = 1e-06
masked_score = -1000000000.0

f32 = jnp.float32
bf16 = jnp.bfloat16

NN = (((1,), (0,)), ((), ()))
NT = (((1,), (1,)), ((), ()))
TN = (((0,), (0,)), ((), ()))


def dot(left, right, dims=NN):
    return lax.dot_general(left, right, dims, preferred_element_type=f32)


def row_major(value):
    return with_layout_constraint(value, Layout(major_to_minor=tuple(range(value.ndim))))


def normalize(values):
    centre = values - jnp.mean(values, -1, keepdims=True)
    spread = jnp.mean(centre * centre, -1, keepdims=True)
    inverse = lax.rsqrt(spread + norm_eps)
    return (centre * inverse, inverse)


def norm_back(grad_hat, normal_part, inverse):
    first_mean = jnp.mean(grad_hat, -1, keepdims=True)
    second_mean = jnp.mean(grad_hat * normal_part, -1, keepdims=True)
    return inverse * (grad_hat - first_mean - normal_part * second_mean)


def gelu_and_slope(values):
    slant = math.sqrt(2.0 / math.pi)
    square = values * values
    curve = jnp.tanh(slant * values * (1.0 + 0.044715 * square))
    lift = 0.5 * (1.0 + curve)
    bend = 0.5 * values * (1.0 - curve * curve) * slant * (1.0 + 3.0 * 0.044715 * square)
    return values * lift, lift + bend


def window(head, head_dim, width):
    first, last = head * head_dim, (head + 1) * head_dim
    start = first // LANES * LANES
    stop = min(-(-last // LANES) * LANES, width)
    return first, last, start, stop


def lane_mask(first, last, start, stop, kind):
    lane = lax.broadcasted_iota(jnp.int32, (1, stop - start), 1) + start
    return jnp.where((lane >= first) & (lane < last), 1.0, 0.0).astype(kind)


def add_tiles(tiles, values, start, stop):
    for at in range(start, stop, LANES):
        part = values[:, at - start : min(at + LANES, stop) - start]
        tiles[at] = part if at not in tiles else tiles[at] + part


def store_tiles(ref, tiles, scale=None, rows=slice(None), base=0):
    for at, part in tiles.items():
        if scale is not None:
            part = part * scale
        ref[0, rows, base + at : base + at + part.shape[1]] = part.astype(ref.dtype)


def spread_kernel(cols, offsets_ref, bias_ref):
    bias_ref[...] = jnp.zeros_like(bias_ref)
    for head in range(bias_ref.shape[0]):
        for gap in range(2 * HALO + 1):
            line = offsets_ref[head, gap : gap + 1]
            lines = jnp.broadcast_to(line, (cols, line.shape[1]))
            first = line.shape[1] - cols + 1
            block = pltpu.roll(lines, first, 1, stride=1, stride_axis=0)[:, :cols]
            for row in range(bias_ref.shape[1] // cols):
                at = (row + gap) * cols
                bias_ref[head, row * cols : (row + 1) * cols, at : at + cols] = block


def attend_kernel(heads, scale, edge, qkv_ref, bias_ref, allow_ref, o_ref, p_ref):
    half = o_ref.shape[-1]
    cells = o_ref.shape[1]

    allowed = allow_ref[0] > 0.5
    queries = qkv_ref[0, edge : edge + cells, :half]
    key = qkv_ref[0, :, half : 2 * half]
    value = qkv_ref[0, :, 2 * half :]
    tiles = {}
    for head in range(heads):
        span = window(head, half // heads, half)
        start, stop = span[2:]
        query = queries[:, start:stop] * lane_mask(*span, bf16)
        scores = dot(query, key[:, start:stop], NT) * scale + bias_ref[head]
        scores = jnp.where(allowed, scores, masked_score)
        expo = jnp.exp(scores - jnp.max(scores, -1, keepdims=True))
        prob = (expo / jnp.sum(expo, -1, keepdims=True)).astype(bf16)
        p_ref[0, head] = prob
        out = dot(prob, value[:, start:stop]) * lane_mask(*span, f32)
        add_tiles(tiles, out, start, stop)
    store_tiles(o_ref, tiles)


def attend_back_kernel(heads, scale, edge, cols, qkv_ref, p_ref, do_ref, d_ref, g_ref, sum_ref):
    cells, half = do_ref.shape[1:]
    rows = cells // cols
    middle = slice(edge, edge + cells)
    step = pl.program_id(0)

    @pl.when(step == 0)
    def _():
        sum_ref[...] = jnp.zeros_like(sum_ref)

    queries = qkv_ref[0, middle, :half]
    key = qkv_ref[0, :, half : 2 * half]
    value = qkv_ref[0, :, 2 * half :]
    dq_tiles, dk_tiles, dv_tiles = {}, {}, {}
    for head in range(heads):
        span = window(head, half // heads, half)
        start, stop = span[2:]
        mask = lane_mask(*span, bf16)
        query = queries[:, start:stop] * mask
        grad_out = do_ref[0, :, start:stop] * mask
        prob = p_ref[0, head]
        full = prob.astype(f32)
        weighted = full * dot(grad_out, value[:, start:stop], NT)
        grad_score = (weighted - full * jnp.sum(weighted, -1, keepdims=True)).astype(bf16)
        sum_ref[head] += grad_score.astype(f32)
        dq = dot(grad_score, key[:, start:stop]) * lane_mask(*span, f32)
        add_tiles(dq_tiles, dq, start, stop)
        add_tiles(dk_tiles, dot(grad_score, query, TN), start, stop)
        add_tiles(dv_tiles, dot(prob, grad_out, TN), start, stop)
    d_ref[0, :edge, :half] = jnp.zeros((edge, half), bf16)
    d_ref[0, edge + cells :, :half] = jnp.zeros((edge, half), bf16)
    store_tiles(d_ref, dq_tiles, scale, middle)
    store_tiles(d_ref, dk_tiles, scale, base=half)
    store_tiles(d_ref, dv_tiles, base=2 * half)

    @pl.when(step == pl.num_programs(0) - 1)
    def _():
        ids = [lax.broadcasted_iota(jnp.int32, (cols, cols), axis) for axis in range(2)]
        turn = jnp.where(ids[0] + ids[1] == cols - 1, 1.0, 0.0)
        for head in range(heads):
            total = sum_ref[head, :cols]
            for row in range(1, rows):
                part = sum_ref[head, row * cols : (row + 1) * cols]
                total += pltpu.roll(part, part.shape[1] - row * cols, 1)
            total = jnp.dot(turn, total, precision=lax.Precision.HIGHEST)
            for gap in range(2 * HALO + 1):
                block = total[:, gap * cols : (gap + 1) * cols]
                block = jnp.concatenate([block, jnp.zeros((cols, LANES - cols), f32)], 1)
                block = pltpu.roll(block, 0, 1, stride=1, stride_axis=0)
                g_ref[head, gap : gap + 1] = jnp.sum(block, 0, keepdims=True)


def per_image(*dims):
    return pl.BlockSpec((1,) + dims, lambda i: (i,) + (0,) * len(dims))


def whole(*dims):
    return pl.BlockSpec(dims, lambda i: (0,) * len(dims))


def spread(offsets, cells, keys, cols):
    block = pl.BlockSpec(memory_space=pltpu.VMEM)
    return pl.pallas_call(
        functools.partial(spread_kernel, cols),
        in_specs=[block],
        out_specs=block,
        out_shape=jax.ShapeDtypeStruct((offsets.shape[0], cells, keys), f32),
        name="spread",
    )(offsets)


def attend(qkv, bias, allowed, scale):
    images, keys, width = qkv.shape
    heads, cells, _ = bias.shape
    half = width // 3
    return pl.pallas_call(
        functools.partial(attend_kernel, heads, scale, (keys - cells) // 2),
        grid=(images,),
        in_specs=[per_image(keys, width), whole(heads, cells, keys), per_image(cells, keys)],
        out_specs=[per_image(cells, half), per_image(heads, cells, keys)],
        out_shape=[
            jax.ShapeDtypeStruct((images, cells, half), bf16),
            jax.ShapeDtypeStruct((images, heads, cells, keys), bf16),
        ],
        compiler_params=pltpu.CompilerParams(vmem_limit_bytes=32 << 20),
        cost_estimate=pl.CostEstimate(flops=1, bytes_accessed=1, transcendentals=0),
        name="attend",
    )(qkv, bias, allowed)


def attend_back(qkv, prob, grad_out, scale, cols):
    images, keys, width = qkv.shape
    heads = prob.shape[1]
    cells, half = grad_out.shape[1:]
    return pl.pallas_call(
        functools.partial(attend_back_kernel, heads, scale, (keys - cells) // 2, cols),
        grid=(images,),
        in_specs=[per_image(keys, width), per_image(heads, cells, keys), per_image(cells, half)],
        out_specs=[per_image(keys, width), whole(heads, 2 * HALO + 1, LANES)],
        out_shape=[
            jax.ShapeDtypeStruct((images, keys, width), bf16),
            jax.ShapeDtypeStruct((heads, 2 * HALO + 1, LANES), f32),
        ],
        scratch_shapes=[pltpu.VMEM((heads, cells, keys), f32)],
        compiler_params=pltpu.CompilerParams(vmem_limit_bytes=32 << 20),
        cost_estimate=pl.CostEstimate(flops=1, bytes_accessed=1, transcendentals=0),
        name="attend_back",
    )(qkv, prob, grad_out)


def on_blocks(kernel, spot, values, shapes, name):
    block = pl.BlockSpec(memory_space=pltpu.VMEM)
    return pl.pallas_call(
        kernel,
        in_specs=[pl.BlockSpec(memory_space=pltpu.SMEM)] + [block] * len(values),
        out_specs=[block] * len(shapes),
        out_shape=[jax.ShapeDtypeStruct(shape, kind) for shape, kind in shapes],
        compiler_params=pltpu.CompilerParams(vmem_limit_bytes=32 << 20),
        name=name,
    )(spot, *values)


def for_each(value, count, body):
    for at in range(count):
        pl.when(value == at)(functools.partial(body, at))


def source_row(spot, group, size, by_core):
    side = jnp.bitwise_xor(spot[1], group >> 1)
    core = jnp.bitwise_xor(spot[2], group & 1) if by_core else group & 1
    return pl.multiple_of((side * 2 + core) * size, 16)


def split_core_kernel(spot, w_ref, keep_ref, send_ref):
    half = keep_ref.shape[1]

    def body(core):
        keep_ref[...] = w_ref[:, core * half : (core + 1) * half]
        send_ref[...] = w_ref[:, (1 - core) * half : (2 - core) * half]

    for_each(spot[2], 2, body)


def split_side_kernel(spot, own_ref, got_ref, fc2_ref, keep1_ref, keep2_ref, send_ref):
    rows, wide = own_ref.shape
    part = wide // 2

    def body(side):
        for at, ref in enumerate((own_ref, got_ref)):
            lanes = slice(at * part, (at + 1) * part)
            keep1_ref[:, lanes] = ref[:, side * part : (side + 1) * part]
            send_ref[:, lanes] = ref[:, (1 - side) * part : (2 - side) * part]
        for at in range(2):
            first = (side * 2 + at) * rows
            other = ((1 - side) * 2 + at) * rows
            keep2_ref[:, at * part : (at + 1) * part] = fc2_ref[first : first + rows]
            send_ref[:, wide + at * part : wide + (at + 1) * part] = fc2_ref[other : other + rows]

    for_each(spot[1], 2, body)


def fill_lanes(ref, first):
    if first < ref.shape[-1]:
        ref[:, first:] = jnp.zeros((ref.shape[0], ref.shape[-1] - first), ref.dtype)


def join_side_kernel(spot, out_ref, far_ref, keep1_ref, keep2_ref, got_ref, one_ref, two_ref):
    part = 2 * out_ref.shape[1]
    wide = keep1_ref.shape[1]
    one_ref[:, : part // 2] = out_ref[...]
    one_ref[:, part // 2 : part] = far_ref[...]
    one_ref[:, part : part + wide] = keep1_ref[...]
    one_ref[:, part + wide : part + 2 * wide] = got_ref[:, :wide]
    fill_lanes(one_ref, part + 2 * wide)
    two_ref[:, :wide] = keep2_ref[...]
    two_ref[:, wide:] = got_ref[:, wide:]


def unpack_kernel(by_core, lead, sides, spot, pieces, *outs):
    rows = pieces.shape[1] // sides
    part = outs[-1].shape[1] // 4
    for block in range(4):
        lanes = slice(block * part, (block + 1) * part)
        for at in range(lead):
            outs[0][at * rows : (at + 1) * rows, lanes] = pieces[
                block, :, at * part : (at + 1) * part
            ]
        for side in range(sides):
            base = jnp.bitwise_xor(spot[3], side) * 4 * rows if sides > 1 else 0
            for group in range(4):
                first = (group + lead) * part
                row = base + source_row(spot, group, rows, by_core)
                outs[-1][pl.ds(pl.multiple_of(row, 16), rows), lanes] = pieces[
                    block, side * rows : (side + 1) * rows, first : first + part
                ]


def pack_kernel(by_core, spot, grad_ref, got_ref, out):
    rows = out.shape[1]
    part = grad_ref.shape[1] // 4
    base = spot[3] * got_ref.shape[0]
    for block in range(4):
        lanes = slice(block * part, (block + 1) * part)
        for group in range(4):
            row = source_row(spot, group, rows, by_core)
            own = grad_ref[pl.ds(pl.multiple_of(base + row, 16), rows), lanes]
            total = own.astype(f32) + got_ref[pl.ds(row, rows), lanes].astype(f32)
            out[block, :, group * part : (group + 1) * part] = total.astype(out.dtype)


def pack_sides_kernel(spot, grad_ref, out):
    rows = out.shape[1] // 2
    part = grad_ref.shape[1] // 4
    for block in range(4):
        lanes = slice(block * part, (block + 1) * part)
        for side in range(2):
            base = jnp.bitwise_xor(spot[3], side) * 4 * rows
            for group in range(4):
                row = pl.multiple_of(base + source_row(spot, group, rows, False), 16)
                out[block, side * rows : (side + 1) * rows, group * part : (group + 1) * part] = (
                    grad_ref[pl.ds(row, rows), lanes]
                )


def split_sums_kernel(spot, one, two, keep1_ref, keep2_ref, send_ref):
    wide = keep1_ref.shape[1]
    keep1_ref[...] = one[:, :wide]
    keep2_ref[...] = two[:, :wide]
    send_ref[:, :wide] = one[:, wide:]
    send_ref[:, wide:] = two[:, wide:]


def turn_core_kernel(spot, keep1_ref, got_ref, send_ref):
    part = send_ref.shape[1] // 2
    send_ref[:, :part] = keep1_ref[:, part:]
    send_ref[:, part:] = got_ref[:, part : 2 * part]


def finish_kernel(spot, keep1_ref, keep2_ref, side_ref, core_ref, fc1_ref, fc2_ref):
    rows, part = fc1_ref.shape[0], fc2_ref.shape[1]

    def body(place):
        core, side = place // 2, place % 2
        parts = {
            (core, side): keep1_ref[:, :part],
            (core, 1 - side): side_ref[:, :part],
            (1 - core, side): core_ref[:, :part],
            (1 - core, 1 - side): core_ref[:, part:],
        }
        for (c, x), value in parts.items():
            fc1_ref[:, (2 * c + x) * part : (2 * c + x + 1) * part] = value.astype(f32)
        for at in range(2):
            lanes = slice(at * part, (at + 1) * part)
            first, other = (side * 2 + at) * rows, ((1 - side) * 2 + at) * rows
            fc2_ref[first : first + rows] = keep2_ref[:, lanes].astype(f32)
            fc2_ref[other : other + rows] = side_ref[:, (2 + at) * part : (3 + at) * part].astype(f32)

    for_each(spot[2] * 2 + spot[1], 4, body)


def qkv_blocks(tile, rows, count):
    for block in range(4):
        for at in range(count):
            for core in range(2):
                yield (
                    block,
                    core,
                    slice((2 * at + core) * rows, (2 * at + core + 1) * rows),
                    slice((block * count + at) * rows, (block * count + at + 1) * rows),
                )


def unpack_qkv_kernel(spot, *refs):
    pieces, kept = refs[:4], refs[4:]
    rows, wide = pieces[0].shape

    def body(place):
        tile, mine = place // 2, place % 2
        for block, core, there, here in qkv_blocks(tile, rows, wide // (2 * rows)):
            kept[core != mine][:, here] = pieces[(tile - block) % 4][:, there]

    for_each(spot[0] * 2 + spot[2], 8, body)


def pack_qkv_kernel(spot, own_ref, got_ref, last_ref, *outs):
    rows, wide = outs[0].shape
    part = last_ref.shape[1] // 4
    wide = wide - part

    def body(place):
        tile, mine = place // 2, place % 2
        for block, core, there, here in qkv_blocks(tile, rows, wide // (2 * rows)):
            source = own_ref if core == mine else got_ref
            outs[(block - tile) % 4][:, there] = source[:, here]
        for block in range(4):
            lanes = slice(block * part, (block + 1) * part)
            outs[(block - tile) % 4][:, wide:] = last_ref[:, lanes]

    for_each(spot[0] * 2 + spot[2], 8, body)


def place_kernel(count, rows_ref, *refs):
    ins, out = refs[:count], refs[count]
    for at, ref in enumerate(ins):
        out[pl.ds(pl.multiple_of(rows_ref[at], 16), ref.shape[0])] = ref[...]


def place_rows(pieces, rows, name):
    height = sum(piece.shape[0] for piece in pieces)
    shape = (height, pieces[0].shape[1]), pieces[0].dtype
    kernel = functools.partial(place_kernel, len(pieces))
    return on_blocks(kernel, jnp.stack(rows).astype(jnp.int32), pieces, [shape], name)[0]


def shards(
    tokens,
    cotangent,
    heights,
    widths,
    timesteps,
    rel_index,
    ln1_gain,
    ln1_bias,
    w_qkv,
    w_time,
    rel_table,
    w_out,
    out_bias,
    ln2_gain,
    ln2_bias,
    w_fc1,
    fc1_bias,
    w_fc2,
    fc2_bias,
):
    here, rows_here, cols, width = tokens.shape
    cells = rows_here * cols
    slots = here * cells
    key_rows = rows_here + 2 * HALO
    keys = key_rows * cols
    head_count = rel_table.shape[1]
    head_dim = width // head_count
    scale = head_dim ** (-0.5)
    image_devices = lax.axis_size("images")
    tiles = lax.axis_size("rows")
    low = image_devices // 8
    chunk = width // 8
    quarter = width // 4
    ff_part = fc1_bias.shape[0] // 16
    place = lax.axis_index("images")
    tile = lax.axis_index("rows")
    bits = {"c": low, "x": 2 * low, "y": 4 * low}
    at_c, at_x, at_y = (place // bits[name] % 2 for name in "cxy")


    def partner(value, bit):
        route = [(d, d ^ bit) for d in range(image_devices)]
        return lax.ppermute(value, "images", route)

    def swap(value, name):
        return partner(value, bits[name])

    def pick(at, pair):
        return jnp.where(at == 0, pair[0], pair[1]), jnp.where(at == 0, pair[1], pair[0])

    def after(value, *others):
        return lax.optimization_barrier((value,) + others)[0]

    def all_after(values, *others):
        return list(lax.optimization_barrier(tuple(values) + others))[: len(values)]

    def with_partner(value, name):
        return jnp.concatenate([value, swap(value, name)], 0)

    def shift(value, step):
        return lax.ppermute(value, "rows", [(d, (d + step) % tiles) for d in range(tiles)])

    def tiles_all(value):
        return lax.all_gather(value, "rows", axis=0)

    def tiles_sum(value):
        return lax.psum_scatter(value, "rows", scatter_dimension=0)

    def shifts(value):
        return [shift(value, step) for step in range(1, tiles)]

    def tile_gather(value):
        for bit in (1, 2):
            other = lax.ppermute(value, "rows", [(d, d ^ bit) for d in range(tiles)])
            value = jnp.concatenate(pick(tile // bit % 2, (value, other)), 1)
        return value

    def tile_scatter(value):
        for bit in (2, 1):
            size = value.shape[1] // 2
            kept, sent = pick(tile // bit % 2, (value[:, :size], value[:, size:]))
            value = kept + lax.ppermute(sent, "rows", [(d, d ^ bit) for d in range(tiles)])
        return value

    low_groups = [[g * low + d for d in range(low)] for g in range(8)]
    def low_gather(value):
        if low == 1:
            return value
        return lax.all_gather(value, "images", axis=0, tiled=True, axis_index_groups=low_groups)

    def low_scatter(value):
        if low == 1:
            return value
        return lax.psum_scatter(
            value, "images", scatter_dimension=0, tiled=True, axis_index_groups=low_groups
        )

    def sides_of(value):
        half = value.shape[0] // 2
        return value[:half], value[half:]

    def part_of(value, at):
        return lax.dynamic_index_in_dim(value, at, 0, keepdims=False)


    slot_row = tile * rows_here + jnp.arange(cells) // cols
    slot_col = jnp.arange(cells) % cols
    valid = (slot_row[None, :] < heights[:, None]) & (slot_col[None, :] < widths[:, None])
    valid_mask = valid.reshape(slots, 1).astype(f32)
    grad_out = cotangent.astype(f32).reshape(slots, width) * valid_mask
    grad_mlp_own = grad_out.astype(bf16)


    spot = jnp.stack([tile, at_x, at_c, at_y]).astype(jnp.int32)
    w_qkv, w_out, w_fc1, w_fc2 = (low_gather(w) for w in (w_qkv, w_out, w_fc1, w_fc2))
    wide = 2 * ff_part
    images = 2 * here
    padded = -(-(2 * quarter + 2 * wide) // LANES) * LANES

    def matrices(*dims):
        return [(dim, bf16) for dim in dims]

    qkv_parts = [w_qkv] + shifts(w_qkv)

    fc1_keep, fc1_send = on_blocks(
        split_core_kernel, spot, [w_fc1], matrices((chunk, wide), (chunk, wide)), "split_core"
    )
    fc1_got = swap(fc1_send, "c")
    keep1, keep2, send = on_blocks(
        split_side_kernel,
        spot,
        [fc1_keep, fc1_got, w_fc2],
        matrices((chunk, wide), (chunk, wide), (chunk, 2 * wide)),
        "split_side",
    )
    got = swap(send, "x")
    one, two = on_blocks(
        join_side_kernel,
        spot,
        [w_out, swap(w_out, "y"), keep1, keep2, got],
        matrices((chunk, padded), (chunk, 2 * wide)),
        "join_side",
    )
    two = with_partner(two, "y")


    orders = [bits["c"], bits["x"], bits["y"]]
    orders += [1 << b for b in range(low.bit_length() - 1)]
    facts = with_partner(jnp.stack([timesteps, heights, widths], 1), "c")
    heights_all, widths_all = facts[:, 1], facts[:, 2]
    steps_all = facts[:, 0]
    for bit in orders[1:]:
        steps_all = jnp.concatenate([steps_all, partner(steps_all, bit)], 0)
    time_rows = w_time.shape[0]
    half_width = width // 2
    feature = place * time_rows + jnp.arange(time_rows)
    exponent = (feature % half_width).astype(f32)
    frequency = jnp.exp(-math.log(10000.0) * exponent / half_width)
    phases = steps_all.astype(f32)[:, None] * frequency[None, :]
    timing = jnp.where(feature[None, :] < half_width, jnp.cos(phases), jnp.sin(phases)).astype(bf16)
    time_part = dot(timing, after(w_time, keep1, *qkv_parts[1:]))
    for bit in orders[:0:-1]:
        half = time_part.shape[0] // 2
        time_part = time_part[:half] + partner(time_part[half:], bit)
    turned = jnp.concatenate([time_part[here:], time_part[:here]], 0)
    time_part = time_part + swap(turned, "c")
    qkv_keep, qkv_send = on_blocks(
        unpack_qkv_kernel,
        spot,
        qkv_parts,
        matrices((chunk, 12 * chunk), (chunk, 12 * chunk)),
        "unpack_qkv",
    )

    gain_one, shift_one = ln1_gain.astype(f32), ln1_bias.astype(f32)
    gain_two, shift_two = ln2_gain.astype(f32), ln2_bias.astype(f32)
    flat_tokens = tokens.astype(f32).reshape(slots, width)
    normal_one, inverse_one = normalize(flat_tokens)
    normed = (normal_one * gain_one + shift_one).astype(bf16).reshape(tokens.shape)

    down = [(d, d + 1) for d in range(tiles - 1)]
    up = [(d + 1, d) for d in range(tiles - 1)]

    edges = [normed[:, rows_here - HALO :], normed[:, :HALO]]
    edges = all_after(edges, *qkv_parts[1:])
    above = lax.ppermute(edges[0], "rows", down)
    below = lax.ppermute(edges[1], "rows", up)

    qkv_pair = jnp.concatenate([qkv_keep, swap(qkv_send, "c")], 0)
    time_pairs = tile_gather(time_part)
    qkv_pair = after(qkv_pair, time_pairs, one, above, below)
    one_parts = tiles_all(after(one, qkv_pair))
    two_parts = tiles_all(two)

    qkv_x, qkv_y = swap(qkv_pair, "x"), swap(qkv_pair, "y")
    normed_ext = jnp.concatenate([after(above, qkv_pair), normed, below], 1)
    normed_all = with_partner(normed_ext, "c").reshape(images * keys, width)
    qkv_x, qkv_y = all_after([qkv_x, qkv_y], normed_all)
    qkv_far = [swap(qkv_x[:chunk], "y"), swap(qkv_y[chunk:], "x")]
    qkv_far = all_after(qkv_far, one_parts)
    spots = at_y * 4 + at_x * 2 + at_c
    qkv_full = place_rows(
        [qkv_pair[:chunk], qkv_pair[chunk:], qkv_x[:chunk], qkv_x[chunk:]]
        + [qkv_y[:chunk], qkv_y[chunk:]]
        + qkv_far,
        [jnp.bitwise_xor(spots, step) * chunk for step in range(8)],
        "place_qkv",
    )

    out_rows, fc1_rows = on_blocks(
        functools.partial(unpack_kernel, True, 2, 1),
        spot,
        [after(one_parts, qkv_full)],
        matrices((2 * chunk, width), (4 * chunk, 4 * ff_part)),
        "unpack_fc1",
    )
    out_got = swap(out_rows, "x")
    places = at_y * 2 + at_x
    out_full = place_rows(
        [out_rows[:chunk], out_rows[chunk:], out_got[:chunk], out_got[chunk:]],
        [jnp.bitwise_xor(places, step) * chunk for step in (0, 2, 1, 3)],
        "place_out",
    )
    fc1_first, fc1_second = sides_of(fc1_rows)
    fc1_first, fc1_second = swap(fc1_first, "y"), swap(fc1_second, "y")
    size = fc1_rows.shape[0]
    fc1_full = place_rows(
        [fc1_rows, fc1_first, fc1_second],
        [at_y * size, (1 - at_y) * size, (1 - at_y) * size + size // 2],
        "place_fc1",
    )
    grad_mlp_x = with_partner(after(grad_mlp_own, qkv_full), "x")
    grad_mlp = with_partner(grad_mlp_x, "c")

    time_pairs = time_pairs.reshape(images, -1, 2, chunk)
    time_mine = pick(at_c, (time_pairs[:, :, 0], time_pairs[:, :, 1]))[0].reshape(images, width)
    half = width // 2
    time_all = jnp.concatenate(
        [time_mine[:, :half], jnp.zeros((images, half), f32), time_mine[:, half:]], 1
    )


    query_row = jnp.arange(cells) // cols
    query_col = jnp.arange(cells) % cols
    key_row = jnp.arange(keys) // cols - HALO
    key_col = jnp.arange(keys) % cols
    near = jnp.abs(key_row[None, :] - query_row[:, None]) <= HALO
    itself = jnp.arange(keys)[None, :] == jnp.arange(cells)[:, None] + HALO * cols
    global_key = tile * rows_here + key_row
    key_ok = (
        (global_key[None, :] >= 0)
        & (global_key[None, :] < heights_all[:, None])
        & (key_col[None, :] < widths_all[:, None])
    )
    allowed = (key_ok[:, None, :] & near[None] | itself[None]).astype(f32)
    heads = head_count // 2
    gaps = 2 * HALO + 1
    spans = 2 * cols - 1
    exact = lax.Precision.HIGHEST
    bucket_hits = (
        rel_index.reshape(-1)[:, None] == jnp.arange(rel_table.shape[0])[None, :]
    ).astype(f32)
    head_ids = jnp.arange(heads)
    head_hits = (
        jnp.arange(head_count)[:, None] == (head_ids // 2 * 4 + at_c * 2 + head_ids % 2)[None, :]
    ).astype(f32)
    table_mine = jnp.dot(after(rel_table, qkv_pair).astype(f32), head_hits, precision=exact)
    offset_values = lax.dot_general(
        table_mine, bucket_hits, (((0,), (1,)), ((), ())), precision=exact
    ).reshape(heads, gaps, spans)
    offset_values = jnp.pad(offset_values, ((0, 0), (0, 0), (0, LANES - spans)))
    bias = spread(offset_values, cells, keys, cols)


    normed_here = after(normed_all, out_rows)
    qkv = (
        dot(normed_here, qkv_full).reshape(images, keys, 3 * half) + time_all[:, None]
    ).astype(bf16)
    attended, prob = attend(qkv, bias, allowed, scale)
    attended = after(attended.reshape(images * cells, half), grad_mlp_x, fc1_first)

    def core_sum(left, right, dims=NN):
        size = left.shape[0] // 2
        sent = swap(dot(left[size:], right, dims).astype(bf16), "c")
        return dot(left[:size], right, dims) + sent.astype(f32)

    middle = flat_tokens + core_sum(attended, out_full) + out_bias.astype(f32)
    normal_two, inverse_two = normalize(middle)
    second = with_partner((normal_two * gain_two + shift_two).astype(bf16), "x")
    second = with_partner(after(second, fc1_full), "c")


    member = at_c * 2 + at_x
    bias_parts = fc1_bias.astype(f32).reshape(tiles, 4, ff_part)
    bias_mine = lax.dynamic_index_in_dim(bias_parts, member, 1, keepdims=False).reshape(-1)
    hidden_pre = dot(second, fc1_full) + bias_mine
    hidden_act, hidden_slope = gelu_and_slope(hidden_pre)
    hidden = hidden_act.astype(bf16)
    hidden_slope = hidden_slope.astype(bf16)
    (fc2_full,) = on_blocks(
        functools.partial(unpack_kernel, False, 0, 2),
        spot,
        [after(two_parts, middle)],
        matrices((8 * chunk, width)),
        "unpack_fc2",
    )
    grad_pre = (dot(grad_mlp, fc2_full, NT) * hidden_slope.astype(f32)).astype(bf16)
    grad_second = core_sum(grad_pre, fc1_full, NT)
    grad_second_sent = grad_second[slots:].astype(bf16)
    grad_second_got = swap(grad_second_sent, "x")
    grad_fc2 = dot(after(hidden, grad_second_sent), grad_mlp, TN).astype(bf16)
    (two_packed,) = on_blocks(
        pack_sides_kernel, spot, [grad_fc2], matrices((tiles, 2 * chunk, 2 * wide)), "pack_fc2"
    )
    two_sum = tiles_sum(two_packed)
    grad_second_got = after(grad_second_got, two_packed)
    grad_second = grad_second[:slots] + grad_second_got.astype(f32)
    grad_fc1 = dot(second, grad_pre, TN).astype(bf16)
    grad_fc2_bias = jnp.sum(grad_mlp_own, 0, dtype=f32)
    grad_fc1_bias = jnp.sum(grad_pre, 0, dtype=f32)

    grad_gain_two = jnp.sum(grad_second * normal_two, 0)
    grad_shift_two = jnp.sum(grad_second, 0)
    grad_middle = grad_out + norm_back(grad_second * gain_two, normal_two, inverse_two)
    grad_branch_own = grad_middle.astype(bf16)
    grad_out_bias = jnp.sum(grad_branch_own, 0, dtype=f32)
    grad_branch = with_partner(grad_branch_own, "c")


    def add_bf16(one, two):
        return (one.astype(f32) + two.astype(f32)).astype(bf16)

    def sides(grad):
        return grad.reshape((2, -1) + grad.shape[1:])

    fc1_got = swap(part_of(sides(grad_fc1), 1 - at_y), "y")
    grad_att = dot(grad_branch, out_full, NT).astype(bf16)
    grad_out_weight = dot(attended, grad_branch, TN).astype(bf16)
    out_sides = grad_out_weight.reshape(2, 2, chunk, width)
    out_sent = out_sides[:, 0], out_sides[:, 1]
    out_kept, out_sent = pick(at_x, out_sent)
    grad_att = after(grad_att, out_sent).reshape(images, cells, half)
    out_got = swap(out_sent, "x")

    grad_proj, grad_strip = attend_back(qkv, prob, grad_att, scale, cols)
    flat_proj = grad_proj.reshape(images * keys, 3 * half)
    grad_qkv = row_major(dot(normed_all, flat_proj, TN).astype(bf16))
    blocks = grad_qkv.reshape(2, 2, 2, chunk, 12 * chunk)

    def blocks_at(y, x, core):
        first = [0 if at is None else at for at in (y, x, core)] + [0, 0]
        size = [2 if at is None else 1 for at in (y, x, core)] + list(blocks.shape[3:])
        return lax.dynamic_slice(blocks, first, size).reshape(-1, chunk, 12 * chunk)

    own_sent = blocks_at(1 - at_y, None, at_c)
    other_sent = blocks_at(None, 1 - at_x, 1 - at_c)
    own_got, other_got = swap(own_sent, "y"), swap(other_sent, "x")
    out_mine = add_bf16(out_kept, after(out_got, grad_qkv))
    out_got = swap(part_of(out_mine, 1 - at_y), "y")
    out_mine = add_bf16(part_of(out_mine, at_y), out_got)

    (one_packed,) = on_blocks(
        functools.partial(pack_kernel, True),
        spot,
        [grad_fc1, after(fc1_got, own_sent, other_sent)],
        matrices((tiles, chunk, 2 * wide)),
        "pack_fc1",
    )
    one_sum = tiles_sum(one_packed)
    flat_proj = after(flat_proj, own_sent, other_sent, one_packed)
    grad_ext = core_sum(flat_proj, qkv_full, NT).reshape(here, key_rows, cols, width)
    mlp_out = core_sum(after(hidden, grad_ext), fc2_full)

    from_below = lax.ppermute(grad_ext[:, :HALO].astype(bf16), "rows", up).astype(f32)
    from_above = lax.ppermute(grad_ext[:, HALO + rows_here :].astype(bf16), "rows", down)
    from_above = from_above.astype(f32)
    rest = ((0, 0), (rows_here - HALO, 0), (0, 0), (0, 0))
    grad_normed = (
        grad_ext[:, HALO : HALO + rows_here]
        + jnp.pad(from_below, rest)
        + jnp.pad(from_above, (rest[0], rest[1][::-1], rest[2], rest[3]))
    ).reshape(slots, width)
    grad_gain_one = jnp.sum(grad_normed * normal_one, 0)
    grad_shift_one = jnp.sum(grad_normed, 0)
    grad_input = grad_middle + norm_back(grad_normed * gain_one, normal_one, inverse_one)
    grad_tokens = grad_input.reshape(tokens.shape).astype(bf16)


    grad_offsets = grad_strip[:, :, :spans].reshape(heads, gaps * spans)
    grad_table = jnp.dot(grad_offsets, bucket_hits, precision=exact)
    grad_table = jnp.dot(head_hits, grad_table, precision=exact)


    own_got, other_got = all_after([own_got, other_got], grad_ext)
    own_two = add_bf16(blocks_at(at_y, None, at_c), own_got)
    other_two = add_bf16(blocks_at(None, at_x, 1 - at_c), other_got)
    far_sent = part_of(own_two, 1 - at_x)
    own_got = swap(far_sent, "x")
    mlp_sent = after(mlp_out[slots:].astype(bf16), far_sent)
    mlp_out = mlp_out[:slots] + swap(mlp_sent, "x").astype(f32) + fc2_bias.astype(f32)
    mixed = (valid_mask * (middle + mlp_out)).reshape(tokens.shape).astype(bf16)
    other_got = swap(part_of(other_two, 1 - at_y), "y")
    own_rows_got, other_rows_got = own_got, other_got


    def row(value):
        return value.reshape(-1, width)

    mine = (jnp.arange(4) == member).astype(f32)
    fc1_bias_all = grad_fc1_bias.reshape(tiles, 1, ff_part) * mine[None, :, None]
    buckets = rel_table.shape[0]
    table_rows = grad_table.reshape(4, -1, buckets)
    table_rows = jnp.concatenate([table_rows[:, at] for at in range(table_rows.shape[1])], 1)
    table_rows = jnp.pad(table_rows, ((0, 0), (0, width - table_rows.shape[1])))
    small = [
        row(grad_gain_one),
        row(grad_shift_one),
        row(grad_out_bias),
        row(grad_gain_two),
        row(grad_shift_two),
        row(grad_fc2_bias),
        row(fc1_bias_all),
        table_rows,
    ]
    count = 6 + 4 * ff_part * tiles // width + 4
    sums = jnp.sum(grad_proj, 1, dtype=f32)
    sums = jnp.concatenate([sums[:, :half], sums[:, 2 * half :]], 1)
    total = jnp.concatenate(small + [sums], 0)
    for step in range(tiles.bit_length() - 1):
        route = [(d, d ^ (1 << step)) for d in range(tiles)]
        total = total + lax.ppermute(total, "rows", route)
    own_rows_got, other_rows_got = all_after([own_rows_got, other_rows_got], total)

    own_rows = add_bf16(part_of(own_two, at_x), own_rows_got)
    other_rows = add_bf16(part_of(other_two, at_y), other_rows_got)
    other_rows = swap(other_rows, "c")
    last_parts = on_blocks(
        pack_qkv_kernel,
        spot,
        [own_rows, other_rows, out_mine],
        matrices(*[(chunk, 6 * chunk + quarter)] * 4),
        "pack_qkv",
    )
    last = last_parts[0].astype(f32)
    for step in range(1, tiles):
        last = last + shift(last_parts[step], step).astype(f32)
    qkv_own, out_own = last[:, : 6 * chunk], last[:, 6 * chunk :]

    two_sum = after(two_sum, far_sent)
    two_sum = add_bf16(two_sum[:chunk], swap(two_sum[chunk:], "y"))
    keep1, keep2, send = on_blocks(
        split_sums_kernel,
        spot,
        [one_sum, two_sum],
        matrices((chunk, wide), (chunk, wide), (chunk, 2 * wide)),
        "split_sums",
    )
    side_got = swap(send, "x")
    (send,) = on_blocks(
        turn_core_kernel, spot, [keep1, side_got], matrices((chunk, wide)), "turn_core"
    )
    fc1_own, fc2_own = on_blocks(
        finish_kernel,
        spot,
        [keep1, keep2, side_got, swap(send, "c")],
        [((chunk, 2 * wide), f32), ((4 * chunk, ff_part), f32)],
        "finish",
    )


    total = after(total, *last_parts)
    total, sums = total[:count], total[count:]
    size = width // tiles
    sums = lax.select_n(tile, *[sums[:, at * size : (at + 1) * size] for at in range(tiles)])
    turned = jnp.concatenate([sums[here:], sums[:here]], 0)

    def both(total, sums, bit):
        room = ((0, 0), (0, width - sums.shape[1]))
        got = partner(jnp.concatenate([total, jnp.pad(sums, room)], 0), bit)
        return total + got[:count], got[count:, : sums.shape[1]]

    total, other = both(total, turned, orders[0])
    pair = pick(at_c, (sums.reshape(images, -1, 1, chunk), other.reshape(images, -1, 1, chunk)))
    sums = jnp.concatenate(pair, 2).reshape(images, -1)
    for bit in orders[1:]:
        total, other = both(total, sums, bit)
        sums = jnp.concatenate([sums, other], 0)
    grad_time = lax.dot_general(timing.astype(f32), sums, TN, precision=exact)
    table = total[count - 4 :, : head_count // 4 * buckets].reshape(head_count, buckets).T
    return (
        mixed,
        grad_tokens,
        total[0],
        total[1],
        low_scatter(qkv_own),
        grad_time,
        table,
        low_scatter(out_own),
        total[2],
        total[3],
        total[4],
        low_scatter(fc1_own),
        total[6 : count - 4].reshape(-1),
        low_scatter(fc2_own),
        total[5],
    )


def solution(mesh):
    tokens, image, weight = P("images", "rows", None, None), P("images"), P("images", "rows")
    return jax.shard_map(
        shards,
        mesh=mesh,
        in_specs=(
            tokens, tokens, image, image, image, P(), P(), P(), weight, weight,
            P(), weight, P(), P(), P(), weight, P(), weight, P(),
        ),
        out_specs=(
            tokens, tokens, P(), P(), weight, weight, P(), weight, P(), P(),
            P(), weight, P(), weight, P(),
        ),
        check_vma=False,
    )
```

```python
import functools
import math

import jax
import jax.numpy as jnp
from jax import lax
from jax.experimental import pallas as pl
from jax.experimental.layout import Layout, with_layout_constraint
from jax.experimental.pallas import tpu as pltpu
from jax.sharding import PartitionSpec as P

HALO = 2
LANES = 128

norm_eps = 1e-06
masked_score = -1000000000.0

f32 = jnp.float32
bf16 = jnp.bfloat16

NN = (((1,), (0,)), ((), ()))
NT = (((1,), (1,)), ((), ()))
TN = (((0,), (0,)), ((), ()))


def dot(left, right, dims=NN):
    return lax.dot_general(left, right, dims, preferred_element_type=f32)


def row_major(value):
    return with_layout_constraint(value, Layout(major_to_minor=tuple(range(value.ndim))))


def normalize(values):
    centre = values - jnp.mean(values, -1, keepdims=True)
    spread = jnp.mean(centre * centre, -1, keepdims=True)
    inverse = lax.rsqrt(spread + norm_eps)
    return (centre * inverse, inverse)


def norm_back(grad_hat, normal_part, inverse):
    first_mean = jnp.mean(grad_hat, -1, keepdims=True)
    second_mean = jnp.mean(grad_hat * normal_part, -1, keepdims=True)
    return inverse * (grad_hat - first_mean - normal_part * second_mean)


def gelu_and_slope(values):
    slant = math.sqrt(2.0 / math.pi)
    square = values * values
    curve = jnp.tanh(slant * values * (1.0 + 0.044715 * square))
    lift = 0.5 * (1.0 + curve)
    bend = 0.5 * values * (1.0 - curve * curve) * slant * (1.0 + 3.0 * 0.044715 * square)
    return values * lift, lift + bend


def window(head, head_dim, width):
    first, last = head * head_dim, (head + 1) * head_dim
    start = first // LANES * LANES
    stop = min(-(-last // LANES) * LANES, width)
    return first, last, start, stop


def lane_mask(first, last, start, stop, kind):
    lane = lax.broadcasted_iota(jnp.int32, (1, stop - start), 1) + start
    return jnp.where((lane >= first) & (lane < last), 1.0, 0.0).astype(kind)


def add_tiles(tiles, values, start, stop):
    for at in range(start, stop, LANES):
        part = values[:, at - start : min(at + LANES, stop) - start]
        tiles[at] = part if at not in tiles else tiles[at] + part


def store_tiles(ref, tiles, scale=None, rows=slice(None), base=0):
    for at, part in tiles.items():
        if scale is not None:
            part = part * scale
        ref[0, rows, base + at : base + at + part.shape[1]] = part.astype(ref.dtype)


def spread_kernel(cols, offsets_ref, bias_ref):
    bias_ref[...] = jnp.zeros_like(bias_ref)
    for head in range(bias_ref.shape[0]):
        for gap in range(2 * HALO + 1):
            line = offsets_ref[head, gap : gap + 1]
            lines = jnp.broadcast_to(line, (cols, line.shape[1]))
            first = line.shape[1] - cols + 1
            block = pltpu.roll(lines, first, 1, stride=1, stride_axis=0)[:, :cols]
            for row in range(bias_ref.shape[1] // cols):
                at = (row + gap) * cols
                bias_ref[head, row * cols : (row + 1) * cols, at : at + cols] = block


def attend_kernel(heads, scale, edge, qkv_ref, bias_ref, allow_ref, o_ref, p_ref):
    half = o_ref.shape[-1]
    cells = o_ref.shape[1]

    allowed = allow_ref[0] > 0.5
    queries = qkv_ref[0, edge : edge + cells, :half]
    key = qkv_ref[0, :, half : 2 * half]
    value = qkv_ref[0, :, 2 * half :]
    tiles = {}
    for head in range(heads):
        span = window(head, half // heads, half)
        start, stop = span[2:]
        query = queries[:, start:stop] * lane_mask(*span, bf16)
        scores = dot(query, key[:, start:stop], NT) * scale + bias_ref[head]
        scores = jnp.where(allowed, scores, masked_score)
        expo = jnp.exp(scores - jnp.max(scores, -1, keepdims=True))
        prob = (expo / jnp.sum(expo, -1, keepdims=True)).astype(bf16)
        p_ref[0, head] = prob
        out = dot(prob, value[:, start:stop]) * lane_mask(*span, f32)
        add_tiles(tiles, out, start, stop)
    store_tiles(o_ref, tiles)


def attend_back_kernel(heads, scale, edge, cols, qkv_ref, p_ref, do_ref, d_ref, g_ref, sum_ref):
    cells, half = do_ref.shape[1:]
    rows = cells // cols
    middle = slice(edge, edge + cells)
    step = pl.program_id(0)

    @pl.when(step == 0)
    def _():
        sum_ref[...] = jnp.zeros_like(sum_ref)

    queries = qkv_ref[0, middle, :half]
    key = qkv_ref[0, :, half : 2 * half]
    value = qkv_ref[0, :, 2 * half :]
    dq_tiles, dk_tiles, dv_tiles = {}, {}, {}
    for head in range(heads):
        span = window(head, half // heads, half)
        start, stop = span[2:]
        mask = lane_mask(*span, bf16)
        query = queries[:, start:stop] * mask
        grad_out = do_ref[0, :, start:stop] * mask
        prob = p_ref[0, head]
        full = prob.astype(f32)
        weighted = full * dot(grad_out, value[:, start:stop], NT)
        grad_score = (weighted - full * jnp.sum(weighted, -1, keepdims=True)).astype(bf16)
        sum_ref[head] += grad_score.astype(f32)
        dq = dot(grad_score, key[:, start:stop]) * lane_mask(*span, f32)
        add_tiles(dq_tiles, dq, start, stop)
        add_tiles(dk_tiles, dot(grad_score, query, TN), start, stop)
        add_tiles(dv_tiles, dot(prob, grad_out, TN), start, stop)
    d_ref[0, :edge, :half] = jnp.zeros((edge, half), bf16)
    d_ref[0, edge + cells :, :half] = jnp.zeros((edge, half), bf16)
    store_tiles(d_ref, dq_tiles, scale, middle)
    store_tiles(d_ref, dk_tiles, scale, base=half)
    store_tiles(d_ref, dv_tiles, base=2 * half)

    @pl.when(step == pl.num_programs(0) - 1)
    def _():
        ids = [lax.broadcasted_iota(jnp.int32, (cols, cols), axis) for axis in range(2)]
        turn = jnp.where(ids[0] + ids[1] == cols - 1, 1.0, 0.0)
        for head in range(heads):
            total = sum_ref[head, :cols]
            for row in range(1, rows):
                part = sum_ref[head, row * cols : (row + 1) * cols]
                total += pltpu.roll(part, part.shape[1] - row * cols, 1)
            total = jnp.dot(turn, total, precision=lax.Precision.HIGHEST)
            for gap in range(2 * HALO + 1):
                block = total[:, gap * cols : (gap + 1) * cols]
                block = jnp.concatenate([block, jnp.zeros((cols, LANES - cols), f32)], 1)
                block = pltpu.roll(block, 0, 1, stride=1, stride_axis=0)
                g_ref[head, gap : gap + 1] = jnp.sum(block, 0, keepdims=True)


def per_image(*dims):
    return pl.BlockSpec((1,) + dims, lambda i: (i,) + (0,) * len(dims))


def whole(*dims):
    return pl.BlockSpec(dims, lambda i: (0,) * len(dims))


def spread(offsets, cells, keys, cols):
    block = pl.BlockSpec(memory_space=pltpu.VMEM)
    return pl.pallas_call(
        functools.partial(spread_kernel, cols),
        in_specs=[block],
        out_specs=block,
        out_shape=jax.ShapeDtypeStruct((offsets.shape[0], cells, keys), f32),
        name="spread",
    )(offsets)


def attend(qkv, bias, allowed, scale):
    images, keys, width = qkv.shape
    heads, cells, _ = bias.shape
    half = width // 3
    return pl.pallas_call(
        functools.partial(attend_kernel, heads, scale, (keys - cells) // 2),
        grid=(images,),
        in_specs=[per_image(keys, width), whole(heads, cells, keys), per_image(cells, keys)],
        out_specs=[per_image(cells, half), per_image(heads, cells, keys)],
        out_shape=[
            jax.ShapeDtypeStruct((images, cells, half), bf16),
            jax.ShapeDtypeStruct((images, heads, cells, keys), bf16),
        ],
        compiler_params=pltpu.CompilerParams(vmem_limit_bytes=56 << 20),
        cost_estimate=pl.CostEstimate(flops=1, bytes_accessed=1, transcendentals=0),
        name="attend",
    )(qkv, bias, allowed)


def attend_back(qkv, prob, grad_out, scale, cols):
    images, keys, width = qkv.shape
    heads = prob.shape[1]
    cells, half = grad_out.shape[1:]
    return pl.pallas_call(
        functools.partial(attend_back_kernel, heads, scale, (keys - cells) // 2, cols),
        grid=(images,),
        in_specs=[per_image(keys, width), per_image(heads, cells, keys), per_image(cells, half)],
        out_specs=[per_image(keys, width), whole(heads, 2 * HALO + 1, LANES)],
        out_shape=[
            jax.ShapeDtypeStruct((images, keys, width), bf16),
            jax.ShapeDtypeStruct((heads, 2 * HALO + 1, LANES), f32),
        ],
        scratch_shapes=[pltpu.VMEM((heads, cells, keys), f32)],
        compiler_params=pltpu.CompilerParams(vmem_limit_bytes=56 << 20),
        cost_estimate=pl.CostEstimate(flops=1, bytes_accessed=1, transcendentals=0),
        name="attend_back",
    )(qkv, prob, grad_out)


def on_blocks(kernel, spot, values, shapes, name):
    block = pl.BlockSpec(memory_space=pltpu.VMEM)
    return pl.pallas_call(
        kernel,
        in_specs=[pl.BlockSpec(memory_space=pltpu.SMEM)] + [block] * len(values),
        out_specs=[block] * len(shapes),
        out_shape=[jax.ShapeDtypeStruct(shape, kind) for shape, kind in shapes],
        compiler_params=pltpu.CompilerParams(vmem_limit_bytes=32 << 20),
        name=name,
    )(spot, *values)


def for_each(value, count, body):
    for at in range(count):
        pl.when(value == at)(functools.partial(body, at))


def source_row(spot, group, size, by_core):
    side = jnp.bitwise_xor(spot[1], group >> 1)
    core = jnp.bitwise_xor(spot[2], group & 1) if by_core else group & 1
    return pl.multiple_of((side * 2 + core) * size, 16)


def split_core_kernel(spot, w_ref, keep_ref, send_ref):
    half = keep_ref.shape[1]

    def body(core):
        keep_ref[...] = w_ref[:, core * half : (core + 1) * half]
        send_ref[...] = w_ref[:, (1 - core) * half : (2 - core) * half]

    for_each(spot[2], 2, body)


def split_side_kernel(spot, own_ref, got_ref, fc2_ref, keep1_ref, keep2_ref, send_ref):
    rows, wide = own_ref.shape
    part = wide // 2

    def body(side):
        for at, ref in enumerate((own_ref, got_ref)):
            lanes = slice(at * part, (at + 1) * part)
            keep1_ref[:, lanes] = ref[:, side * part : (side + 1) * part]
            send_ref[:, lanes] = ref[:, (1 - side) * part : (2 - side) * part]
        for at in range(2):
            first = (side * 2 + at) * rows
            other = ((1 - side) * 2 + at) * rows
            keep2_ref[:, at * part : (at + 1) * part] = fc2_ref[first : first + rows]
            send_ref[:, wide + at * part : wide + (at + 1) * part] = fc2_ref[other : other + rows]

    for_each(spot[1], 2, body)


def fill_lanes(ref, first):
    if first < ref.shape[-1]:
        ref[:, first:] = jnp.zeros((ref.shape[0], ref.shape[-1] - first), ref.dtype)


def join_side_kernel(spot, out_ref, far_ref, keep1_ref, keep2_ref, got_ref, one_ref, two_ref):
    part = 2 * out_ref.shape[1]
    wide = keep1_ref.shape[1]
    one_ref[:, : part // 2] = out_ref[...]
    one_ref[:, part // 2 : part] = far_ref[...]
    one_ref[:, part : part + wide] = keep1_ref[...]
    one_ref[:, part + wide : part + 2 * wide] = got_ref[:, :wide]
    fill_lanes(one_ref, part + 2 * wide)
    two_ref[:, :wide] = keep2_ref[...]
    two_ref[:, wide:] = got_ref[:, wide:]


def unpack_kernel(by_core, lead, sides, spot, pieces, *outs):
    rows = pieces.shape[1] // sides
    part = outs[-1].shape[1] // 4
    for block in range(4):
        lanes = slice(block * part, (block + 1) * part)
        for at in range(lead):
            outs[0][at * rows : (at + 1) * rows, lanes] = pieces[
                block, :, at * part : (at + 1) * part
            ]
        for side in range(sides):
            base = jnp.bitwise_xor(spot[3], side) * 4 * rows if sides > 1 else 0
            for group in range(4):
                first = (group + lead) * part
                row = base + source_row(spot, group, rows, by_core)
                outs[-1][pl.ds(pl.multiple_of(row, 16), rows), lanes] = pieces[
                    block, side * rows : (side + 1) * rows, first : first + part
                ]


def pack_kernel(by_core, spot, grad_ref, got_ref, out):
    rows = out.shape[1]
    part = grad_ref.shape[1] // 4
    base = spot[3] * got_ref.shape[0]
    for block in range(4):
        lanes = slice(block * part, (block + 1) * part)
        for group in range(4):
            row = source_row(spot, group, rows, by_core)
            own = grad_ref[pl.ds(pl.multiple_of(base + row, 16), rows), lanes]
            total = own.astype(f32) + got_ref[pl.ds(row, rows), lanes].astype(f32)
            out[block, :, group * part : (group + 1) * part] = total.astype(out.dtype)


def pack_sides_kernel(spot, grad_ref, out):
    rows = out.shape[1] // 2
    part = grad_ref.shape[1] // 4
    for block in range(4):
        lanes = slice(block * part, (block + 1) * part)
        for side in range(2):
            base = jnp.bitwise_xor(spot[3], side) * 4 * rows
            for group in range(4):
                row = pl.multiple_of(base + source_row(spot, group, rows, False), 16)
                out[block, side * rows : (side + 1) * rows, group * part : (group + 1) * part] = (
                    grad_ref[pl.ds(row, rows), lanes]
                )


def split_sums_kernel(spot, one, two, keep1_ref, keep2_ref, send_ref):
    wide = keep1_ref.shape[1]
    keep1_ref[...] = one[:, :wide]
    keep2_ref[...] = two[:, :wide]
    send_ref[:, :wide] = one[:, wide:]
    send_ref[:, wide:] = two[:, wide:]


def turn_core_kernel(spot, keep1_ref, got_ref, send_ref):
    part = send_ref.shape[1] // 2
    send_ref[:, :part] = keep1_ref[:, part:]
    send_ref[:, part:] = got_ref[:, part : 2 * part]


def finish_kernel(spot, keep1_ref, keep2_ref, side_ref, core_ref, fc1_ref, fc2_ref):
    rows, part = fc1_ref.shape[0], fc2_ref.shape[1]

    def body(place):
        core, side = place // 2, place % 2
        parts = {
            (core, side): keep1_ref[:, :part],
            (core, 1 - side): side_ref[:, :part],
            (1 - core, side): core_ref[:, :part],
            (1 - core, 1 - side): core_ref[:, part:],
        }
        for (c, x), value in parts.items():
            fc1_ref[:, (2 * c + x) * part : (2 * c + x + 1) * part] = value.astype(f32)
        for at in range(2):
            lanes = slice(at * part, (at + 1) * part)
            first, other = (side * 2 + at) * rows, ((1 - side) * 2 + at) * rows
            fc2_ref[first : first + rows] = keep2_ref[:, lanes].astype(f32)
            fc2_ref[other : other + rows] = side_ref[:, (2 + at) * part : (3 + at) * part].astype(f32)

    for_each(spot[2] * 2 + spot[1], 4, body)


def qkv_blocks(tile, rows, count):
    for block in range(4):
        for at in range(count):
            for core in range(2):
                yield (
                    block,
                    core,
                    slice((2 * at + core) * rows, (2 * at + core + 1) * rows),
                    slice((block * count + at) * rows, (block * count + at + 1) * rows),
                )


def unpack_qkv_kernel(spot, *refs):
    pieces, kept = refs[:4], refs[4:]
    rows, wide = pieces[0].shape

    def body(place):
        tile, mine = place // 2, place % 2
        for block, core, there, here in qkv_blocks(tile, rows, wide // (2 * rows)):
            kept[core != mine][:, here] = pieces[(tile - block) % 4][:, there]

    for_each(spot[0] * 2 + spot[2], 8, body)


def pack_qkv_kernel(spot, own_ref, got_ref, last_ref, *outs):
    rows, wide = outs[0].shape
    part = last_ref.shape[1] // 4
    wide = wide - part

    def body(place):
        tile, mine = place // 2, place % 2
        for block, core, there, here in qkv_blocks(tile, rows, wide // (2 * rows)):
            source = own_ref if core == mine else got_ref
            outs[(block - tile) % 4][:, there] = source[:, here]
        for block in range(4):
            lanes = slice(block * part, (block + 1) * part)
            outs[(block - tile) % 4][:, wide:] = last_ref[:, lanes]

    for_each(spot[0] * 2 + spot[2], 8, body)


def place_kernel(count, rows_ref, *refs):
    ins, out = refs[:count], refs[count]
    for at, ref in enumerate(ins):
        out[pl.ds(pl.multiple_of(rows_ref[at], 16), ref.shape[0])] = ref[...]


def place_rows(pieces, rows, name):
    height = sum(piece.shape[0] for piece in pieces)
    shape = (height, pieces[0].shape[1]), pieces[0].dtype
    kernel = functools.partial(place_kernel, len(pieces))
    return on_blocks(kernel, jnp.stack(rows).astype(jnp.int32), pieces, [shape], name)[0]


def shards(
    tokens,
    cotangent,
    heights,
    widths,
    timesteps,
    rel_index,
    ln1_gain,
    ln1_bias,
    w_qkv,
    w_time,
    rel_table,
    w_out,
    out_bias,
    ln2_gain,
    ln2_bias,
    w_fc1,
    fc1_bias,
    w_fc2,
    fc2_bias,
):
    here, rows_here, cols, width = tokens.shape
    cells = rows_here * cols
    slots = here * cells
    key_rows = rows_here + 2 * HALO
    keys = key_rows * cols
    head_count = rel_table.shape[1]
    head_dim = width // head_count
    scale = head_dim ** (-0.5)
    image_devices = lax.axis_size("images")
    tiles = lax.axis_size("rows")
    low = image_devices // 8
    chunk = width // 8
    quarter = width // 4
    ff_part = fc1_bias.shape[0] // 16
    place = lax.axis_index("images")
    tile = lax.axis_index("rows")
    bits = {"c": low, "x": 2 * low, "y": 4 * low}
    at_c, at_x, at_y = (place // bits[name] % 2 for name in "cxy")


    def partner(value, bit):
        route = [(d, d ^ bit) for d in range(image_devices)]
        return lax.ppermute(value, "images", route)

    def swap(value, name):
        return partner(value, bits[name])

    def pick(at, pair):
        return jnp.where(at == 0, pair[0], pair[1]), jnp.where(at == 0, pair[1], pair[0])

    def after(value, *others):
        return lax.optimization_barrier((value,) + others)[0]

    def all_after(values, *others):
        return list(lax.optimization_barrier(tuple(values) + others))[: len(values)]

    def with_partner(value, name):
        return jnp.concatenate([value, swap(value, name)], 0)

    def shift(value, step):
        return lax.ppermute(value, "rows", [(d, (d + step) % tiles) for d in range(tiles)])

    def tiles_all(value):
        return lax.all_gather(value, "rows", axis=0)

    def tiles_sum(value):
        return lax.psum_scatter(value, "rows", scatter_dimension=0)

    def shifts(value):
        return [shift(value, step) for step in range(1, tiles)]

    def tile_gather(value):
        for bit in (1, 2):
            other = lax.ppermute(value, "rows", [(d, d ^ bit) for d in range(tiles)])
            value = jnp.concatenate(pick(tile // bit % 2, (value, other)), 1)
        return value

    def tile_scatter(value):
        for bit in (2, 1):
            size = value.shape[1] // 2
            kept, sent = pick(tile // bit % 2, (value[:, :size], value[:, size:]))
            value = kept + lax.ppermute(sent, "rows", [(d, d ^ bit) for d in range(tiles)])
        return value

    low_groups = [[g * low + d for d in range(low)] for g in range(8)]
    def low_gather(value):
        if low == 1:
            return value
        return lax.all_gather(value, "images", axis=0, tiled=True, axis_index_groups=low_groups)

    def low_scatter(value):
        if low == 1:
            return value
        return lax.psum_scatter(
            value, "images", scatter_dimension=0, tiled=True, axis_index_groups=low_groups
        )

    def sides_of(value):
        half = value.shape[0] // 2
        return value[:half], value[half:]

    def part_of(value, at):
        return lax.dynamic_index_in_dim(value, at, 0, keepdims=False)


    slot_row = tile * rows_here + jnp.arange(cells) // cols
    slot_col = jnp.arange(cells) % cols
    valid = (slot_row[None, :] < heights[:, None]) & (slot_col[None, :] < widths[:, None])
    valid_mask = valid.reshape(slots, 1).astype(f32)
    grad_out = cotangent.astype(f32).reshape(slots, width) * valid_mask
    grad_mlp_own = grad_out.astype(bf16)


    spot = jnp.stack([tile, at_x, at_c, at_y]).astype(jnp.int32)
    w_qkv, w_out, w_fc1, w_fc2 = (low_gather(w) for w in (w_qkv, w_out, w_fc1, w_fc2))
    wide = 2 * ff_part
    images = 2 * here
    padded = -(-(2 * quarter + 2 * wide) // LANES) * LANES

    def matrices(*dims):
        return [(dim, bf16) for dim in dims]

    qkv_parts = [w_qkv] + shifts(w_qkv)

    fc1_keep, fc1_send = on_blocks(
        split_core_kernel, spot, [w_fc1], matrices((chunk, wide), (chunk, wide)), "split_core"
    )
    fc1_got = swap(fc1_send, "c")
    keep1, keep2, send = on_blocks(
        split_side_kernel,
        spot,
        [fc1_keep, fc1_got, w_fc2],
        matrices((chunk, wide), (chunk, wide), (chunk, 2 * wide)),
        "split_side",
    )
    got = swap(send, "x")
    one, two = on_blocks(
        join_side_kernel,
        spot,
        [w_out, swap(w_out, "y"), keep1, keep2, got],
        matrices((chunk, padded), (chunk, 2 * wide)),
        "join_side",
    )
    two = with_partner(two, "y")


    orders = [bits["c"], bits["x"], bits["y"]]
    orders += [1 << b for b in range(low.bit_length() - 1)]
    facts = with_partner(jnp.stack([timesteps, heights, widths], 1), "c")
    heights_all, widths_all = facts[:, 1], facts[:, 2]
    steps_all = facts[:, 0]
    for bit in orders[1:]:
        steps_all = jnp.concatenate([steps_all, partner(steps_all, bit)], 0)
    qkv_keep, qkv_send = on_blocks(
        unpack_qkv_kernel,
        spot,
        qkv_parts,
        matrices((chunk, 12 * chunk), (chunk, 12 * chunk)),
        "unpack_qkv",
    )
    qkv_got = swap(qkv_send, "c")
    time_rows = w_time.shape[0]
    half_width = width // 2
    feature = place * time_rows + jnp.arange(time_rows)
    exponent = (feature % half_width).astype(f32)
    frequency = jnp.exp(-math.log(10000.0) * exponent / half_width)
    phases = steps_all.astype(f32)[:, None] * frequency[None, :]
    timing = jnp.where(feature[None, :] < half_width, jnp.cos(phases), jnp.sin(phases)).astype(bf16)
    time_part = dot(timing, after(w_time, keep1, qkv_keep))
    ties = {bits["y"]: qkv_got, bits["x"]: got}
    for bit in orders[:0:-1]:
        half = time_part.shape[0] // 2
        time_part = time_part[:half] + partner(time_part[half:], bit)
        if bit in ties:
            time_part = after(time_part, ties[bit])
    turned = jnp.concatenate([time_part[here:], time_part[:here]], 0)
    time_part = time_part + swap(turned, "c")

    gain_one, shift_one = ln1_gain.astype(f32), ln1_bias.astype(f32)
    gain_two, shift_two = ln2_gain.astype(f32), ln2_bias.astype(f32)
    flat_tokens = tokens.astype(f32).reshape(slots, width)
    normal_one, inverse_one = normalize(flat_tokens)
    normed = (normal_one * gain_one + shift_one).astype(bf16).reshape(tokens.shape)

    down = [(d, d + 1) for d in range(tiles - 1)]
    up = [(d + 1, d) for d in range(tiles - 1)]

    edges = [normed[:, rows_here - HALO :], normed[:, :HALO]]
    edges = all_after(edges, *qkv_parts[1:])
    above = lax.ppermute(edges[0], "rows", down)
    below = lax.ppermute(edges[1], "rows", up)

    qkv_pair = jnp.concatenate([qkv_keep, qkv_got], 0)
    time_pairs = tile_gather(time_part)
    qkv_pair = after(qkv_pair, time_part, above, below)
    one_parts = tiles_all(after(one, time_pairs, qkv_pair))
    two_parts = tiles_all(two)

    qkv_x, qkv_y = swap(qkv_pair, "x"), swap(qkv_pair, "y")
    normed_ext = jnp.concatenate([after(above, qkv_pair), normed, below], 1)
    normed_all = with_partner(normed_ext, "c").reshape(images * keys, width)
    qkv_x, qkv_y = all_after([qkv_x, qkv_y], normed_all)
    qkv_far = [swap(qkv_x[:chunk], "y"), swap(qkv_y[chunk:], "x")]
    qkv_far = all_after(qkv_far, one_parts)
    spots = at_y * 4 + at_x * 2 + at_c
    qkv_full = place_rows(
        [qkv_pair[:chunk], qkv_pair[chunk:], qkv_x[:chunk], qkv_x[chunk:]]
        + [qkv_y[:chunk], qkv_y[chunk:]]
        + qkv_far,
        [jnp.bitwise_xor(spots, step) * chunk for step in range(8)],
        "place_qkv",
    )

    out_rows, fc1_rows = on_blocks(
        functools.partial(unpack_kernel, True, 2, 1),
        spot,
        [after(one_parts, qkv_full)],
        matrices((2 * chunk, width), (4 * chunk, 4 * ff_part)),
        "unpack_fc1",
    )
    out_got = swap(out_rows, "x")
    places = at_y * 2 + at_x
    out_full = place_rows(
        [out_rows[:chunk], out_rows[chunk:], out_got[:chunk], out_got[chunk:]],
        [jnp.bitwise_xor(places, step) * chunk for step in (0, 2, 1, 3)],
        "place_out",
    )
    fc1_first, fc1_second = sides_of(fc1_rows)
    fc1_first, fc1_second = swap(fc1_first, "y"), swap(fc1_second, "y")
    size = fc1_rows.shape[0]
    fc1_full = place_rows(
        [fc1_rows, fc1_first, fc1_second],
        [at_y * size, (1 - at_y) * size, (1 - at_y) * size + size // 2],
        "place_fc1",
    )
    grad_mlp_x = with_partner(after(grad_mlp_own, qkv_full), "x")
    grad_mlp = with_partner(grad_mlp_x, "c")

    time_pairs = time_pairs.reshape(images, -1, 2, chunk)
    time_mine = pick(at_c, (time_pairs[:, :, 0], time_pairs[:, :, 1]))[0].reshape(images, width)
    half = width // 2
    time_all = jnp.concatenate(
        [time_mine[:, :half], jnp.zeros((images, half), f32), time_mine[:, half:]], 1
    )


    query_row = jnp.arange(cells) // cols
    query_col = jnp.arange(cells) % cols
    key_row = jnp.arange(keys) // cols - HALO
    key_col = jnp.arange(keys) % cols
    near = jnp.abs(key_row[None, :] - query_row[:, None]) <= HALO
    itself = jnp.arange(keys)[None, :] == jnp.arange(cells)[:, None] + HALO * cols
    global_key = tile * rows_here + key_row
    key_ok = (
        (global_key[None, :] >= 0)
        & (global_key[None, :] < heights_all[:, None])
        & (key_col[None, :] < widths_all[:, None])
    )
    allowed = (key_ok[:, None, :] & near[None] | itself[None]).astype(f32)
    heads = head_count // 2
    gaps = 2 * HALO + 1
    spans = 2 * cols - 1
    exact = lax.Precision.HIGHEST
    bucket_hits = (
        rel_index.reshape(-1)[:, None] == jnp.arange(rel_table.shape[0])[None, :]
    ).astype(f32)
    head_ids = jnp.arange(heads)
    head_hits = (
        jnp.arange(head_count)[:, None] == (head_ids // 2 * 4 + at_c * 2 + head_ids % 2)[None, :]
    ).astype(f32)
    table_mine = jnp.dot(after(rel_table, qkv_pair).astype(f32), head_hits, precision=exact)
    offset_values = lax.dot_general(
        table_mine, bucket_hits, (((0,), (1,)), ((), ())), precision=exact
    ).reshape(heads, gaps, spans)
    offset_values = jnp.pad(offset_values, ((0, 0), (0, 0), (0, LANES - spans)))
    bias = spread(offset_values, cells, keys, cols)


    normed_here = after(normed_all, out_rows)
    qkv = (
        dot(normed_here, qkv_full).reshape(images, keys, 3 * half) + time_all[:, None]
    ).astype(bf16)
    attended, prob = attend(qkv, bias, allowed, scale)
    attended = after(attended.reshape(images * cells, half), fc1_first)

    def core_sum(left, right, dims=NN):
        size = left.shape[0] // 2
        sent = swap(dot(left[size:], right, dims).astype(bf16), "c")
        return dot(left[:size], right, dims) + sent.astype(f32)

    middle = flat_tokens + core_sum(attended, out_full) + out_bias.astype(f32)
    normal_two, inverse_two = normalize(middle)
    second = (normal_two * gain_two + shift_two).astype(bf16)
    second_x, second_c = swap(second, "x"), swap(second, "c")
    second_x = after(second_x, fc1_full, grad_mlp_x)
    second = jnp.concatenate([second, second_x, second_c, swap(second_x, "c")], 0)


    member = at_c * 2 + at_x
    bias_parts = fc1_bias.astype(f32).reshape(tiles, 4, ff_part)
    bias_mine = lax.dynamic_index_in_dim(bias_parts, member, 1, keepdims=False).reshape(-1)
    hidden_pre = dot(second, fc1_full) + bias_mine
    hidden_act, hidden_slope = gelu_and_slope(hidden_pre)
    hidden = hidden_act.astype(bf16)
    hidden_slope = hidden_slope.astype(bf16)
    (fc2_full,) = on_blocks(
        functools.partial(unpack_kernel, False, 0, 2),
        spot,
        [after(two_parts, middle)],
        matrices((8 * chunk, width)),
        "unpack_fc2",
    )
    grad_pre = (dot(grad_mlp, fc2_full, NT) * hidden_slope.astype(f32)).astype(bf16)
    grad_second = core_sum(grad_pre, fc1_full, NT)
    grad_second_sent = grad_second[slots:].astype(bf16)
    grad_second_got = swap(grad_second_sent, "x")
    grad_fc2 = dot(after(hidden, grad_second_sent), grad_mlp, TN).astype(bf16)
    (two_packed,) = on_blocks(
        pack_sides_kernel, spot, [grad_fc2], matrices((tiles, 2 * chunk, 2 * wide)), "pack_fc2"
    )
    two_sum = tiles_sum(two_packed)
    grad_second_got = after(grad_second_got, two_packed)
    grad_second = grad_second[:slots] + grad_second_got.astype(f32)
    grad_fc1 = dot(second, grad_pre, TN).astype(bf16)
    grad_fc2_bias = jnp.sum(grad_mlp_own, 0, dtype=f32)
    grad_fc1_bias = jnp.sum(grad_pre, 0, dtype=f32)

    grad_gain_two = jnp.sum(grad_second * normal_two, 0)
    grad_shift_two = jnp.sum(grad_second, 0)
    grad_middle = grad_out + norm_back(grad_second * gain_two, normal_two, inverse_two)
    grad_branch_own = grad_middle.astype(bf16)
    grad_out_bias = jnp.sum(grad_branch_own, 0, dtype=f32)
    grad_branch = with_partner(grad_branch_own, "c")


    def add_bf16(one, two):
        return (one.astype(f32) + two.astype(f32)).astype(bf16)

    def sides(grad):
        return grad.reshape((2, -1) + grad.shape[1:])

    fc1_got = swap(part_of(sides(grad_fc1), 1 - at_y), "y")
    grad_att = dot(grad_branch, out_full, NT).astype(bf16)
    grad_out_weight = dot(attended, grad_branch, TN).astype(bf16)
    out_sides = grad_out_weight.reshape(2, 2, chunk, width)
    out_sent = out_sides[:, 0], out_sides[:, 1]
    out_kept, out_sent = pick(at_x, out_sent)
    grad_att = after(grad_att, out_sent).reshape(images, cells, half)
    out_got = swap(out_sent, "x")

    grad_proj, grad_strip = attend_back(qkv, prob, grad_att, scale, cols)
    flat_proj = grad_proj.reshape(images * keys, 3 * half)
    grad_qkv = row_major(dot(normed_all, flat_proj, TN).astype(bf16))
    blocks = grad_qkv.reshape(2, 2, 2, chunk, 12 * chunk)

    def blocks_at(y, x, core):
        first = [0 if at is None else at for at in (y, x, core)] + [0, 0]
        size = [2 if at is None else 1 for at in (y, x, core)] + list(blocks.shape[3:])
        return lax.dynamic_slice(blocks, first, size).reshape(-1, chunk, 12 * chunk)

    own_sent = blocks_at(1 - at_y, None, at_c)
    other_sent = blocks_at(None, 1 - at_x, 1 - at_c)
    own_got, other_got = swap(own_sent, "y"), swap(other_sent, "x")
    out_mine = add_bf16(out_kept, after(out_got, grad_qkv))
    out_got = swap(part_of(out_mine, 1 - at_y), "y")
    out_mine = add_bf16(part_of(out_mine, at_y), out_got)

    (one_packed,) = on_blocks(
        functools.partial(pack_kernel, True),
        spot,
        [grad_fc1, after(fc1_got, own_sent, other_sent)],
        matrices((tiles, chunk, 2 * wide)),
        "pack_fc1",
    )
    one_sum = tiles_sum(one_packed)
    flat_proj = after(flat_proj, own_sent, other_sent, one_packed)
    grad_ext = core_sum(flat_proj, qkv_full, NT).reshape(here, key_rows, cols, width)
    mlp_out = core_sum(after(hidden, grad_ext), fc2_full)

    from_below = lax.ppermute(grad_ext[:, :HALO].astype(bf16), "rows", up).astype(f32)
    from_above = lax.ppermute(grad_ext[:, HALO + rows_here :].astype(bf16), "rows", down)
    from_above = from_above.astype(f32)
    rest = ((0, 0), (rows_here - HALO, 0), (0, 0), (0, 0))
    grad_normed = (
        grad_ext[:, HALO : HALO + rows_here]
        + jnp.pad(from_below, rest)
        + jnp.pad(from_above, (rest[0], rest[1][::-1], rest[2], rest[3]))
    ).reshape(slots, width)
    grad_gain_one = jnp.sum(grad_normed * normal_one, 0)
    grad_shift_one = jnp.sum(grad_normed, 0)
    grad_input = grad_middle + norm_back(grad_normed * gain_one, normal_one, inverse_one)
    grad_tokens = grad_input.reshape(tokens.shape).astype(bf16)


    grad_offsets = grad_strip[:, :, :spans].reshape(heads, gaps * spans)
    grad_table = jnp.dot(grad_offsets, bucket_hits, precision=exact)
    grad_table = jnp.dot(head_hits, grad_table, precision=exact)


    own_got, other_got = all_after([own_got, other_got], grad_ext)
    own_two = add_bf16(blocks_at(at_y, None, at_c), own_got)
    other_two = add_bf16(blocks_at(None, at_x, 1 - at_c), other_got)
    far_sent = part_of(own_two, 1 - at_x)
    own_got = swap(far_sent, "x")
    mlp_sent = after(mlp_out[slots:].astype(bf16), far_sent)
    mlp_out = mlp_out[:slots] + swap(mlp_sent, "x").astype(f32) + fc2_bias.astype(f32)
    mixed = (valid_mask * (middle + mlp_out)).reshape(tokens.shape).astype(bf16)
    other_got = swap(part_of(other_two, 1 - at_y), "y")
    own_rows_got, other_rows_got = own_got, other_got


    def row(value):
        return value.reshape(-1, width)

    mine = (jnp.arange(4) == member).astype(f32)
    fc1_bias_all = grad_fc1_bias.reshape(tiles, 1, ff_part) * mine[None, :, None]
    buckets = rel_table.shape[0]
    table_rows = grad_table.reshape(4, -1, buckets)
    table_rows = jnp.concatenate([table_rows[:, at] for at in range(table_rows.shape[1])], 1)
    table_rows = jnp.pad(table_rows, ((0, 0), (0, width - table_rows.shape[1])))
    small = [
        row(grad_gain_one),
        row(grad_shift_one),
        row(grad_out_bias),
        row(grad_gain_two),
        row(grad_shift_two),
        row(grad_fc2_bias),
        row(fc1_bias_all),
        table_rows,
    ]
    count = 6 + 4 * ff_part * tiles // width + 4
    sums = jnp.sum(grad_proj, 1, dtype=f32)
    sums = jnp.concatenate([sums[:, :half], sums[:, 2 * half :]], 1)
    total = jnp.concatenate(small + [sums], 0)
    for step in range(tiles.bit_length() - 1):
        route = [(d, d ^ (1 << step)) for d in range(tiles)]
        total = total + lax.ppermute(total, "rows", route)
    own_rows_got, other_rows_got = all_after([own_rows_got, other_rows_got], total)

    own_rows = add_bf16(part_of(own_two, at_x), own_rows_got)
    other_rows = add_bf16(part_of(other_two, at_y), other_rows_got)
    other_rows = swap(other_rows, "c")
    last_parts = on_blocks(
        pack_qkv_kernel,
        spot,
        [own_rows, other_rows, out_mine],
        matrices(*[(chunk, 6 * chunk + quarter)] * 4),
        "pack_qkv",
    )
    last = last_parts[0].astype(f32)
    for step in range(1, tiles):
        last = last + shift(last_parts[step], step).astype(f32)
    qkv_own, out_own = last[:, : 6 * chunk], last[:, 6 * chunk :]

    two_sum = after(two_sum, far_sent)
    two_sum = add_bf16(two_sum[:chunk], swap(two_sum[chunk:], "y"))
    keep1, keep2, send = on_blocks(
        split_sums_kernel,
        spot,
        [one_sum, two_sum],
        matrices((chunk, wide), (chunk, wide), (chunk, 2 * wide)),
        "split_sums",
    )
    side_got = swap(send, "x")
    (send,) = on_blocks(
        turn_core_kernel, spot, [keep1, side_got], matrices((chunk, wide)), "turn_core"
    )
    fc1_own, fc2_own = on_blocks(
        finish_kernel,
        spot,
        [keep1, keep2, side_got, swap(send, "c")],
        [((chunk, 2 * wide), f32), ((4 * chunk, ff_part), f32)],
        "finish",
    )


    total = after(total, *last_parts)
    total, sums = total[:count], total[count:]
    size = width // tiles
    sums = lax.select_n(tile, *[sums[:, at * size : (at + 1) * size] for at in range(tiles)])
    turned = jnp.concatenate([sums[here:], sums[:here]], 0)

    def both(total, sums, bit):
        room = ((0, 0), (0, width - sums.shape[1]))
        got = partner(jnp.concatenate([total, jnp.pad(sums, room)], 0), bit)
        return total + got[:count], got[count:, : sums.shape[1]]

    total, other = both(total, turned, orders[0])
    pair = pick(at_c, (sums.reshape(images, -1, 1, chunk), other.reshape(images, -1, 1, chunk)))
    sums = jnp.concatenate(pair, 2).reshape(images, -1)
    for bit in orders[1:]:
        total, other = both(total, sums, bit)
        sums = jnp.concatenate([sums, other], 0)
    grad_time = lax.dot_general(timing.astype(f32), sums, TN, precision=exact)
    table = total[count - 4 :, : head_count // 4 * buckets].reshape(head_count, buckets).T
    return (
        mixed,
        grad_tokens,
        total[0],
        total[1],
        low_scatter(qkv_own),
        grad_time,
        table,
        low_scatter(out_own),
        total[2],
        total[3],
        total[4],
        low_scatter(fc1_own),
        total[6 : count - 4].reshape(-1),
        low_scatter(fc2_own),
        total[5],
    )


def solution(mesh):
    tokens, image, weight = P("images", "rows", None, None), P("images"), P("images", "rows")
    return jax.shard_map(
        shards,
        mesh=mesh,
        in_specs=(
            tokens, tokens, image, image, image, P(), P(), P(), weight, weight,
            P(), weight, P(), P(), P(), weight, P(), weight, P(),
        ),
        out_specs=(
            tokens, tokens, P(), P(), weight, weight, P(), weight, P(), P(),
            P(), weight, P(), weight, P(),
        ),
        check_vma=False,
    )
```

```python
import functools
import math

import jax
import jax.numpy as jnp
from jax import lax
from jax.experimental import pallas as pl
from jax.experimental.layout import Layout, with_layout_constraint
from jax.experimental.pallas import tpu as pltpu
from jax.sharding import PartitionSpec as P

HALO = 2
LANES = 128

norm_eps = 1e-06
masked_score = -1000000000.0

f32 = jnp.float32
bf16 = jnp.bfloat16

NN = (((1,), (0,)), ((), ()))
NT = (((1,), (1,)), ((), ()))
TN = (((0,), (0,)), ((), ()))


def dot(left, right, dims=NN):
    return lax.dot_general(left, right, dims, preferred_element_type=f32)


def row_major(value):
    return with_layout_constraint(value, Layout(major_to_minor=tuple(range(value.ndim))))


def normalize(values):
    centre = values - jnp.mean(values, -1, keepdims=True)
    spread = jnp.mean(centre * centre, -1, keepdims=True)
    inverse = lax.rsqrt(spread + norm_eps)
    return (centre * inverse, inverse)


def norm_back(grad_hat, normal_part, inverse):
    first_mean = jnp.mean(grad_hat, -1, keepdims=True)
    second_mean = jnp.mean(grad_hat * normal_part, -1, keepdims=True)
    return inverse * (grad_hat - first_mean - normal_part * second_mean)


def gelu_and_slope(values):
    slant = math.sqrt(2.0 / math.pi)
    square = values * values
    curve = jnp.tanh(slant * values * (1.0 + 0.044715 * square))
    lift = 0.5 * (1.0 + curve)
    bend = 0.5 * values * (1.0 - curve * curve) * slant * (1.0 + 3.0 * 0.044715 * square)
    return values * lift, lift + bend


def window(head, head_dim, width):
    first, last = head * head_dim, (head + 1) * head_dim
    start = first // LANES * LANES
    stop = min(-(-last // LANES) * LANES, width)
    return first, last, start, stop


def lane_mask(first, last, start, stop, kind):
    lane = lax.broadcasted_iota(jnp.int32, (1, stop - start), 1) + start
    return jnp.where((lane >= first) & (lane < last), 1.0, 0.0).astype(kind)


def add_tiles(tiles, values, start, stop):
    for at in range(start, stop, LANES):
        part = values[:, at - start : min(at + LANES, stop) - start]
        tiles[at] = part if at not in tiles else tiles[at] + part


def store_tiles(ref, tiles, scale=None, rows=slice(None), base=0):
    for at, part in tiles.items():
        if scale is not None:
            part = part * scale
        ref[0, rows, base + at : base + at + part.shape[1]] = part.astype(ref.dtype)


def spread_kernel(cols, offsets_ref, bias_ref):
    bias_ref[...] = jnp.zeros_like(bias_ref)
    for head in range(bias_ref.shape[0]):
        for gap in range(2 * HALO + 1):
            line = offsets_ref[head, gap : gap + 1]
            lines = jnp.broadcast_to(line, (cols, line.shape[1]))
            first = line.shape[1] - cols + 1
            block = pltpu.roll(lines, first, 1, stride=1, stride_axis=0)[:, :cols]
            for row in range(bias_ref.shape[1] // cols):
                at = (row + gap) * cols
                bias_ref[head, row * cols : (row + 1) * cols, at : at + cols] = block


def attend_kernel(heads, scale, edge, qkv_ref, bias_ref, allow_ref, o_ref, p_ref):
    half = o_ref.shape[-1]
    cells = o_ref.shape[1]

    allowed = allow_ref[0] > 0.5
    queries = qkv_ref[0, edge : edge + cells, :half]
    key = qkv_ref[0, :, half : 2 * half]
    value = qkv_ref[0, :, 2 * half :]
    tiles = {}
    for head in range(heads):
        span = window(head, half // heads, half)
        start, stop = span[2:]
        query = queries[:, start:stop] * lane_mask(*span, bf16)
        scores = dot(query, key[:, start:stop], NT) * scale + bias_ref[head]
        scores = jnp.where(allowed, scores, masked_score)
        expo = jnp.exp(scores - jnp.max(scores, -1, keepdims=True))
        prob = (expo / jnp.sum(expo, -1, keepdims=True)).astype(bf16)
        p_ref[0, head] = prob
        out = dot(prob, value[:, start:stop]) * lane_mask(*span, f32)
        add_tiles(tiles, out, start, stop)
    store_tiles(o_ref, tiles)


def attend_back_kernel(
    heads, scale, edge, cols, qkv_ref, p_ref, dz_ref, weight_ref, d_ref, g_ref, sum_ref
):
    cells = dz_ref.shape[1]
    half = weight_ref.shape[0]
    rows = cells // cols
    middle = slice(edge, edge + cells)
    step = pl.program_id(0)

    @pl.when(step == 0)
    def _():
        sum_ref[...] = jnp.zeros_like(sum_ref)

    queries = qkv_ref[0, middle, :half]
    key = qkv_ref[0, :, half : 2 * half]
    value = qkv_ref[0, :, 2 * half :]
    grad_outs = dot(dz_ref[0], weight_ref[...], NT).astype(bf16)
    dq_tiles, dk_tiles, dv_tiles = {}, {}, {}
    for head in range(heads):
        span = window(head, half // heads, half)
        start, stop = span[2:]
        mask = lane_mask(*span, bf16)
        query = queries[:, start:stop] * mask
        grad_out = grad_outs[:, start:stop] * mask
        prob = p_ref[0, head]
        full = prob.astype(f32)
        weighted = full * dot(grad_out, value[:, start:stop], NT)
        grad_score = (weighted - full * jnp.sum(weighted, -1, keepdims=True)).astype(bf16)
        sum_ref[head] += grad_score.astype(f32)
        dq = dot(grad_score, key[:, start:stop]) * lane_mask(*span, f32)
        add_tiles(dq_tiles, dq, start, stop)
        add_tiles(dk_tiles, dot(grad_score, query, TN), start, stop)
        add_tiles(dv_tiles, dot(prob, grad_out, TN), start, stop)
    d_ref[0, :edge, :half] = jnp.zeros((edge, half), bf16)
    d_ref[0, edge + cells :, :half] = jnp.zeros((edge, half), bf16)
    store_tiles(d_ref, dq_tiles, scale, middle)
    store_tiles(d_ref, dk_tiles, scale, base=half)
    store_tiles(d_ref, dv_tiles, base=2 * half)

    @pl.when(step == pl.num_programs(0) - 1)
    def _():
        ids = [lax.broadcasted_iota(jnp.int32, (cols, cols), axis) for axis in range(2)]
        turn = jnp.where(ids[0] + ids[1] == cols - 1, 1.0, 0.0)
        for head in range(heads):
            total = sum_ref[head, :cols]
            for row in range(1, rows):
                part = sum_ref[head, row * cols : (row + 1) * cols]
                total += pltpu.roll(part, part.shape[1] - row * cols, 1)
            total = jnp.dot(turn, total, precision=lax.Precision.HIGHEST)
            for gap in range(2 * HALO + 1):
                block = total[:, gap * cols : (gap + 1) * cols]
                block = jnp.concatenate([block, jnp.zeros((cols, LANES - cols), f32)], 1)
                block = pltpu.roll(block, 0, 1, stride=1, stride_axis=0)
                g_ref[head, gap : gap + 1] = jnp.sum(block, 0, keepdims=True)


def per_image(*dims):
    return pl.BlockSpec((1,) + dims, lambda i: (i,) + (0,) * len(dims))


def whole(*dims):
    return pl.BlockSpec(dims, lambda i: (0,) * len(dims))


def spread(offsets, cells, keys, cols):
    block = pl.BlockSpec(memory_space=pltpu.VMEM)
    return pl.pallas_call(
        functools.partial(spread_kernel, cols),
        in_specs=[block],
        out_specs=block,
        out_shape=jax.ShapeDtypeStruct((offsets.shape[0], cells, keys), f32),
        name="spread",
    )(offsets)


def attend(qkv, bias, allowed, scale):
    images, keys, width = qkv.shape
    heads, cells, _ = bias.shape
    half = width // 3
    return pl.pallas_call(
        functools.partial(attend_kernel, heads, scale, (keys - cells) // 2),
        grid=(images,),
        in_specs=[per_image(keys, width), whole(heads, cells, keys), per_image(cells, keys)],
        out_specs=[per_image(cells, half), per_image(heads, cells, keys)],
        out_shape=[
            jax.ShapeDtypeStruct((images, cells, half), bf16),
            jax.ShapeDtypeStruct((images, heads, cells, keys), bf16),
        ],
        compiler_params=pltpu.CompilerParams(vmem_limit_bytes=56 << 20),
        cost_estimate=pl.CostEstimate(flops=1, bytes_accessed=1, transcendentals=0),
        name="attend",
    )(qkv, bias, allowed)


def attend_back(qkv, prob, grad, weight, scale, cols):
    images, keys, width = qkv.shape
    heads, cells = prob.shape[1:3]
    half, total = weight.shape
    return pl.pallas_call(
        functools.partial(attend_back_kernel, heads, scale, (keys - cells) // 2, cols),
        grid=(images,),
        in_specs=[
            per_image(keys, width),
            per_image(heads, cells, keys),
            per_image(cells, total),
            whole(half, total),
        ],
        out_specs=[per_image(keys, width), whole(heads, 2 * HALO + 1, LANES)],
        out_shape=[
            jax.ShapeDtypeStruct((images, keys, width), bf16),
            jax.ShapeDtypeStruct((heads, 2 * HALO + 1, LANES), f32),
        ],
        scratch_shapes=[pltpu.VMEM((heads, cells, keys), f32)],
        compiler_params=pltpu.CompilerParams(vmem_limit_bytes=56 << 20),
        cost_estimate=pl.CostEstimate(flops=1, bytes_accessed=1, transcendentals=0),
        name="attend_back",
    )(qkv, prob, grad, weight)


def on_blocks(kernel, spot, values, shapes, name):
    block = pl.BlockSpec(memory_space=pltpu.VMEM)
    return pl.pallas_call(
        kernel,
        in_specs=[pl.BlockSpec(memory_space=pltpu.SMEM)] + [block] * len(values),
        out_specs=[block] * len(shapes),
        out_shape=[jax.ShapeDtypeStruct(shape, kind) for shape, kind in shapes],
        compiler_params=pltpu.CompilerParams(vmem_limit_bytes=32 << 20),
        name=name,
    )(spot, *values)


def for_each(value, count, body):
    for at in range(count):
        pl.when(value == at)(functools.partial(body, at))


def source_row(spot, group, size, by_core):
    side = jnp.bitwise_xor(spot[1], group >> 1)
    core = jnp.bitwise_xor(spot[2], group & 1) if by_core else group & 1
    return pl.multiple_of((side * 2 + core) * size, 16)


def split_core_kernel(spot, w_ref, keep_ref, send_ref):
    half = keep_ref.shape[1]

    def body(core):
        keep_ref[...] = w_ref[:, core * half : (core + 1) * half]
        send_ref[...] = w_ref[:, (1 - core) * half : (2 - core) * half]

    for_each(spot[2], 2, body)


def split_side_kernel(spot, own_ref, got_ref, fc2_ref, keep1_ref, keep2_ref, send_ref):
    rows, wide = own_ref.shape
    part = wide // 2

    def body(side):
        for at, ref in enumerate((own_ref, got_ref)):
            lanes = slice(at * part, (at + 1) * part)
            keep1_ref[:, lanes] = ref[:, side * part : (side + 1) * part]
            send_ref[:, lanes] = ref[:, (1 - side) * part : (2 - side) * part]
        for at in range(2):
            first = (side * 2 + at) * rows
            other = ((1 - side) * 2 + at) * rows
            keep2_ref[:, at * part : (at + 1) * part] = fc2_ref[first : first + rows]
            send_ref[:, wide + at * part : wide + (at + 1) * part] = fc2_ref[other : other + rows]

    for_each(spot[1], 2, body)


def fill_lanes(ref, first):
    if first < ref.shape[-1]:
        ref[:, first:] = jnp.zeros((ref.shape[0], ref.shape[-1] - first), ref.dtype)


def join_side_kernel(spot, out_ref, far_ref, keep1_ref, keep2_ref, got_ref, one_ref, two_ref):
    part = 2 * out_ref.shape[1]
    wide = keep1_ref.shape[1]
    one_ref[:, : part // 2] = out_ref[...]
    one_ref[:, part // 2 : part] = far_ref[...]
    one_ref[:, part : part + wide] = keep1_ref[...]
    one_ref[:, part + wide : part + 2 * wide] = got_ref[:, :wide]
    fill_lanes(one_ref, part + 2 * wide)
    two_ref[:, :wide] = keep2_ref[...]
    two_ref[:, wide:] = got_ref[:, wide:]


def unpack_kernel(by_core, lead, sides, spot, pieces, *outs):
    rows = pieces.shape[1] // sides
    part = outs[-1].shape[1] // 4
    for block in range(4):
        lanes = slice(block * part, (block + 1) * part)
        for at in range(lead):
            outs[0][at * rows : (at + 1) * rows, lanes] = pieces[
                block, :, at * part : (at + 1) * part
            ]
        for side in range(sides):
            base = jnp.bitwise_xor(spot[3], side) * 4 * rows if sides > 1 else 0
            for group in range(4):
                first = (group + lead) * part
                row = base + source_row(spot, group, rows, by_core)
                outs[-1][pl.ds(pl.multiple_of(row, 16), rows), lanes] = pieces[
                    block, side * rows : (side + 1) * rows, first : first + part
                ]


def pack_kernel(by_core, spot, grad_ref, got_ref, out):
    rows = out.shape[1]
    part = grad_ref.shape[1] // 4
    base = spot[3] * got_ref.shape[0]
    for block in range(4):
        lanes = slice(block * part, (block + 1) * part)
        for group in range(4):
            row = source_row(spot, group, rows, by_core)
            own = grad_ref[pl.ds(pl.multiple_of(base + row, 16), rows), lanes]
            total = own.astype(f32) + got_ref[pl.ds(row, rows), lanes].astype(f32)
            out[block, :, group * part : (group + 1) * part] = total.astype(out.dtype)


def pack_sides_kernel(spot, grad_ref, out):
    rows = out.shape[1] // 2
    part = grad_ref.shape[1] // 4
    for block in range(4):
        lanes = slice(block * part, (block + 1) * part)
        for side in range(2):
            base = jnp.bitwise_xor(spot[3], side) * 4 * rows
            for group in range(4):
                row = pl.multiple_of(base + source_row(spot, group, rows, False), 16)
                out[block, side * rows : (side + 1) * rows, group * part : (group + 1) * part] = (
                    grad_ref[pl.ds(row, rows), lanes]
                )


def split_sums_kernel(spot, one, two, keep1_ref, keep2_ref, send_ref):
    wide = keep1_ref.shape[1]
    keep1_ref[...] = one[:, :wide]
    keep2_ref[...] = two[:, :wide]
    send_ref[:, :wide] = one[:, wide:]
    send_ref[:, wide:] = two[:, wide:]


def turn_core_kernel(spot, keep1_ref, got_ref, send_ref):
    part = send_ref.shape[1] // 2
    send_ref[:, :part] = keep1_ref[:, part:]
    send_ref[:, part:] = got_ref[:, part : 2 * part]


def finish_kernel(spot, keep1_ref, keep2_ref, side_ref, core_ref, fc1_ref, fc2_ref):
    rows, part = fc1_ref.shape[0], fc2_ref.shape[1]

    def body(place):
        core, side = place // 2, place % 2
        parts = {
            (core, side): keep1_ref[:, :part],
            (core, 1 - side): side_ref[:, :part],
            (1 - core, side): core_ref[:, :part],
            (1 - core, 1 - side): core_ref[:, part:],
        }
        for (c, x), value in parts.items():
            fc1_ref[:, (2 * c + x) * part : (2 * c + x + 1) * part] = value.astype(f32)
        for at in range(2):
            lanes = slice(at * part, (at + 1) * part)
            first, other = (side * 2 + at) * rows, ((1 - side) * 2 + at) * rows
            fc2_ref[first : first + rows] = keep2_ref[:, lanes].astype(f32)
            fc2_ref[other : other + rows] = side_ref[:, (2 + at) * part : (3 + at) * part].astype(f32)

    for_each(spot[2] * 2 + spot[1], 4, body)


def qkv_blocks(tile, rows, count):
    for block in range(4):
        for at in range(count):
            for core in range(2):
                yield (
                    block,
                    core,
                    slice((2 * at + core) * rows, (2 * at + core + 1) * rows),
                    slice((block * count + at) * rows, (block * count + at + 1) * rows),
                )


def unpack_qkv_kernel(spot, *refs):
    pieces, kept = refs[:4], refs[4:]
    rows, wide = pieces[0].shape

    def body(place):
        tile, mine = place // 2, place % 2
        for block, core, there, here in qkv_blocks(tile, rows, wide // (2 * rows)):
            kept[core != mine][:, here] = pieces[(tile - block) % 4][:, there]

    for_each(spot[0] * 2 + spot[2], 8, body)


def pack_qkv_kernel(spot, own_ref, got_ref, last_ref, *outs):
    rows, wide = outs[0].shape
    part = last_ref.shape[1] // 4
    wide = wide - part

    def body(place):
        tile, mine = place // 2, place % 2
        for block, core, there, here in qkv_blocks(tile, rows, wide // (2 * rows)):
            source = own_ref if core == mine else got_ref
            outs[(block - tile) % 4][:, there] = source[:, here]
        for block in range(4):
            lanes = slice(block * part, (block + 1) * part)
            outs[(block - tile) % 4][:, wide:] = last_ref[:, lanes]

    for_each(spot[0] * 2 + spot[2], 8, body)


def place_kernel(count, rows_ref, *refs):
    ins, out = refs[:count], refs[count]
    for at, ref in enumerate(ins):
        out[pl.ds(pl.multiple_of(rows_ref[at], 16), ref.shape[0])] = ref[...]


def place_rows(pieces, rows, name):
    height = sum(piece.shape[0] for piece in pieces)
    shape = (height, pieces[0].shape[1]), pieces[0].dtype
    kernel = functools.partial(place_kernel, len(pieces))
    return on_blocks(kernel, jnp.stack(rows).astype(jnp.int32), pieces, [shape], name)[0]


def shards(
    tokens,
    cotangent,
    heights,
    widths,
    timesteps,
    rel_index,
    ln1_gain,
    ln1_bias,
    w_qkv,
    w_time,
    rel_table,
    w_out,
    out_bias,
    ln2_gain,
    ln2_bias,
    w_fc1,
    fc1_bias,
    w_fc2,
    fc2_bias,
):
    here, rows_here, cols, width = tokens.shape
    cells = rows_here * cols
    slots = here * cells
    key_rows = rows_here + 2 * HALO
    keys = key_rows * cols
    head_count = rel_table.shape[1]
    head_dim = width // head_count
    scale = head_dim ** (-0.5)
    image_devices = lax.axis_size("images")
    tiles = lax.axis_size("rows")
    low = image_devices // 8
    chunk = width // 8
    quarter = width // 4
    ff_part = fc1_bias.shape[0] // 16
    place = lax.axis_index("images")
    tile = lax.axis_index("rows")
    bits = {"c": low, "x": 2 * low, "y": 4 * low}
    at_c, at_x, at_y = (place // bits[name] % 2 for name in "cxy")


    def partner(value, bit):
        route = [(d, d ^ bit) for d in range(image_devices)]
        return lax.ppermute(value, "images", route)

    def swap(value, name):
        return partner(value, bits[name])

    def pick(at, pair):
        return jnp.where(at == 0, pair[0], pair[1]), jnp.where(at == 0, pair[1], pair[0])

    def after(value, *others):
        return lax.optimization_barrier((value,) + others)[0]

    def all_after(values, *others):
        return list(lax.optimization_barrier(tuple(values) + others))[: len(values)]

    def with_partner(value, name):
        return jnp.concatenate([value, swap(value, name)], 0)

    def shift(value, step):
        return lax.ppermute(value, "rows", [(d, (d + step) % tiles) for d in range(tiles)])

    def tiles_all(value):
        return lax.all_gather(value, "rows", axis=0)

    def tiles_sum(value):
        return lax.psum_scatter(value, "rows", scatter_dimension=0)

    def shifts(value):
        return [shift(value, step) for step in range(1, tiles)]

    def tile_gather(value):
        for bit in (1, 2):
            other = lax.ppermute(value, "rows", [(d, d ^ bit) for d in range(tiles)])
            value = jnp.concatenate(pick(tile // bit % 2, (value, other)), 1)
        return value

    def tile_scatter(value):
        for bit in (2, 1):
            size = value.shape[1] // 2
            kept, sent = pick(tile // bit % 2, (value[:, :size], value[:, size:]))
            value = kept + lax.ppermute(sent, "rows", [(d, d ^ bit) for d in range(tiles)])
        return value

    low_groups = [[g * low + d for d in range(low)] for g in range(8)]
    def low_gather(value):
        if low == 1:
            return value
        return lax.all_gather(value, "images", axis=0, tiled=True, axis_index_groups=low_groups)

    def low_scatter(value):
        if low == 1:
            return value
        return lax.psum_scatter(
            value, "images", scatter_dimension=0, tiled=True, axis_index_groups=low_groups
        )

    def sides_of(value):
        half = value.shape[0] // 2
        return value[:half], value[half:]

    def part_of(value, at):
        return lax.dynamic_index_in_dim(value, at, 0, keepdims=False)


    slot_row = tile * rows_here + jnp.arange(cells) // cols
    slot_col = jnp.arange(cells) % cols
    valid = (slot_row[None, :] < heights[:, None]) & (slot_col[None, :] < widths[:, None])
    valid_mask = valid.reshape(slots, 1).astype(f32)
    grad_out = cotangent.astype(f32).reshape(slots, width) * valid_mask
    grad_mlp_own = grad_out.astype(bf16)


    spot = jnp.stack([tile, at_x, at_c, at_y]).astype(jnp.int32)
    w_qkv, w_out, w_fc1, w_fc2 = (low_gather(w) for w in (w_qkv, w_out, w_fc1, w_fc2))
    wide = 2 * ff_part
    images = 2 * here
    padded = -(-(2 * quarter + 2 * wide) // LANES) * LANES

    def matrices(*dims):
        return [(dim, bf16) for dim in dims]

    qkv_parts = [w_qkv] + shifts(w_qkv)

    fc1_keep, fc1_send = on_blocks(
        split_core_kernel, spot, [w_fc1], matrices((chunk, wide), (chunk, wide)), "split_core"
    )
    fc1_got = swap(fc1_send, "c")
    keep1, keep2, send = on_blocks(
        split_side_kernel,
        spot,
        [fc1_keep, fc1_got, w_fc2],
        matrices((chunk, wide), (chunk, wide), (chunk, 2 * wide)),
        "split_side",
    )
    got = swap(send, "x")
    one, two = on_blocks(
        join_side_kernel,
        spot,
        [w_out, swap(w_out, "y"), keep1, keep2, got],
        matrices((chunk, padded), (chunk, 2 * wide)),
        "join_side",
    )
    two = with_partner(two, "y")


    orders = [bits["c"], bits["x"], bits["y"]]
    orders += [1 << b for b in range(low.bit_length() - 1)]
    facts = with_partner(jnp.stack([timesteps, heights, widths], 1), "c")
    heights_all, widths_all = facts[:, 1], facts[:, 2]
    steps_all = facts[:, 0]
    for bit in orders[1:]:
        steps_all = jnp.concatenate([steps_all, partner(steps_all, bit)], 0)
    qkv_keep, qkv_send = on_blocks(
        unpack_qkv_kernel,
        spot,
        qkv_parts,
        matrices((chunk, 12 * chunk), (chunk, 12 * chunk)),
        "unpack_qkv",
    )
    qkv_got = swap(qkv_send, "c")
    time_rows = w_time.shape[0]
    half_width = width // 2
    feature = place * time_rows + jnp.arange(time_rows)
    exponent = (feature % half_width).astype(f32)
    frequency = jnp.exp(-math.log(10000.0) * exponent / half_width)
    phases = steps_all.astype(f32)[:, None] * frequency[None, :]
    timing = jnp.where(feature[None, :] < half_width, jnp.cos(phases), jnp.sin(phases)).astype(bf16)
    time_part = dot(timing, after(w_time, keep1, qkv_keep))
    ties = {bits["y"]: qkv_got, bits["x"]: got}
    for bit in orders[:0:-1]:
        half = time_part.shape[0] // 2
        time_part = time_part[:half] + partner(time_part[half:], bit)
        if bit in ties:
            time_part = after(time_part, ties[bit])
    turned = jnp.concatenate([time_part[here:], time_part[:here]], 0)
    time_part = time_part + swap(turned, "c")

    gain_one, shift_one = ln1_gain.astype(f32), ln1_bias.astype(f32)
    gain_two, shift_two = ln2_gain.astype(f32), ln2_bias.astype(f32)
    flat_tokens = tokens.astype(f32).reshape(slots, width)
    normal_one, inverse_one = normalize(flat_tokens)
    normed = (normal_one * gain_one + shift_one).astype(bf16).reshape(tokens.shape)

    down = [(d, d + 1) for d in range(tiles - 1)]
    up = [(d + 1, d) for d in range(tiles - 1)]

    edges = [normed[:, rows_here - HALO :], normed[:, :HALO]]
    edges = all_after(edges, *qkv_parts[1:])
    above = lax.ppermute(edges[0], "rows", down)
    below = lax.ppermute(edges[1], "rows", up)

    qkv_pair = jnp.concatenate([qkv_keep, qkv_got], 0)
    time_pairs = tile_gather(time_part)
    qkv_pair = after(qkv_pair, time_part, above, below)
    one_parts = tiles_all(after(one, time_pairs, qkv_pair))
    two_parts = tiles_all(two)

    qkv_x, qkv_y = swap(qkv_pair, "x"), swap(qkv_pair, "y")
    normed_ext = jnp.concatenate([after(above, qkv_pair), normed, below], 1)
    normed_all = with_partner(normed_ext, "c").reshape(images * keys, width)
    qkv_x, qkv_y = all_after([qkv_x, qkv_y], normed_all)
    qkv_far = [swap(qkv_x[:chunk], "y"), swap(qkv_y[chunk:], "x")]
    qkv_far = all_after(qkv_far, one_parts)
    spots = at_y * 4 + at_x * 2 + at_c
    qkv_full = place_rows(
        [qkv_pair[:chunk], qkv_pair[chunk:], qkv_x[:chunk], qkv_x[chunk:]]
        + [qkv_y[:chunk], qkv_y[chunk:]]
        + qkv_far,
        [jnp.bitwise_xor(spots, step) * chunk for step in range(8)],
        "place_qkv",
    )

    out_rows, fc1_rows = on_blocks(
        functools.partial(unpack_kernel, True, 2, 1),
        spot,
        [after(one_parts, qkv_full)],
        matrices((2 * chunk, width), (4 * chunk, 4 * ff_part)),
        "unpack_fc1",
    )
    out_got = swap(out_rows, "x")
    places = at_y * 2 + at_x
    out_full = place_rows(
        [out_rows[:chunk], out_rows[chunk:], out_got[:chunk], out_got[chunk:]],
        [jnp.bitwise_xor(places, step) * chunk for step in (0, 2, 1, 3)],
        "place_out",
    )
    fc1_first, fc1_second = sides_of(fc1_rows)
    fc1_first, fc1_second = swap(fc1_first, "y"), swap(fc1_second, "y")
    size = fc1_rows.shape[0]
    fc1_full = place_rows(
        [fc1_rows, fc1_first, fc1_second],
        [at_y * size, (1 - at_y) * size, (1 - at_y) * size + size // 2],
        "place_fc1",
    )
    grad_mlp_x = with_partner(after(grad_mlp_own, qkv_full), "x")
    grad_mlp = with_partner(grad_mlp_x, "c")

    time_pairs = time_pairs.reshape(images, -1, 2, chunk)
    time_mine = pick(at_c, (time_pairs[:, :, 0], time_pairs[:, :, 1]))[0].reshape(images, width)
    half = width // 2
    time_all = jnp.concatenate(
        [time_mine[:, :half], jnp.zeros((images, half), f32), time_mine[:, half:]], 1
    )


    query_row = jnp.arange(cells) // cols
    query_col = jnp.arange(cells) % cols
    key_row = jnp.arange(keys) // cols - HALO
    key_col = jnp.arange(keys) % cols
    near = jnp.abs(key_row[None, :] - query_row[:, None]) <= HALO
    itself = jnp.arange(keys)[None, :] == jnp.arange(cells)[:, None] + HALO * cols
    global_key = tile * rows_here + key_row
    key_ok = (
        (global_key[None, :] >= 0)
        & (global_key[None, :] < heights_all[:, None])
        & (key_col[None, :] < widths_all[:, None])
    )
    allowed = (key_ok[:, None, :] & near[None] | itself[None]).astype(f32)
    heads = head_count // 2
    gaps = 2 * HALO + 1
    spans = 2 * cols - 1
    exact = lax.Precision.HIGHEST
    bucket_hits = (
        rel_index.reshape(-1)[:, None] == jnp.arange(rel_table.shape[0])[None, :]
    ).astype(f32)
    head_ids = jnp.arange(heads)
    head_hits = (
        jnp.arange(head_count)[:, None] == (head_ids // 2 * 4 + at_c * 2 + head_ids % 2)[None, :]
    ).astype(f32)
    table_mine = jnp.dot(after(rel_table, qkv_pair).astype(f32), head_hits, precision=exact)
    offset_values = lax.dot_general(
        table_mine, bucket_hits, (((0,), (1,)), ((), ())), precision=exact
    ).reshape(heads, gaps, spans)
    offset_values = jnp.pad(offset_values, ((0, 0), (0, 0), (0, LANES - spans)))
    bias = spread(offset_values, cells, keys, cols)


    normed_here = after(normed_all, out_rows)
    qkv = (
        dot(normed_here, qkv_full).reshape(images, keys, 3 * half) + time_all[:, None]
    ).astype(bf16)
    attended, prob = attend(qkv, bias, allowed, scale)
    attended = after(attended.reshape(images * cells, half), fc1_first)

    def core_sum(left, right, dims=NN):
        size = left.shape[0] // 2
        sent = swap(dot(left[size:], right, dims).astype(bf16), "c")
        return dot(left[:size], right, dims) + sent.astype(f32)

    middle = flat_tokens + core_sum(attended, out_full) + out_bias.astype(f32)
    normal_two, inverse_two = normalize(middle)
    second = (normal_two * gain_two + shift_two).astype(bf16)
    second_x, second_c = swap(second, "x"), swap(second, "c")
    second_x = after(second_x, fc1_full, grad_mlp_x)
    second = jnp.concatenate([second, second_x, second_c, swap(second_x, "c")], 0)


    member = at_c * 2 + at_x
    bias_parts = fc1_bias.astype(f32).reshape(tiles, 4, ff_part)
    bias_mine = lax.dynamic_index_in_dim(bias_parts, member, 1, keepdims=False).reshape(-1)
    hidden_pre = dot(second, fc1_full) + bias_mine
    hidden_act, hidden_slope = gelu_and_slope(hidden_pre)
    hidden = hidden_act.astype(bf16)
    hidden_slope = hidden_slope.astype(bf16)
    (fc2_full,) = on_blocks(
        functools.partial(unpack_kernel, False, 0, 2),
        spot,
        [after(two_parts, middle)],
        matrices((8 * chunk, width)),
        "unpack_fc2",
    )
    grad_pre = (dot(grad_mlp, fc2_full, NT) * hidden_slope.astype(f32)).astype(bf16)
    grad_second = core_sum(grad_pre, fc1_full, NT)
    grad_second_sent = grad_second[slots:].astype(bf16)
    grad_second_got = swap(grad_second_sent, "x")
    grad_fc2 = dot(after(hidden, grad_second_sent), grad_mlp, TN).astype(bf16)
    (two_packed,) = on_blocks(
        pack_sides_kernel, spot, [grad_fc2], matrices((tiles, 2 * chunk, 2 * wide)), "pack_fc2"
    )
    two_sum = tiles_sum(two_packed)
    grad_second_got = after(grad_second_got, two_packed)
    grad_second = grad_second[:slots] + grad_second_got.astype(f32)
    grad_fc1 = dot(second, grad_pre, TN).astype(bf16)
    grad_fc2_bias = jnp.sum(grad_mlp_own, 0, dtype=f32)
    grad_fc1_bias = jnp.sum(grad_pre, 0, dtype=f32)

    grad_gain_two = jnp.sum(grad_second * normal_two, 0)
    grad_shift_two = jnp.sum(grad_second, 0)
    grad_middle = grad_out + norm_back(grad_second * gain_two, normal_two, inverse_two)
    grad_branch_own = grad_middle.astype(bf16)
    grad_out_bias = jnp.sum(grad_branch_own, 0, dtype=f32)
    grad_branch = with_partner(grad_branch_own, "c")


    def add_bf16(one, two):
        return (one.astype(f32) + two.astype(f32)).astype(bf16)

    def sides(grad):
        return grad.reshape((2, -1) + grad.shape[1:])

    fc1_got = swap(part_of(sides(grad_fc1), 1 - at_y), "y")
    grad_out_weight = dot(attended, grad_branch, TN).astype(bf16)
    out_sides = grad_out_weight.reshape(2, 2, chunk, width)
    out_sent = out_sides[:, 0], out_sides[:, 1]
    out_kept, out_sent = pick(at_x, out_sent)
    grad_att = grad_branch.reshape(images, cells, width)
    out_got = swap(out_sent, "x")

    grad_proj, grad_strip = attend_back(qkv, prob, grad_att, out_full, scale, cols)
    flat_proj = grad_proj.reshape(images * keys, 3 * half)
    grad_qkv = row_major(dot(normed_all, flat_proj, TN).astype(bf16))
    blocks = grad_qkv.reshape(2, 2, 2, chunk, 12 * chunk)

    def blocks_at(y, x, core):
        first = [0 if at is None else at for at in (y, x, core)] + [0, 0]
        size = [2 if at is None else 1 for at in (y, x, core)] + list(blocks.shape[3:])
        return lax.dynamic_slice(blocks, first, size).reshape(-1, chunk, 12 * chunk)

    own_sent = blocks_at(1 - at_y, None, at_c)
    other_sent = blocks_at(None, 1 - at_x, 1 - at_c)
    own_got, other_got = swap(own_sent, "y"), swap(other_sent, "x")
    out_mine = add_bf16(out_kept, after(out_got, grad_qkv))
    out_got = swap(part_of(out_mine, 1 - at_y), "y")

    (one_packed,) = on_blocks(
        functools.partial(pack_kernel, True),
        spot,
        [grad_fc1, after(fc1_got, own_sent, other_sent)],
        matrices((tiles, chunk, 2 * wide)),
        "pack_fc1",
    )
    one_sum = tiles_sum(one_packed)
    flat_proj = after(flat_proj, own_sent, other_sent, one_packed)
    grad_ext = core_sum(flat_proj, qkv_full, NT).reshape(here, key_rows, cols, width)
    mlp_out = core_sum(after(hidden, grad_ext), fc2_full)

    from_below = lax.ppermute(grad_ext[:, :HALO].astype(bf16), "rows", up).astype(f32)
    from_above = lax.ppermute(grad_ext[:, HALO + rows_here :].astype(bf16), "rows", down)
    from_above = from_above.astype(f32)
    rest = ((0, 0), (rows_here - HALO, 0), (0, 0), (0, 0))
    grad_normed = (
        grad_ext[:, HALO : HALO + rows_here]
        + jnp.pad(from_below, rest)
        + jnp.pad(from_above, (rest[0], rest[1][::-1], rest[2], rest[3]))
    ).reshape(slots, width)
    grad_gain_one = jnp.sum(grad_normed * normal_one, 0)
    grad_shift_one = jnp.sum(grad_normed, 0)
    grad_input = grad_middle + norm_back(grad_normed * gain_one, normal_one, inverse_one)
    grad_tokens = grad_input.reshape(tokens.shape).astype(bf16)


    grad_offsets = grad_strip[:, :, :spans].reshape(heads, gaps * spans)
    grad_table = jnp.dot(grad_offsets, bucket_hits, precision=exact)
    grad_table = jnp.dot(head_hits, grad_table, precision=exact)


    own_got, other_got = all_after([own_got, other_got], grad_ext)
    own_two = add_bf16(blocks_at(at_y, None, at_c), own_got)
    other_two = add_bf16(blocks_at(None, at_x, 1 - at_c), other_got)
    far_sent = part_of(own_two, 1 - at_x)
    own_got = swap(far_sent, "x")
    mlp_sent = after(mlp_out[slots:].astype(bf16), far_sent)
    mlp_out = mlp_out[:slots] + swap(mlp_sent, "x").astype(f32) + fc2_bias.astype(f32)
    mixed = (valid_mask * (middle + mlp_out)).reshape(tokens.shape).astype(bf16)
    other_got = swap(part_of(other_two, 1 - at_y), "y")
    own_rows_got, other_rows_got = own_got, other_got
    out_mine = add_bf16(part_of(out_mine, at_y), after(out_got, far_sent))


    def row(value):
        return value.reshape(-1, width)

    mine = (jnp.arange(4) == member).astype(f32)
    fc1_bias_all = grad_fc1_bias.reshape(tiles, 1, ff_part) * mine[None, :, None]
    buckets = rel_table.shape[0]
    table_rows = grad_table.reshape(4, -1, buckets)
    table_rows = jnp.concatenate([table_rows[:, at] for at in range(table_rows.shape[1])], 1)
    table_rows = jnp.pad(table_rows, ((0, 0), (0, width - table_rows.shape[1])))
    small = [
        row(grad_gain_one),
        row(grad_shift_one),
        row(grad_out_bias),
        row(grad_gain_two),
        row(grad_shift_two),
        row(grad_fc2_bias),
        row(fc1_bias_all),
        table_rows,
    ]
    count = 6 + 4 * ff_part * tiles // width + 4
    sums = jnp.sum(grad_proj, 1, dtype=f32)
    sums = jnp.concatenate([sums[:, :half], sums[:, 2 * half :]], 1)
    total = jnp.concatenate(small + [sums], 0)
    for step in range(tiles.bit_length() - 1):
        route = [(d, d ^ (1 << step)) for d in range(tiles)]
        total = total + lax.ppermute(total, "rows", route)
    own_rows_got, other_rows_got = all_after([own_rows_got, other_rows_got], total)

    own_rows = add_bf16(part_of(own_two, at_x), own_rows_got)
    other_rows = add_bf16(part_of(other_two, at_y), other_rows_got)
    other_rows = swap(other_rows, "c")
    last_parts = on_blocks(
        pack_qkv_kernel,
        spot,
        [own_rows, other_rows, out_mine],
        matrices(*[(chunk, 6 * chunk + quarter)] * 4),
        "pack_qkv",
    )
    last = last_parts[0].astype(f32)
    for step in range(1, tiles):
        last = last + shift(last_parts[step], step).astype(f32)
    qkv_own, out_own = last[:, : 6 * chunk], last[:, 6 * chunk :]

    two_sum = after(two_sum, far_sent)
    two_sum = add_bf16(two_sum[:chunk], swap(two_sum[chunk:], "y"))
    keep1, keep2, send = on_blocks(
        split_sums_kernel,
        spot,
        [one_sum, two_sum],
        matrices((chunk, wide), (chunk, wide), (chunk, 2 * wide)),
        "split_sums",
    )
    side_got = swap(send, "x")
    (send,) = on_blocks(
        turn_core_kernel, spot, [keep1, side_got], matrices((chunk, wide)), "turn_core"
    )
    fc1_own, fc2_own = on_blocks(
        finish_kernel,
        spot,
        [keep1, keep2, side_got, swap(send, "c")],
        [((chunk, 2 * wide), f32), ((4 * chunk, ff_part), f32)],
        "finish",
    )


    total = after(total, *last_parts)
    total, sums = total[:count], total[count:]
    size = width // tiles
    sums = lax.select_n(tile, *[sums[:, at * size : (at + 1) * size] for at in range(tiles)])
    turned = jnp.concatenate([sums[here:], sums[:here]], 0)

    def both(total, sums, bit):
        room = ((0, 0), (0, width - sums.shape[1]))
        got = partner(jnp.concatenate([total, jnp.pad(sums, room)], 0), bit)
        return total + got[:count], got[count:, : sums.shape[1]]

    total, other = both(total, turned, orders[0])
    pair = pick(at_c, (sums.reshape(images, -1, 1, chunk), other.reshape(images, -1, 1, chunk)))
    sums = jnp.concatenate(pair, 2).reshape(images, -1)
    for bit in orders[1:]:
        total, other = both(total, sums, bit)
        sums = jnp.concatenate([sums, other], 0)
    grad_time = lax.dot_general(timing.astype(f32), sums, TN, precision=exact)
    table = total[count - 4 :, : head_count // 4 * buckets].reshape(head_count, buckets).T
    return (
        mixed,
        grad_tokens,
        total[0],
        total[1],
        low_scatter(qkv_own),
        grad_time,
        table,
        low_scatter(out_own),
        total[2],
        total[3],
        total[4],
        low_scatter(fc1_own),
        total[6 : count - 4].reshape(-1),
        low_scatter(fc2_own),
        total[5],
    )


def solution(mesh):
    tokens, image, weight = P("images", "rows", None, None), P("images"), P("images", "rows")
    return jax.shard_map(
        shards,
        mesh=mesh,
        in_specs=(
            tokens, tokens, image, image, image, P(), P(), P(), weight, weight,
            P(), weight, P(), P(), P(), weight, P(), weight, P(),
        ),
        out_specs=(
            tokens, tokens, P(), P(), weight, weight, P(), weight, P(), P(),
            P(), weight, P(), weight, P(),
        ),
        check_vma=False,
    )
```

```python
import functools
import math

import jax
import jax.numpy as jnp
from jax import lax
from jax.experimental import pallas as pl
from jax.experimental.layout import Layout, with_layout_constraint
from jax.experimental.pallas import tpu as pltpu
from jax.sharding import PartitionSpec as P

HALO = 2
LANES = 128

norm_eps = 1e-06
masked_score = -1000000000.0

f32 = jnp.float32
bf16 = jnp.bfloat16

NN = (((1,), (0,)), ((), ()))
NT = (((1,), (1,)), ((), ()))
TN = (((0,), (0,)), ((), ()))


def dot(left, right, dims=NN):
    return lax.dot_general(left, right, dims, preferred_element_type=f32)


def row_major(value):
    return with_layout_constraint(value, Layout(major_to_minor=tuple(range(value.ndim))))


def normalize(values):
    centre = values - jnp.mean(values, -1, keepdims=True)
    spread = jnp.mean(centre * centre, -1, keepdims=True)
    inverse = lax.rsqrt(spread + norm_eps)
    return (centre * inverse, inverse)


def norm_back(grad_hat, normal_part, inverse):
    first_mean = jnp.mean(grad_hat, -1, keepdims=True)
    second_mean = jnp.mean(grad_hat * normal_part, -1, keepdims=True)
    return inverse * (grad_hat - first_mean - normal_part * second_mean)


def gelu_and_slope(values):
    slant = math.sqrt(2.0 / math.pi)
    square = values * values
    curve = jnp.tanh(slant * values * (1.0 + 0.044715 * square))
    lift = 0.5 * (1.0 + curve)
    bend = 0.5 * values * (1.0 - curve * curve) * slant * (1.0 + 3.0 * 0.044715 * square)
    return values * lift, lift + bend


def window(head, head_dim, width):
    first, last = head * head_dim, (head + 1) * head_dim
    start = first // LANES * LANES
    stop = min(-(-last // LANES) * LANES, width)
    return first, last, start, stop


def lane_mask(first, last, start, stop, kind):
    lane = lax.broadcasted_iota(jnp.int32, (1, stop - start), 1) + start
    return jnp.where((lane >= first) & (lane < last), 1.0, 0.0).astype(kind)


def add_tiles(tiles, values, start, stop):
    for at in range(start, stop, LANES):
        part = values[:, at - start : min(at + LANES, stop) - start]
        tiles[at] = part if at not in tiles else tiles[at] + part


def store_tiles(ref, tiles, scale=None, rows=slice(None), base=0):
    for at, part in tiles.items():
        if scale is not None:
            part = part * scale
        ref[0, rows, base + at : base + at + part.shape[1]] = part.astype(ref.dtype)


def spread_kernel(cols, offsets_ref, bias_ref):
    bias_ref[...] = jnp.zeros_like(bias_ref)
    for head in range(bias_ref.shape[0]):
        for gap in range(2 * HALO + 1):
            line = offsets_ref[head, gap : gap + 1]
            lines = jnp.broadcast_to(line, (cols, line.shape[1]))
            first = line.shape[1] - cols + 1
            block = pltpu.roll(lines, first, 1, stride=1, stride_axis=0)[:, :cols]
            for row in range(bias_ref.shape[1] // cols):
                at = (row + gap) * cols
                bias_ref[head, row * cols : (row + 1) * cols, at : at + cols] = block.astype(bf16)


def attend_kernel(heads, scale, edge, qkv_ref, bias_ref, allow_ref, o_ref, p_ref):
    half = o_ref.shape[-1]
    cells = o_ref.shape[1]

    allowed = allow_ref[0] > 0.5
    queries = qkv_ref[0, edge : edge + cells, :half]
    key = qkv_ref[0, :, half : 2 * half]
    value = qkv_ref[0, :, 2 * half :]
    tiles = {}
    for head in range(heads):
        span = window(head, half // heads, half)
        start, stop = span[2:]
        query = queries[:, start:stop] * lane_mask(*span, bf16)
        scores = dot(query, key[:, start:stop], NT) * scale + bias_ref[head].astype(f32)
        scores = jnp.where(allowed, scores, masked_score)
        expo = jnp.exp(scores - jnp.max(scores, -1, keepdims=True))
        prob = (expo / jnp.sum(expo, -1, keepdims=True)).astype(bf16)
        p_ref[0, head] = prob
        out = dot(prob, value[:, start:stop]) * lane_mask(*span, f32)
        add_tiles(tiles, out, start, stop)
    store_tiles(o_ref, tiles)


def attend_back_kernel(
    heads, scale, edge, cols, qkv_ref, p_ref, dz_ref, weight_ref, d_ref, g_ref, sum_ref
):
    cells = dz_ref.shape[1]
    half = weight_ref.shape[0]
    rows = cells // cols
    middle = slice(edge, edge + cells)
    step = pl.program_id(0)

    @pl.when(step == 0)
    def _():
        sum_ref[...] = jnp.zeros_like(sum_ref)

    queries = qkv_ref[0, middle, :half]
    key = qkv_ref[0, :, half : 2 * half]
    value = qkv_ref[0, :, 2 * half :]
    grad_outs = dot(dz_ref[0], weight_ref[...], NT).astype(bf16)
    dq_tiles, dk_tiles, dv_tiles = {}, {}, {}
    for head in range(heads):
        span = window(head, half // heads, half)
        start, stop = span[2:]
        mask = lane_mask(*span, bf16)
        query = queries[:, start:stop] * mask
        grad_out = grad_outs[:, start:stop] * mask
        prob = p_ref[0, head]
        full = prob.astype(f32)
        weighted = full * dot(grad_out, value[:, start:stop], NT)
        grad_score = (weighted - full * jnp.sum(weighted, -1, keepdims=True)).astype(bf16)
        sum_ref[head] += grad_score.astype(f32)
        dq = dot(grad_score, key[:, start:stop]) * lane_mask(*span, f32)
        add_tiles(dq_tiles, dq, start, stop)
        add_tiles(dk_tiles, dot(grad_score, query, TN), start, stop)
        add_tiles(dv_tiles, dot(prob, grad_out, TN), start, stop)
    d_ref[0, :edge, :half] = jnp.zeros((edge, half), bf16)
    d_ref[0, edge + cells :, :half] = jnp.zeros((edge, half), bf16)
    store_tiles(d_ref, dq_tiles, scale, middle)
    store_tiles(d_ref, dk_tiles, scale, base=half)
    store_tiles(d_ref, dv_tiles, base=2 * half)

    @pl.when(step == pl.num_programs(0) - 1)
    def _():
        ids = [lax.broadcasted_iota(jnp.int32, (cols, cols), axis) for axis in range(2)]
        turn = jnp.where(ids[0] + ids[1] == cols - 1, 1.0, 0.0)
        for head in range(heads):
            total = sum_ref[head, :cols]
            for row in range(1, rows):
                part = sum_ref[head, row * cols : (row + 1) * cols]
                total += pltpu.roll(part, part.shape[1] - row * cols, 1)
            total = jnp.dot(turn, total, precision=lax.Precision.HIGHEST)
            for gap in range(2 * HALO + 1):
                block = total[:, gap * cols : (gap + 1) * cols]
                block = jnp.concatenate([block, jnp.zeros((cols, LANES - cols), f32)], 1)
                block = pltpu.roll(block, 0, 1, stride=1, stride_axis=0)
                g_ref[head, gap : gap + 1] = jnp.sum(block, 0, keepdims=True)


def per_image(*dims):
    return pl.BlockSpec((1,) + dims, lambda i: (i,) + (0,) * len(dims))


def whole(*dims):
    return pl.BlockSpec(dims, lambda i: (0,) * len(dims))


def spread(offsets, cells, keys, cols):
    block = pl.BlockSpec(memory_space=pltpu.VMEM)
    return pl.pallas_call(
        functools.partial(spread_kernel, cols),
        in_specs=[block],
        out_specs=block,
        out_shape=jax.ShapeDtypeStruct((offsets.shape[0], cells, keys), bf16),
        name="spread",
    )(offsets)


def attend(qkv, bias, allowed, scale):
    images, keys, width = qkv.shape
    heads, cells, _ = bias.shape
    half = width // 3
    return pl.pallas_call(
        functools.partial(attend_kernel, heads, scale, (keys - cells) // 2),
        grid=(images,),
        in_specs=[per_image(keys, width), whole(heads, cells, keys), per_image(cells, keys)],
        out_specs=[per_image(cells, half), per_image(heads, cells, keys)],
        out_shape=[
            jax.ShapeDtypeStruct((images, cells, half), bf16),
            jax.ShapeDtypeStruct((images, heads, cells, keys), bf16),
        ],
        compiler_params=pltpu.CompilerParams(vmem_limit_bytes=56 << 20),
        cost_estimate=pl.CostEstimate(flops=1, bytes_accessed=1, transcendentals=0),
        name="attend",
    )(qkv, bias, allowed)


def attend_back(qkv, prob, grad, weight, scale, cols):
    images, keys, width = qkv.shape
    heads, cells = prob.shape[1:3]
    half, total = weight.shape
    return pl.pallas_call(
        functools.partial(attend_back_kernel, heads, scale, (keys - cells) // 2, cols),
        grid=(images,),
        in_specs=[
            per_image(keys, width),
            per_image(heads, cells, keys),
            per_image(cells, total),
            whole(half, total),
        ],
        out_specs=[per_image(keys, width), whole(heads, 2 * HALO + 1, LANES)],
        out_shape=[
            jax.ShapeDtypeStruct((images, keys, width), bf16),
            jax.ShapeDtypeStruct((heads, 2 * HALO + 1, LANES), f32),
        ],
        scratch_shapes=[pltpu.VMEM((heads, cells, keys), f32)],
        compiler_params=pltpu.CompilerParams(vmem_limit_bytes=56 << 20),
        cost_estimate=pl.CostEstimate(flops=1, bytes_accessed=1, transcendentals=0),
        name="attend_back",
    )(qkv, prob, grad, weight)


def on_blocks(kernel, spot, values, shapes, name):
    block = pl.BlockSpec(memory_space=pltpu.VMEM)
    return pl.pallas_call(
        kernel,
        in_specs=[pl.BlockSpec(memory_space=pltpu.SMEM)] + [block] * len(values),
        out_specs=[block] * len(shapes),
        out_shape=[jax.ShapeDtypeStruct(shape, kind) for shape, kind in shapes],
        compiler_params=pltpu.CompilerParams(vmem_limit_bytes=32 << 20),
        name=name,
    )(spot, *values)


def for_each(value, count, body):
    for at in range(count):
        pl.when(value == at)(functools.partial(body, at))


def source_row(spot, group, size, by_core):
    side = jnp.bitwise_xor(spot[1], group >> 1)
    core = jnp.bitwise_xor(spot[2], group & 1) if by_core else group & 1
    return pl.multiple_of((side * 2 + core) * size, 16)


def split_core_kernel(spot, w_ref, keep_ref, send_ref):
    half = keep_ref.shape[1]

    def body(core):
        keep_ref[...] = w_ref[:, core * half : (core + 1) * half]
        send_ref[...] = w_ref[:, (1 - core) * half : (2 - core) * half]

    for_each(spot[2], 2, body)


def split_side_kernel(spot, own_ref, got_ref, fc2_ref, keep1_ref, keep2_ref, send_ref):
    rows, wide = own_ref.shape
    part = wide // 2

    def body(side):
        for at, ref in enumerate((own_ref, got_ref)):
            lanes = slice(at * part, (at + 1) * part)
            keep1_ref[:, lanes] = ref[:, side * part : (side + 1) * part]
            send_ref[:, lanes] = ref[:, (1 - side) * part : (2 - side) * part]
        for at in range(2):
            first = (side * 2 + at) * rows
            other = ((1 - side) * 2 + at) * rows
            keep2_ref[:, at * part : (at + 1) * part] = fc2_ref[first : first + rows]
            send_ref[:, wide + at * part : wide + (at + 1) * part] = fc2_ref[other : other + rows]

    for_each(spot[1], 2, body)


def fill_lanes(ref, first):
    if first < ref.shape[-1]:
        ref[:, first:] = jnp.zeros((ref.shape[0], ref.shape[-1] - first), ref.dtype)


def join_side_kernel(spot, out_ref, far_ref, keep1_ref, keep2_ref, got_ref, one_ref, two_ref):
    part = 2 * out_ref.shape[1]
    wide = keep1_ref.shape[1]
    one_ref[:, : part // 2] = out_ref[...]
    one_ref[:, part // 2 : part] = far_ref[...]
    one_ref[:, part : part + wide] = keep1_ref[...]
    one_ref[:, part + wide : part + 2 * wide] = got_ref[:, :wide]
    fill_lanes(one_ref, part + 2 * wide)
    two_ref[:, :wide] = keep2_ref[...]
    two_ref[:, wide:] = got_ref[:, wide:]


def unpack_kernel(by_core, lead, sides, spot, pieces, *outs):
    rows = pieces.shape[1] // sides
    part = outs[-1].shape[1] // 4
    for block in range(4):
        lanes = slice(block * part, (block + 1) * part)
        for at in range(lead):
            outs[0][at * rows : (at + 1) * rows, lanes] = pieces[
                block, :, at * part : (at + 1) * part
            ]
        for side in range(sides):
            base = jnp.bitwise_xor(spot[3], side) * 4 * rows if sides > 1 else 0
            for group in range(4):
                first = (group + lead) * part
                row = base + source_row(spot, group, rows, by_core)
                outs[-1][pl.ds(pl.multiple_of(row, 16), rows), lanes] = pieces[
                    block, side * rows : (side + 1) * rows, first : first + part
                ]


def pack_kernel(by_core, spot, grad_ref, got_ref, out):
    rows = out.shape[1]
    part = grad_ref.shape[1] // 4
    base = spot[3] * got_ref.shape[0]
    for block in range(4):
        lanes = slice(block * part, (block + 1) * part)
        for group in range(4):
            row = source_row(spot, group, rows, by_core)
            own = grad_ref[pl.ds(pl.multiple_of(base + row, 16), rows), lanes]
            total = own.astype(f32) + got_ref[pl.ds(row, rows), lanes].astype(f32)
            out[block, :, group * part : (group + 1) * part] = total.astype(out.dtype)


def pack_sides_kernel(spot, grad_ref, out):
    rows = out.shape[1] // 2
    part = grad_ref.shape[1] // 4
    for block in range(4):
        lanes = slice(block * part, (block + 1) * part)
        for side in range(2):
            base = jnp.bitwise_xor(spot[3], side) * 4 * rows
            for group in range(4):
                row = pl.multiple_of(base + source_row(spot, group, rows, False), 16)
                out[block, side * rows : (side + 1) * rows, group * part : (group + 1) * part] = (
                    grad_ref[pl.ds(row, rows), lanes]
                )


def split_sums_kernel(spot, one, two, keep1_ref, keep2_ref, send_ref):
    wide = keep1_ref.shape[1]
    keep1_ref[...] = one[:, :wide]
    keep2_ref[...] = two[:, :wide]
    send_ref[:, :wide] = one[:, wide:]
    send_ref[:, wide:] = two[:, wide:]


def turn_core_kernel(spot, keep1_ref, got_ref, send_ref):
    part = send_ref.shape[1] // 2
    send_ref[:, :part] = keep1_ref[:, part:]
    send_ref[:, part:] = got_ref[:, part : 2 * part]


def finish_kernel(spot, keep1_ref, keep2_ref, side_ref, core_ref, fc1_ref, fc2_ref):
    rows, part = fc1_ref.shape[0], fc2_ref.shape[1]

    def body(place):
        core, side = place // 2, place % 2
        parts = {
            (core, side): keep1_ref[:, :part],
            (core, 1 - side): side_ref[:, :part],
            (1 - core, side): core_ref[:, :part],
            (1 - core, 1 - side): core_ref[:, part:],
        }
        for (c, x), value in parts.items():
            fc1_ref[:, (2 * c + x) * part : (2 * c + x + 1) * part] = value.astype(f32)
        for at in range(2):
            lanes = slice(at * part, (at + 1) * part)
            first, other = (side * 2 + at) * rows, ((1 - side) * 2 + at) * rows
            fc2_ref[first : first + rows] = keep2_ref[:, lanes].astype(f32)
            fc2_ref[other : other + rows] = side_ref[:, (2 + at) * part : (3 + at) * part].astype(f32)

    for_each(spot[2] * 2 + spot[1], 4, body)


def qkv_blocks(tile, rows, count):
    for block in range(4):
        for at in range(count):
            for core in range(2):
                yield (
                    block,
                    core,
                    slice((2 * at + core) * rows, (2 * at + core + 1) * rows),
                    slice((block * count + at) * rows, (block * count + at + 1) * rows),
                )


def unpack_qkv_kernel(spot, *refs):
    pieces, kept = refs[:4], refs[4:]
    rows, wide = pieces[0].shape

    def body(place):
        tile, mine = place // 2, place % 2
        for block, core, there, here in qkv_blocks(tile, rows, wide // (2 * rows)):
            kept[core != mine][:, here] = pieces[(tile - block) % 4][:, there]

    for_each(spot[0] * 2 + spot[2], 8, body)


def pack_qkv_kernel(spot, own_ref, got_ref, last_ref, *outs):
    rows, wide = outs[0].shape
    part = last_ref.shape[1] // 4
    wide = wide - part

    def body(place):
        tile, mine = place // 2, place % 2
        for block, core, there, here in qkv_blocks(tile, rows, wide // (2 * rows)):
            source = own_ref if core == mine else got_ref
            outs[(block - tile) % 4][:, there] = source[:, here]
        for block in range(4):
            lanes = slice(block * part, (block + 1) * part)
            outs[(block - tile) % 4][:, wide:] = last_ref[:, lanes]

    for_each(spot[0] * 2 + spot[2], 8, body)


def place_kernel(count, rows_ref, *refs):
    ins, out = refs[:count], refs[count]
    for at, ref in enumerate(ins):
        out[pl.ds(pl.multiple_of(rows_ref[at], 16), ref.shape[0])] = ref[...]


def place_rows(pieces, rows, name):
    height = sum(piece.shape[0] for piece in pieces)
    shape = (height, pieces[0].shape[1]), pieces[0].dtype
    kernel = functools.partial(place_kernel, len(pieces))
    return on_blocks(kernel, jnp.stack(rows).astype(jnp.int32), pieces, [shape], name)[0]


def shards(
    tokens,
    cotangent,
    heights,
    widths,
    timesteps,
    rel_index,
    ln1_gain,
    ln1_bias,
    w_qkv,
    w_time,
    rel_table,
    w_out,
    out_bias,
    ln2_gain,
    ln2_bias,
    w_fc1,
    fc1_bias,
    w_fc2,
    fc2_bias,
):
    here, rows_here, cols, width = tokens.shape
    cells = rows_here * cols
    slots = here * cells
    key_rows = rows_here + 2 * HALO
    keys = key_rows * cols
    head_count = rel_table.shape[1]
    head_dim = width // head_count
    scale = head_dim ** (-0.5)
    image_devices = lax.axis_size("images")
    tiles = lax.axis_size("rows")
    low = image_devices // 8
    chunk = width // 8
    quarter = width // 4
    ff_part = fc1_bias.shape[0] // 16
    place = lax.axis_index("images")
    tile = lax.axis_index("rows")
    bits = {"c": low, "x": 2 * low, "y": 4 * low}
    at_c, at_x, at_y = (place // bits[name] % 2 for name in "cxy")


    def partner(value, bit):
        route = [(d, d ^ bit) for d in range(image_devices)]
        return lax.ppermute(value, "images", route)

    def swap(value, name):
        return partner(value, bits[name])

    def pick(at, pair):
        return jnp.where(at == 0, pair[0], pair[1]), jnp.where(at == 0, pair[1], pair[0])

    def after(value, *others):
        return lax.optimization_barrier((value,) + others)[0]

    def all_after(values, *others):
        return list(lax.optimization_barrier(tuple(values) + others))[: len(values)]

    def with_partner(value, name):
        return jnp.concatenate([value, swap(value, name)], 0)

    def shift(value, step):
        return lax.ppermute(value, "rows", [(d, (d + step) % tiles) for d in range(tiles)])

    def tiles_all(value):
        return lax.all_gather(value, "rows", axis=0)

    def tiles_sum(value):
        return lax.psum_scatter(value, "rows", scatter_dimension=0)

    def shifts(value):
        return [shift(value, step) for step in range(1, tiles)]

    def tile_gather(value):
        for bit in (1, 2):
            other = lax.ppermute(value, "rows", [(d, d ^ bit) for d in range(tiles)])
            value = jnp.concatenate(pick(tile // bit % 2, (value, other)), 1)
        return value

    def tile_scatter(value):
        for bit in (2, 1):
            size = value.shape[1] // 2
            kept, sent = pick(tile // bit % 2, (value[:, :size], value[:, size:]))
            value = kept + lax.ppermute(sent, "rows", [(d, d ^ bit) for d in range(tiles)])
        return value

    low_groups = [[g * low + d for d in range(low)] for g in range(8)]
    def low_gather(value):
        if low == 1:
            return value
        return lax.all_gather(value, "images", axis=0, tiled=True, axis_index_groups=low_groups)

    def low_scatter(value):
        if low == 1:
            return value
        return lax.psum_scatter(
            value, "images", scatter_dimension=0, tiled=True, axis_index_groups=low_groups
        )

    def sides_of(value):
        half = value.shape[0] // 2
        return value[:half], value[half:]

    def part_of(value, at):
        return lax.dynamic_index_in_dim(value, at, 0, keepdims=False)


    slot_row = tile * rows_here + jnp.arange(cells) // cols
    slot_col = jnp.arange(cells) % cols
    valid = (slot_row[None, :] < heights[:, None]) & (slot_col[None, :] < widths[:, None])
    valid_mask = valid.reshape(slots, 1).astype(f32)
    grad_out = cotangent.astype(f32).reshape(slots, width) * valid_mask
    grad_mlp_own = grad_out.astype(bf16)


    spot = jnp.stack([tile, at_x, at_c, at_y]).astype(jnp.int32)
    w_qkv, w_out, w_fc1, w_fc2 = (low_gather(w) for w in (w_qkv, w_out, w_fc1, w_fc2))
    wide = 2 * ff_part
    images = 2 * here
    padded = -(-(2 * quarter + 2 * wide) // LANES) * LANES

    def matrices(*dims):
        return [(dim, bf16) for dim in dims]

    qkv_parts = [w_qkv] + shifts(w_qkv)

    fc1_keep, fc1_send = on_blocks(
        split_core_kernel, spot, [w_fc1], matrices((chunk, wide), (chunk, wide)), "split_core"
    )
    fc1_got = swap(fc1_send, "c")
    keep1, keep2, send = on_blocks(
        split_side_kernel,
        spot,
        [fc1_keep, fc1_got, w_fc2],
        matrices((chunk, wide), (chunk, wide), (chunk, 2 * wide)),
        "split_side",
    )
    got = swap(send, "x")
    one, two = on_blocks(
        join_side_kernel,
        spot,
        [w_out, swap(w_out, "y"), keep1, keep2, got],
        matrices((chunk, padded), (chunk, 2 * wide)),
        "join_side",
    )
    two = with_partner(two, "y")


    orders = [bits["c"], bits["x"], bits["y"]]
    orders += [1 << b for b in range(low.bit_length() - 1)]
    facts = with_partner(jnp.stack([timesteps, heights, widths], 1), "c")
    heights_all, widths_all = facts[:, 1], facts[:, 2]
    steps_all = facts[:, 0]
    for bit in orders[1:]:
        steps_all = jnp.concatenate([steps_all, partner(steps_all, bit)], 0)
    qkv_keep, qkv_send = on_blocks(
        unpack_qkv_kernel,
        spot,
        qkv_parts,
        matrices((chunk, 12 * chunk), (chunk, 12 * chunk)),
        "unpack_qkv",
    )
    qkv_got = swap(qkv_send, "c")
    time_rows = w_time.shape[0]
    half_width = width // 2
    feature = place * time_rows + jnp.arange(time_rows)
    exponent = (feature % half_width).astype(f32)
    frequency = jnp.exp(-math.log(10000.0) * exponent / half_width)
    phases = steps_all.astype(f32)[:, None] * frequency[None, :]
    timing = jnp.where(feature[None, :] < half_width, jnp.cos(phases), jnp.sin(phases)).astype(bf16)
    time_part = dot(timing, after(w_time, keep1, qkv_keep))
    ties = {bits["y"]: qkv_got, bits["x"]: got}
    for bit in orders[:0:-1]:
        half = time_part.shape[0] // 2
        time_part = time_part[:half] + partner(time_part[half:], bit)
        if bit in ties:
            time_part = after(time_part, ties[bit])
    turned = jnp.concatenate([time_part[here:], time_part[:here]], 0)
    time_part = time_part + swap(turned, "c")

    gain_one, shift_one = ln1_gain.astype(f32), ln1_bias.astype(f32)
    gain_two, shift_two = ln2_gain.astype(f32), ln2_bias.astype(f32)
    flat_tokens = tokens.astype(f32).reshape(slots, width)
    normal_one, inverse_one = normalize(flat_tokens)
    normed = (normal_one * gain_one + shift_one).astype(bf16).reshape(tokens.shape)

    down = [(d, d + 1) for d in range(tiles - 1)]
    up = [(d + 1, d) for d in range(tiles - 1)]

    edges = [normed[:, rows_here - HALO :], normed[:, :HALO]]
    edges = all_after(edges, *qkv_parts[1:])
    above = lax.ppermute(edges[0], "rows", down)
    below = lax.ppermute(edges[1], "rows", up)

    qkv_pair = jnp.concatenate([qkv_keep, qkv_got], 0)
    time_pairs = tile_gather(time_part)
    qkv_pair = after(qkv_pair, time_part, above, below)
    one_parts = tiles_all(after(one, time_pairs, qkv_pair))
    two_parts = tiles_all(two)

    qkv_x, qkv_y = swap(qkv_pair, "x"), swap(qkv_pair, "y")
    normed_ext = jnp.concatenate([after(above, qkv_pair), normed, below], 1)
    normed_all = with_partner(normed_ext, "c").reshape(images * keys, width)
    qkv_x, qkv_y = all_after([qkv_x, qkv_y], normed_all)
    qkv_far = [swap(qkv_x[:chunk], "y"), swap(qkv_y[chunk:], "x")]
    qkv_far = all_after(qkv_far, one_parts)
    spots = at_y * 4 + at_x * 2 + at_c
    qkv_full = place_rows(
        [qkv_pair[:chunk], qkv_pair[chunk:], qkv_x[:chunk], qkv_x[chunk:]]
        + [qkv_y[:chunk], qkv_y[chunk:]]
        + qkv_far,
        [jnp.bitwise_xor(spots, step) * chunk for step in range(8)],
        "place_qkv",
    )

    out_rows, fc1_rows = on_blocks(
        functools.partial(unpack_kernel, True, 2, 1),
        spot,
        [after(one_parts, qkv_full)],
        matrices((2 * chunk, width), (4 * chunk, 4 * ff_part)),
        "unpack_fc1",
    )
    out_got = swap(out_rows, "x")
    places = at_y * 2 + at_x
    out_full = place_rows(
        [out_rows[:chunk], out_rows[chunk:], out_got[:chunk], out_got[chunk:]],
        [jnp.bitwise_xor(places, step) * chunk for step in (0, 2, 1, 3)],
        "place_out",
    )
    fc1_first, fc1_second = sides_of(fc1_rows)
    fc1_first, fc1_second = swap(fc1_first, "y"), swap(fc1_second, "y")
    size = fc1_rows.shape[0]
    fc1_full = place_rows(
        [fc1_rows, fc1_first, fc1_second],
        [at_y * size, (1 - at_y) * size, (1 - at_y) * size + size // 2],
        "place_fc1",
    )
    grad_mlp_x = with_partner(after(grad_mlp_own, qkv_full), "x")
    grad_mlp = with_partner(grad_mlp_x, "c")

    time_pairs = time_pairs.reshape(images, -1, 2, chunk)
    time_mine = pick(at_c, (time_pairs[:, :, 0], time_pairs[:, :, 1]))[0].reshape(images, width)
    half = width // 2
    time_all = jnp.concatenate(
        [time_mine[:, :half], jnp.zeros((images, half), f32), time_mine[:, half:]], 1
    )


    query_row = jnp.arange(cells) // cols
    query_col = jnp.arange(cells) % cols
    key_row = jnp.arange(keys) // cols - HALO
    key_col = jnp.arange(keys) % cols
    near = jnp.abs(key_row[None, :] - query_row[:, None]) <= HALO
    itself = jnp.arange(keys)[None, :] == jnp.arange(cells)[:, None] + HALO * cols
    global_key = tile * rows_here + key_row
    key_ok = (
        (global_key[None, :] >= 0)
        & (global_key[None, :] < heights_all[:, None])
        & (key_col[None, :] < widths_all[:, None])
    )
    allowed = (key_ok[:, None, :] & near[None] | itself[None]).astype(f32)
    heads = head_count // 2
    gaps = 2 * HALO + 1
    spans = 2 * cols - 1
    exact = lax.Precision.HIGHEST
    bucket_hits = (
        rel_index.reshape(-1)[:, None] == jnp.arange(rel_table.shape[0])[None, :]
    ).astype(f32)
    head_ids = jnp.arange(heads)
    head_hits = (
        jnp.arange(head_count)[:, None] == (head_ids // 2 * 4 + at_c * 2 + head_ids % 2)[None, :]
    ).astype(f32)
    table_mine = jnp.dot(after(rel_table, qkv_pair).astype(f32), head_hits, precision=exact)
    offset_values = lax.dot_general(
        table_mine, bucket_hits, (((0,), (1,)), ((), ())), precision=exact
    ).reshape(heads, gaps, spans)
    offset_values = jnp.pad(offset_values, ((0, 0), (0, 0), (0, LANES - spans)))
    bias = spread(offset_values, cells, keys, cols)


    normed_here = after(normed_all, out_rows)
    qkv = (
        dot(normed_here, qkv_full).reshape(images, keys, 3 * half) + time_all[:, None]
    ).astype(bf16)
    attended, prob = attend(qkv, bias, allowed, scale)
    attended = after(attended.reshape(images * cells, half), fc1_first)

    def core_sum(left, right, dims=NN):
        size = left.shape[0] // 2
        sent = swap(dot(left[size:], right, dims).astype(bf16), "c")
        return dot(left[:size], right, dims) + sent.astype(f32)

    middle = flat_tokens + core_sum(attended, out_full) + out_bias.astype(f32)
    normal_two, inverse_two = normalize(middle)
    second = (normal_two * gain_two + shift_two).astype(bf16)
    second_x, second_c = swap(second, "x"), swap(second, "c")
    second_x = after(second_x, fc1_full, grad_mlp_x)
    second = jnp.concatenate([second, second_x, second_c, swap(second_x, "c")], 0)


    member = at_c * 2 + at_x
    bias_parts = fc1_bias.astype(f32).reshape(tiles, 4, ff_part)
    bias_mine = lax.dynamic_index_in_dim(bias_parts, member, 1, keepdims=False).reshape(-1)
    hidden_pre = dot(second, fc1_full) + bias_mine
    hidden_act, hidden_slope = gelu_and_slope(hidden_pre)
    hidden = hidden_act.astype(bf16)
    hidden_slope = hidden_slope.astype(bf16)
    (fc2_full,) = on_blocks(
        functools.partial(unpack_kernel, False, 0, 2),
        spot,
        [after(two_parts, middle)],
        matrices((8 * chunk, width)),
        "unpack_fc2",
    )
    grad_pre = (dot(grad_mlp, fc2_full, NT) * hidden_slope.astype(f32)).astype(bf16)
    grad_second = core_sum(grad_pre, fc1_full, NT)
    grad_second_sent = grad_second[slots:].astype(bf16)
    grad_second_got = swap(grad_second_sent, "x")
    grad_fc2 = dot(after(hidden, grad_second_sent), grad_mlp, TN).astype(bf16)
    (two_packed,) = on_blocks(
        pack_sides_kernel, spot, [grad_fc2], matrices((tiles, 2 * chunk, 2 * wide)), "pack_fc2"
    )
    two_sum = tiles_sum(two_packed)
    grad_second_got = after(grad_second_got, two_packed)
    grad_second = grad_second[:slots] + grad_second_got.astype(f32)
    grad_fc1 = dot(second, grad_pre, TN).astype(bf16)
    grad_fc2_bias = jnp.sum(grad_mlp_own, 0, dtype=f32)
    grad_fc1_bias = jnp.sum(grad_pre, 0, dtype=f32)

    grad_gain_two = jnp.sum(grad_second * normal_two, 0)
    grad_shift_two = jnp.sum(grad_second, 0)
    grad_middle = grad_out + norm_back(grad_second * gain_two, normal_two, inverse_two)
    grad_branch_own = grad_middle.astype(bf16)
    grad_out_bias = jnp.sum(grad_branch_own, 0, dtype=f32)
    grad_branch = with_partner(grad_branch_own, "c")


    def add_bf16(one, two):
        return (one.astype(f32) + two.astype(f32)).astype(bf16)

    def sides(grad):
        return grad.reshape((2, -1) + grad.shape[1:])

    fc1_got = swap(part_of(sides(grad_fc1), 1 - at_y), "y")
    grad_out_weight = dot(attended, grad_branch, TN).astype(bf16)
    out_sides = grad_out_weight.reshape(2, 2, chunk, width)
    out_sent = out_sides[:, 0], out_sides[:, 1]
    out_kept, out_sent = pick(at_x, out_sent)
    grad_att = grad_branch.reshape(images, cells, width)
    out_got = swap(out_sent, "x")

    grad_proj, grad_strip = attend_back(qkv, prob, grad_att, out_full, scale, cols)
    flat_proj = grad_proj.reshape(images * keys, 3 * half)
    grad_qkv = row_major(dot(normed_all, flat_proj, TN).astype(bf16))
    blocks = grad_qkv.reshape(2, 2, 2, chunk, 12 * chunk)

    def blocks_at(y, x, core):
        first = [0 if at is None else at for at in (y, x, core)] + [0, 0]
        size = [2 if at is None else 1 for at in (y, x, core)] + list(blocks.shape[3:])
        return lax.dynamic_slice(blocks, first, size).reshape(-1, chunk, 12 * chunk)

    own_sent = blocks_at(1 - at_y, None, at_c)
    other_sent = blocks_at(None, 1 - at_x, 1 - at_c)
    own_got, other_got = swap(own_sent, "y"), swap(other_sent, "x")
    out_mine = add_bf16(out_kept, after(out_got, grad_qkv))
    out_got = swap(part_of(out_mine, 1 - at_y), "y")

    (one_packed,) = on_blocks(
        functools.partial(pack_kernel, True),
        spot,
        [grad_fc1, after(fc1_got, own_sent, other_sent)],
        matrices((tiles, chunk, 2 * wide)),
        "pack_fc1",
    )
    one_sum = tiles_sum(one_packed)
    flat_proj = after(flat_proj, own_sent, other_sent, one_packed)
    grad_ext = core_sum(flat_proj, qkv_full, NT).reshape(here, key_rows, cols, width)
    mlp_out = core_sum(after(hidden, grad_ext), fc2_full)

    from_below = lax.ppermute(grad_ext[:, :HALO].astype(bf16), "rows", up).astype(f32)
    from_above = lax.ppermute(grad_ext[:, HALO + rows_here :].astype(bf16), "rows", down)
    from_above = from_above.astype(f32)
    rest = ((0, 0), (rows_here - HALO, 0), (0, 0), (0, 0))
    grad_normed = (
        grad_ext[:, HALO : HALO + rows_here]
        + jnp.pad(from_below, rest)
        + jnp.pad(from_above, (rest[0], rest[1][::-1], rest[2], rest[3]))
    ).reshape(slots, width)
    grad_gain_one = jnp.sum(grad_normed * normal_one, 0)
    grad_shift_one = jnp.sum(grad_normed, 0)
    grad_input = grad_middle + norm_back(grad_normed * gain_one, normal_one, inverse_one)
    grad_tokens = grad_input.reshape(tokens.shape).astype(bf16)


    grad_offsets = grad_strip[:, :, :spans].reshape(heads, gaps * spans)
    grad_table = jnp.dot(grad_offsets, bucket_hits, precision=exact)
    grad_table = jnp.dot(head_hits, grad_table, precision=exact)


    own_got, other_got = all_after([own_got, other_got], grad_ext)
    own_two = add_bf16(blocks_at(at_y, None, at_c), own_got)
    other_two = add_bf16(blocks_at(None, at_x, 1 - at_c), other_got)
    far_sent = part_of(own_two, 1 - at_x)
    own_got = swap(far_sent, "x")
    mlp_sent = after(mlp_out[slots:].astype(bf16), far_sent)
    mlp_out = mlp_out[:slots] + swap(mlp_sent, "x").astype(f32) + fc2_bias.astype(f32)
    mixed = (valid_mask * (middle + mlp_out)).reshape(tokens.shape).astype(bf16)
    other_got = swap(part_of(other_two, 1 - at_y), "y")
    own_rows_got, other_rows_got = own_got, other_got
    out_mine = add_bf16(part_of(out_mine, at_y), after(out_got, far_sent))


    def row(value):
        return value.reshape(-1, width)

    mine = (jnp.arange(4) == member).astype(f32)
    fc1_bias_all = grad_fc1_bias.reshape(tiles, 1, ff_part) * mine[None, :, None]
    buckets = rel_table.shape[0]
    table_rows = grad_table.reshape(4, -1, buckets)
    table_rows = jnp.concatenate([table_rows[:, at] for at in range(table_rows.shape[1])], 1)
    table_rows = jnp.pad(table_rows, ((0, 0), (0, width - table_rows.shape[1])))
    small = [
        row(grad_gain_one),
        row(grad_shift_one),
        row(grad_out_bias),
        row(grad_gain_two),
        row(grad_shift_two),
        row(grad_fc2_bias),
        row(fc1_bias_all),
        table_rows,
    ]
    count = 6 + 4 * ff_part * tiles // width + 4
    sums = jnp.sum(grad_proj, 1, dtype=f32)
    sums = jnp.concatenate([sums[:, :half], sums[:, 2 * half :]], 1)
    total = jnp.concatenate(small + [sums], 0)
    for step in range(tiles.bit_length() - 1):
        route = [(d, d ^ (1 << step)) for d in range(tiles)]
        total = total + lax.ppermute(total, "rows", route)
    own_rows_got, other_rows_got = all_after([own_rows_got, other_rows_got], total)

    own_rows = add_bf16(part_of(own_two, at_x), own_rows_got)
    other_rows = add_bf16(part_of(other_two, at_y), other_rows_got)
    other_rows = swap(other_rows, "c")
    last_parts = on_blocks(
        pack_qkv_kernel,
        spot,
        [own_rows, other_rows, out_mine],
        matrices(*[(chunk, 6 * chunk + quarter)] * 4),
        "pack_qkv",
    )
    last = last_parts[0].astype(f32)
    for step in range(1, tiles):
        last = last + shift(last_parts[step], step).astype(f32)
    qkv_own, out_own = last[:, : 6 * chunk], last[:, 6 * chunk :]

    two_sum = after(two_sum, far_sent)
    two_sum = add_bf16(two_sum[:chunk], swap(two_sum[chunk:], "y"))
    keep1, keep2, send = on_blocks(
        split_sums_kernel,
        spot,
        [one_sum, two_sum],
        matrices((chunk, wide), (chunk, wide), (chunk, 2 * wide)),
        "split_sums",
    )
    side_got = swap(send, "x")
    (send,) = on_blocks(
        turn_core_kernel, spot, [keep1, side_got], matrices((chunk, wide)), "turn_core"
    )
    fc1_own, fc2_own = on_blocks(
        finish_kernel,
        spot,
        [keep1, keep2, side_got, swap(send, "c")],
        [((chunk, 2 * wide), f32), ((4 * chunk, ff_part), f32)],
        "finish",
    )


    total = after(total, *last_parts)
    total, sums = total[:count], total[count:]
    size = width // tiles
    sums = lax.select_n(tile, *[sums[:, at * size : (at + 1) * size] for at in range(tiles)])
    turned = jnp.concatenate([sums[here:], sums[:here]], 0)

    def both(total, sums, bit):
        room = ((0, 0), (0, width - sums.shape[1]))
        got = partner(jnp.concatenate([total, jnp.pad(sums, room)], 0), bit)
        return total + got[:count], got[count:, : sums.shape[1]]

    total, other = both(total, turned, orders[0])
    pair = pick(at_c, (sums.reshape(images, -1, 1, chunk), other.reshape(images, -1, 1, chunk)))
    sums = jnp.concatenate(pair, 2).reshape(images, -1)
    for bit in orders[1:]:
        total, other = both(total, sums, bit)
        sums = jnp.concatenate([sums, other], 0)
    grad_time = lax.dot_general(timing.astype(f32), sums, TN, precision=exact)
    table = total[count - 4 :, : head_count // 4 * buckets].reshape(head_count, buckets).T
    return (
        mixed,
        grad_tokens,
        total[0],
        total[1],
        low_scatter(qkv_own),
        grad_time,
        table,
        low_scatter(out_own),
        total[2],
        total[3],
        total[4],
        low_scatter(fc1_own),
        total[6 : count - 4].reshape(-1),
        low_scatter(fc2_own),
        total[5],
    )


def solution(mesh):
    tokens, image, weight = P("images", "rows", None, None), P("images"), P("images", "rows")
    return jax.shard_map(
        shards,
        mesh=mesh,
        in_specs=(
            tokens, tokens, image, image, image, P(), P(), P(), weight, weight,
            P(), weight, P(), P(), P(), weight, P(), weight, P(),
        ),
        out_specs=(
            tokens, tokens, P(), P(), weight, weight, P(), weight, P(), P(),
            P(), weight, P(), weight, P(),
        ),
        check_vma=False,
    )
```
